128 devices in a mesh: section: 8 (over y, x_hi), dp: 16 (over z, x_lo, core).
Axes of the slice: x: 4 (x_hi: 2, x_lo: 2; x = x_hi * 2 + x_lo), y: 4, z: 4, core: 2. Of those that a mesh axis runs over, the one named last changes fastest.
Arguments:
- inputs: bfloat16 [16, 2, 1, 128, 1024], P('dp'), may hold values from -120 to 120
- cotangent: bfloat16 [16, 2, 1, 128, 1024], P('dp'), may hold values from -0.4375 to 0.4375
- w_qkv: bfloat16 [8, 1024, 1536], P('section'), may hold values from -0.1875 to 0.1875
- w_out: bfloat16 [8, 1024, 1024], P('section'), may hold values from -0.1875 to 0.1875
Outputs:
- grad_qkv: float32 [8, 1024, 1536], P('section', 'dp')
- grad_out: float32 [8, 1024, 1024], P('section', 'dp')
The draws below stay inside these ranges and needn't reach their ends.
All inputs are finite; a program needn't handle non-finite values.
Results may differ from the reference program's by a relative error of at most 0.039.
Values may be sent and summed in bfloat16 or wider, within the bound.
A program may use at most 128 MiB of HBM per device.

```python
import math
import jax
import jax.numpy as jnp
from jax import lax

D = 1024
HD = 64
QH = 16
KH = 4
SEQ = 128
M = 1
LAYERS = 8
REPLICAS = 16
QW = 1024
QKV = 1536


def draw_inputs(key, part):
    key = jax.random.fold_in(key, 7)
    noise_key, row_key, column_key = jax.random.split(key, 3)
    shape = (REPLICAS, 2, M, SEQ, D)
    row_scale = jnp.exp(jax.random.uniform(row_key, (REPLICAS, 2, M, SEQ, 1), jnp.float32, 0.0, math.log(10.0)))
    column_scale = jnp.exp(jax.random.uniform(column_key, (1, 1, 1, 1, D), jnp.float32, 0.0, math.log(10.0)))
    base = jnp.clip(jax.random.normal(noise_key, shape, jnp.float32), -4.0, 4.0)
    return (0.3 * base * row_scale * column_scale).astype(jnp.bfloat16)


def spiked(drawn, own_key, source, target, blocks, factor):
    def block_of(axis_at):
        return (jnp.arange(drawn.shape[axis_at]) // (drawn.shape[axis_at] // blocks)).reshape((-1,) + (1,) * (drawn.ndim - 1 - axis_at))

    first = jax.random.permutation(own_key, blocks)[block_of(target)]
    other_side = (block_of(target) + blocks // 2) % blocks
    return jnp.where((block_of(source) == first) | (block_of(source) == other_side), factor * drawn, drawn)


def block_levels(rng, dims, cuts, low, largest):
    def one(axis_at, blocks):
        steps = jax.random.uniform(jax.random.fold_in(jax.random.fold_in(rng, 6), axis_at), (blocks,), jnp.float32, low / len(cuts), largest / len(cuts))
        return jnp.repeat(jnp.exp(steps), dims[axis_at] // blocks).reshape((-1,) + (1,) * (len(dims) - axis_at - 1))

    factor_of = one(*cuts[0])
    for cut in cuts[1:]:
        factor_of = factor_of * one(*cut)
    return factor_of


def noise(own_key, shape, scale, most, cuts=(), kind=jnp.bfloat16):
    values = scale * jax.random.normal(own_key, shape, jnp.float32)
    if cuts:
        values = values * block_levels(own_key, shape, cuts, -0.22, 0.18)
    return jnp.clip(values, -most, most).astype(kind)


def heavy_noise(rng, dims, width, most, cuts, heavy, held_as=jnp.bfloat16):
    entries = width * jax.random.normal(rng, dims, jnp.float32)
    if cuts:
        entries = entries * block_levels(rng, dims, cuts, -0.22, 0.18)
    return jnp.clip(spiked(entries, jax.random.fold_in(rng, 3), *heavy), -most, most).astype(held_as)


def setup_inputs(seed: int = 0) -> dict:
    key_list = jax.random.split(jax.random.key(seed), 5)
    inputs = draw_inputs(jax.random.fold_in(key_list[4], 71), 0)
    cotangent = heavy_noise(key_list[1], (REPLICAS, 2, M, SEQ, D), 0.05, 0.4375, ((0, 16),), (0, 4, 16, 2.0))
    w_qkv = noise(key_list[2], (LAYERS, D, QKV), D ** -0.5, 0.1875, ((0, 8),))
    w_out = noise(key_list[3], (LAYERS, D, QW), QW ** -0.5, 0.1875, ((0, 8),))
    return dict(inputs=inputs, cotangent=cotangent, w_qkv=w_qkv, w_out=w_out)


EPSILON = 1e-05

def split_heads(joined):
    leading = joined.shape[:2]
    q_width = QH * HD
    kv_width = KH * HD
    queries = joined[..., :q_width].reshape(leading + (KH, QH // KH, HD))
    key_heads = joined[..., q_width:q_width + kv_width].reshape(leading + (KH, HD))
    value_heads = joined[..., q_width + kv_width:].reshape(leading + (KH, HD))
    return (queries, key_heads, value_heads)

def layer_forward(hidden, weight_qkv, weight_out):
    leading = hidden.shape[:2]
    seq_len = hidden.shape[1]
    widened = hidden.astype(jnp.float32)
    inverse = lax.rsqrt(lax.optimization_barrier(jnp.mean(widened * widened, axis=-1, keepdims=True)) + EPSILON)
    normed = (widened * inverse).astype(jnp.bfloat16)
    joined = jnp.einsum('btd,do->bto', normed.astype(jnp.float32), weight_qkv.astype(jnp.float32)).astype(jnp.bfloat16)
    queries, key_heads, value_heads = split_heads(joined)
    scores = jnp.einsum('bikgd,bjkd->bkgij', queries.astype(jnp.float32), key_heads.astype(jnp.float32)) * HD ** (-0.5)
    causal = jnp.tril(jnp.ones((seq_len, seq_len), dtype=jnp.bool_))
    exponent = jnp.where(causal, jnp.exp(scores), 0.0)
    attn_probs = (exponent / lax.optimization_barrier(jnp.sum(exponent, axis=-1, keepdims=True))).astype(jnp.bfloat16)
    mixture = jnp.einsum('bkgij,bjkd->bikgd', attn_probs.astype(jnp.float32), value_heads.astype(jnp.float32))
    attention = mixture.reshape(leading + (QH * HD,)).astype(jnp.bfloat16)
    update = jnp.einsum('btq,dq->btd', attention.astype(jnp.float32), weight_out.astype(jnp.float32))
    result = (widened + update).astype(jnp.bfloat16)
    return (result, normed, joined, attn_probs, attention)

def layer_backward(cotangents, hidden, weight_qkv, weight_out, joined, attn_probs):
    leading = joined.shape[:2]
    queries, key_heads, value_heads = split_heads(joined)
    d_attention = jnp.einsum('btd,dq->btq', cotangents.astype(jnp.float32), weight_out.astype(jnp.float32)).astype(jnp.bfloat16)
    d_heads = d_attention.reshape(leading + (KH, QH // KH, HD)).astype(jnp.float32)
    probs_wide = attn_probs.astype(jnp.float32)
    d_probs = jnp.einsum('bikgd,bjkd->bkgij', d_heads, value_heads.astype(jnp.float32))
    d_values = jnp.einsum('bkgij,bikgd->bjkd', probs_wide, d_heads)
    d_scores = (probs_wide * (d_probs - lax.optimization_barrier(jnp.sum(probs_wide * d_probs, axis=-1, keepdims=True))) * HD ** (-0.5)).astype(jnp.bfloat16)
    d_queries = jnp.einsum('bkgij,bjkd->bikgd', d_scores.astype(jnp.float32), key_heads.astype(jnp.float32))
    d_keys = jnp.einsum('bkgij,bikgd->bjkd', d_scores.astype(jnp.float32), queries.astype(jnp.float32))
    d_joined = jnp.concatenate([d_queries.reshape(leading + (QH * HD,)), d_keys.reshape(leading + (KH * HD,)), d_values.reshape(leading + (KH * HD,))], axis=-1).astype(jnp.bfloat16)
    d_normed = jnp.einsum('bto,do->btd', d_joined.astype(jnp.float32), weight_qkv.astype(jnp.float32))
    widened = hidden.astype(jnp.float32)
    inverse = lax.rsqrt(lax.optimization_barrier(jnp.mean(widened * widened, axis=-1, keepdims=True)) + EPSILON)
    scaled = widened * inverse
    d_hidden = (cotangents.astype(jnp.float32) + inverse * (d_normed - scaled * lax.optimization_barrier(jnp.mean(d_normed * scaled, axis=-1, keepdims=True)))).astype(jnp.bfloat16)
    return (d_hidden, d_joined)

def reference(inputs, cotangent, w_qkv, w_out):
    replica_count = inputs.shape[0]
    sequences = replica_count * 2 * M
    hidden = inputs.reshape(sequences, SEQ, D)
    layer_count = w_qkv.shape[0]
    stored = []
    for layer_index in range(layer_count):
        result, normed, joined, attn_probs, attention = layer_forward(hidden, w_qkv[layer_index], w_out[layer_index])
        stored.append((hidden, normed, joined, attn_probs, attention))
        hidden = result
    cotangents = cotangent.reshape(sequences, SEQ, D)
    grads_qkv = [None] * layer_count
    grads_out = [None] * layer_count
    for layer_index in reversed(range(layer_count)):
        layer_input, normed, joined, attn_probs, attention = stored[layer_index]
        grads_out[layer_index] = jnp.einsum('btd,btq->dq', cotangents.astype(jnp.float32), attention.astype(jnp.float32))
        d_hidden, d_joined = layer_backward(cotangents, layer_input, w_qkv[layer_index], w_out[layer_index], joined, attn_probs)
        grads_qkv[layer_index] = jnp.einsum('btd,bto->do', normed.astype(jnp.float32), d_joined.astype(jnp.float32))
        cotangents = d_hidden
    return (jnp.stack(grads_qkv), jnp.stack(grads_out))
```

```python
import functools

import jax
import jax.numpy as jnp
from jax import lax
from jax.experimental import pallas as pl
from jax.experimental.pallas import tpu as pltpu
from jax.sharding import PartitionSpec as P

MESH = pl.DeviceIdType.MESH
F32 = jnp.float32
BF16 = jnp.bfloat16
EPSILON = 1e-05

D = 1024
SEQ = 128
QKV = 1536
COLS = 2560
HALF = 1280
QUARTER = 640
CHUNK = 64


def mm(a, b):
    return jnp.dot(a, b, preferred_element_type=F32)


def mm_nt(a, b):
    return lax.dot_general(a, b, (((1,), (1,)), ((), ())), preferred_element_type=F32)


def mm_tn(a, b):
    return lax.dot_general(a, b, (((0,), (0,)), ((), ())), preferred_element_type=F32)


def block_diagonal(pair, group):
    low = lax.broadcasted_iota(jnp.int32, pair.shape, 1) < 64
    wide = pair.astype(F32)
    rolled = pltpu.roll(wide, 64, 1)
    first, second = (wide, rolled) if group % 2 == 0 else (rolled, wide)
    zero = jnp.zeros_like(wide)
    return jnp.concatenate([jnp.where(low, first, zero), jnp.where(low, zero, second)], axis=0).astype(BF16)


def half_sums(x):
    return (jnp.sum(x[:, :128], axis=1, keepdims=True), jnp.sum(x[:, 128:], axis=1, keepdims=True))


def stack_pairs(x, group):
    at = group * 256
    return jnp.concatenate([x[:, at : at + 128], x[:, at + 128 : at + 256]], axis=0)


def kv_pairs(joined, group):
    at = (group // 2) * 128
    return joined[:, D + at : D + at + 128], joined[:, D + 256 + at : D + 256 + at + 128]


def attention_forward(joined, probs_ref, att_ref, layer):
    rows = lax.broadcasted_iota(jnp.int32, (256, 256), 0) & 127
    cols = lax.broadcasted_iota(jnp.int32, (256, 256), 1) & 127
    causal = rows >= cols
    for group in range(4):
        queries = stack_pairs(joined, group)
        keys, values = kv_pairs(joined, group)
        scores = mm_nt(queries, block_diagonal(keys, group)) * 0.125
        exponent = jnp.where(causal, jnp.exp(scores), 0.0)
        left, right = half_sums(exponent)
        probs = jnp.concatenate([exponent[:, :128] / left, exponent[:, 128:] / right], axis=1).astype(BF16)
        probs_ref[layer, group] = probs
        mixed = mm(probs, block_diagonal(values, group)).astype(BF16)
        at = group * 256
        att_ref[layer, 0:SEQ, at : at + 128] = mixed[:128]
        att_ref[layer, 0:SEQ, at + 128 : at + 256] = mixed[128:]


def attention_backward(joined, d_attention, probs_ref, dj_ref, layer):
    d_keys, d_values = [], []
    for group in range(4):
        queries = stack_pairs(joined, group)
        d_heads = stack_pairs(d_attention, group)
        keys, values = kv_pairs(joined, group)
        probs = probs_ref[layer, group]
        d_probs = mm_nt(d_heads, block_diagonal(values, group))
        wide = probs.astype(F32)
        left, right = half_sums(wide * d_probs)
        centred = jnp.concatenate([d_probs[:, :128] - left, d_probs[:, 128:] - right], axis=1)
        d_scores = (wide * centred * 0.125).astype(BF16)
        d_queries = mm(d_scores, block_diagonal(keys, group)).astype(BF16)
        at = group * 256
        dj_ref[layer, 0:SEQ, at : at + 128] = d_queries[:128]
        dj_ref[layer, 0:SEQ, at + 128 : at + 256] = d_queries[128:]
        d_keys.append(mm_tn(d_scores, queries))
        d_values.append(mm_tn(probs, d_heads))
    low = lax.broadcasted_iota(jnp.int32, (128, 128), 1) < 64

    def merged(even, odd):
        first = even[:128] + pltpu.roll(even[128:], 64, 1)
        second = pltpu.roll(odd[:128], 64, 1) + odd[128:]
        return jnp.where(low, first, second).astype(BF16)

    for pair in range(2):
        at = D + pair * 128
        dj_ref[layer, 0:SEQ, at : at + 128] = merged(d_keys[2 * pair], d_keys[2 * pair + 1])
        dj_ref[layer, 0:SEQ, at + 256 : at + 384] = merged(d_values[2 * pair], d_values[2 * pair + 1])


def inverse_norm(wide):
    return lax.rsqrt(jnp.mean(wide * wide, axis=-1, keepdims=True) + EPSILON)


def kernel(
    inputs_ref, cotangent_ref, wq_ref, wo_ref,
    gq_ref, go_ref,
    wq, wo, hidden, normed, joined, probs, att, upstream, dj, grads,
    z_a1, z_b1, z_m2, z_p2, z_r, z_sa1, z_sb1, z_sm2, z_sp2,
    x_a1, x_b1, x_m2, x_p2, x_r, x_sa1, x_sb1, x_sm2, x_sp2,
    load_sem, flip_send, flip_recv, spread_send, spread_recv, core_send, core_recv,
    hop_send, hop_recv, share_send, share_recv, sum_send, sum_recv,
):
    section, dp = lax.axis_index("section"), lax.axis_index("dp")
    y, x_hi = lax.div(section, 2), lax.rem(section, 2)
    z, x_lo, core = lax.div(dp, 4), lax.rem(lax.div(dp, 2), 2), lax.rem(dp, 2)
    x = 2 * x_hi + x_lo

    def place(y, x, z, core):
        return (2 * y + lax.div(x, 2), 4 * z + 2 * lax.rem(x, 2) + core)

    core_dev = place(y, x, z, 1 - core)
    xp_dev, xm_dev = place(y, lax.rem(x + 1, 4), z, core), place(y, lax.rem(x + 3, 4), z, core)
    zp_dev, zm_dev = place(y, x, lax.rem(z + 1, 4), core), place(y, x, lax.rem(z + 3, 4), core)
    yp_dev, ym_dev = place(lax.rem(y + 1, 4), x, z, core), place(lax.rem(y + 3, 4), x, z, core)
    flip_dev = place(y, 3 - x, z, core)
    side_dev = place(y, 2 * x_hi + 1 - x_lo, z, core)

    def remote(src, dst, send_sem, recv_sem, device):
        return pltpu.make_async_remote_copy(
            src_ref=src, dst_ref=dst, send_sem=send_sem, recv_sem=recv_sem, device_id=device, device_id_type=MESH
        )

    sent = []

    def go(copy):
        copy.start()
        sent.append(copy)

    loads = [
        pltpu.make_async_copy(wq_ref.at[0], wq.at[x_hi], load_sem.at[0]),
        pltpu.make_async_copy(wo_ref.at[0], wo.at[x_hi], load_sem.at[1]),
    ]
    load_in = pltpu.make_async_copy(inputs_ref.at[0, x_hi, 0], hidden.at[0], load_sem.at[2])
    load_cot = pltpu.make_async_copy(cotangent_ref.at[0, x_hi, 0], upstream.at[2, 0:SEQ], load_sem.at[3])
    for copy in loads:
        copy.start()

    @pl.when(y == 0)
    def _():
        load_in.start()

    @pl.when(y == 3)
    def _():
        load_cot.start()

    barrier = pltpu.get_barrier_semaphore()
    for device in (core_dev, xp_dev, xm_dev, zp_dev, zm_dev, yp_dev, ym_dev):
        pl.semaphore_signal(barrier, inc=1, device_id=device, device_id_type=MESH)
    pl.semaphore_wait(barrier, 7)

    other = 1 - x_hi
    piece = lax.rem(z + 2 * x_lo, 4)
    pieces = [lax.rem(piece + k, 4) for k in range(4)]

    def chunk_rows(which, half, part):
        return pl.ds(pl.multiple_of(which * 256 + half * 128 + (part % 2) * CHUNK, CHUNK), CHUNK)

    def chunk(buf_q, buf_o, slot, which, half, part):
        rows = chunk_rows(which, half, part)
        return (buf_q if part < 2 else buf_o).at[slot, rows]

    for part in range(4):
        src = chunk(wq_ref, wo_ref, 0, pieces[2], core, part)
        go(remote(src, chunk(wq, wo, x_hi, pieces[2], core, part), flip_send.at[part], flip_recv.at[part], flip_dev))

    def await_flip(part):
        block = chunk(wq, wo, other, pieces[0], core, part)
        remote(block, block, flip_send.at[part], flip_recv.at[part], flip_dev).wait_recv()

    def spread(part):
        block = chunk(wq, wo, other, pieces[0], core, part)
        for slot, device in ((1, zm_dev), (2, side_dev), (3, zp_dev)):
            go(remote(block, block, spread_send.at[part, slot], spread_recv.at[part, slot], device))

    def to_core(part, k):
        block = chunk(wq, wo, other, pieces[k], core, part)
        go(remote(block, block, core_send.at[part, k], core_recv.at[part, k], core_dev))

    def gather_rest(part):
        for k in (1, 2, 3):
            block = chunk(wq, wo, other, pieces[k], core, part)
            remote(block, block, spread_send.at[part, k], spread_recv.at[part, k], side_dev).wait_recv()
            to_core(part, k)

    for part in range(4):
        await_flip(part)
        spread(part)
        to_core(part, 0)
        if part > 0:
            gather_rest(part - 1)
    gather_rest(3)
    for part in range(4):
        for k in range(4):
            block = chunk(wq, wo, other, pieces[k], 1 - core, part)
            remote(block, block, core_send.at[part, k], core_recv.at[part, k], core_dev).wait_recv()
    for copy in loads:
        copy.wait()

    h_hop = remote(hidden.at[2], hidden.at[0], hop_send.at[0], hop_recv.at[0], yp_dev)
    c_hop = remote(upstream.at[0, 0:SEQ], upstream.at[2, 0:SEQ], hop_send.at[1], hop_recv.at[1], ym_dev)

    @pl.when(y == 0)
    def _():
        load_in.wait()

    @pl.when(y > 0)
    def _():
        h_hop.wait_recv()

    def forward(layer, carry):
        h = hidden[layer]
        wide = h.astype(F32)
        inverse = inverse_norm(wide)
        normed[layer, 0:SEQ] = (wide * inverse).astype(BF16)
        joined[layer] = (mm(h, wq[layer]) * inverse).astype(BF16)
        attention_forward(joined[layer], probs, att, layer)
        hidden[layer + 1] = (wide + mm_nt(att[layer, 0:SEQ], wo[layer])).astype(BF16)
        return carry

    lax.fori_loop(0, 2, forward, 0)

    @pl.when(y < 3)
    def _():
        h_hop.start()

    def share(buf, slot, number):
        go(remote(buf.at[slot, 0:SEQ], buf.at[slot, SEQ : 2 * SEQ], share_send.at[number], share_recv.at[number], core_dev))

    shared = [(normed, 0), (normed, 1), (att, 0), (att, 1), (upstream, 2), (upstream, 1), (dj, 1), (dj, 0)]
    for number in range(4):
        share(*shared[number], number)

    @pl.when(y == 3)
    def _():
        load_cot.wait()

    @pl.when(y < 3)
    def _():
        c_hop.wait_recv()

    def backward(step, carry):
        layer = 1 - step
        c = upstream[layer + 1, 0:SEQ]
        d_attention = mm(c, wo[layer]).astype(BF16)
        attention_backward(joined[layer], d_attention, probs, dj, layer)
        d_normed = mm_nt(dj[layer, 0:SEQ], wq[layer])
        wide = hidden[layer].astype(F32)
        inverse = inverse_norm(wide)
        scaled = wide * inverse
        along = jnp.mean(d_normed * scaled, axis=-1, keepdims=True)
        upstream[layer, 0:SEQ] = (c.astype(F32) + inverse * (d_normed - scaled * along)).astype(BF16)
        return carry

    lax.fori_loop(0, 2, backward, 0)

    @pl.when(y > 0)
    def _():
        c_hop.start()

    for number in range(4, 8):
        share(*shared[number], number)
    for number, (buf, slot) in enumerate(shared):
        remote(
            buf.at[slot, 0:SEQ], buf.at[slot, SEQ : 2 * SEQ], share_send.at[number], share_recv.at[number], core_dev
        ).wait_recv()

    low = lax.broadcasted_iota(jnp.int32, (2 * SEQ, 128), 1) < 64

    def own_columns(block):
        def tile(k):
            return block[:, 128 * k : 128 * k + 128].astype(F32)

        tiles = []
        for lo in range(2):
            for pair in range(2):
                a, b = tile(4 * pair + lo), tile(4 * pair + 2 + lo)
                first = jnp.where(core == 0, a, pltpu.roll(a, 64, 1))
                second = jnp.where(core == 0, pltpu.roll(b, 64, 1), b)
                tiles.append(jnp.where(low, first, second).astype(BF16))
        return jnp.concatenate(tiles, axis=1)

    for layer in (1, 0):
        left = own_columns(normed[layer])
        for lo in range(2):
            part = mm_tn(left[:, 256 * lo : 256 * lo + 256], dj[layer]).astype(BF16)
            grads[2 * layer + lo, :, :, 0:QKV] = part.reshape(4, 64, QKV)
        left = own_columns(upstream[layer + 1])
        for lo in range(2):
            part = mm_tn(left[:, 256 * lo : 256 * lo + 256], att[layer]).astype(BF16)
            grads[2 * layer + lo, :, :, QKV:COLS] = part.reshape(4, 64, D)

    def ring_sum(view, position, plus, minus, bufs, sems):
        a1, b1, m2, p2, alpha, beta = bufs
        opposite, after, before = (lax.rem(position + k, 4) for k in (2, 1, 3))
        s, r = sum_send.at, sum_recv.at

        def first():
            go(remote(view(opposite, 0), a1, s[sems], r[sems], plus))
            go(remote(view(opposite, 1), b1, s[sems + 1], r[sems + 1], minus))
            go(remote(view(after, 1), m2.at[beta], s[sems + 2], r[sems + 2], plus))
            go(remote(view(before, 0), p2.at[alpha], s[sems + 3], r[sems + 3], minus))

        def second():
            mine = view(after, 0)
            remote(mine, a1, s[sems], r[sems], plus).wait_recv()
            mine[...] = (mine[...].astype(F32) + a1[...].astype(F32)).astype(BF16)
            go(remote(mine, m2.at[alpha], s[sems + 4], r[sems + 4], plus))
            mine = view(before, 1)
            remote(mine, b1, s[sems + 1], r[sems + 1], minus).wait_recv()
            mine[...] = (mine[...].astype(F32) + b1[...].astype(F32)).astype(BF16)
            go(remote(mine, p2.at[beta], s[sems + 5], r[sems + 5], minus))

        def last():
            remote(view(after, 1), m2.at[beta], s[sems + 2], r[sems + 2], plus).wait_recv()
            remote(view(before, 0), p2.at[alpha], s[sems + 3], r[sems + 3], minus).wait_recv()
            remote(view(after, 0), m2.at[alpha], s[sems + 4], r[sems + 4], plus).wait_recv()
            remote(view(before, 1), p2.at[beta], s[sems + 5], r[sems + 5], minus).wait_recv()

        return first, second, last

    def halves(offset):
        return [pl.ds(offset, QUARTER), pl.ds(offset + QUARTER, QUARTER)]

    z_cols, x_cols, own_cols = halves(0), halves(HALF), halves(0)
    wide_at = [(slice(None), slice(None), cols) for cols in own_cols]
    flat_at = [(slice(None), cols) for cols in own_cols]
    z_big = ring_sum(
        lambda t, k: grads.at[:, t, :, z_cols[k]], z, zp_dev, zm_dev, (z_a1, z_b1, z_m2, z_p2, *wide_at), 0
    )
    x_big = ring_sum(
        lambda t, k: grads.at[t, :, :, x_cols[k]], x, xp_dev, xm_dev, (x_a1, x_b1, x_m2, x_p2, *wide_at), 6
    )
    z_small = ring_sum(
        lambda t, k: z_r.at[t, :, own_cols[k]], x, xp_dev, xm_dev, (z_sa1, z_sb1, z_sm2, z_sp2, *flat_at), 12
    )
    x_small = ring_sum(
        lambda t, k: x_r.at[t, :, own_cols[k]], z, zp_dev, zm_dev, (x_sa1, x_sb1, x_sm2, x_sp2, *flat_at), 18
    )
    z_big[0]()
    x_big[0]()
    z_big[1]()
    x_big[1]()
    z_big[2]()
    z_r[...] = (grads[:, z, :, 0:HALF].astype(F32) + z_m2[...].astype(F32) + z_p2[...].astype(F32)).astype(BF16)
    z_small[0]()
    x_big[2]()
    x_r[...] = (grads[x, :, :, HALF:COLS].astype(F32) + x_m2[...].astype(F32) + x_p2[...].astype(F32)).astype(BF16)
    x_small[0]()
    z_small[1]()
    x_small[1]()
    z_small[2]()
    gq_ref[0, :, 0:HALF] = z_r[x].astype(F32) + z_sm2[...].astype(F32) + z_sp2[...].astype(F32)
    x_small[2]()
    total = x_r[z].astype(F32) + x_sm2[...].astype(F32) + x_sp2[...].astype(F32)
    gq_ref[0, :, HALF:QKV] = total[:, : QKV - HALF]
    go_ref[0] = total[:, QKV - HALF :]

    for copy in sent:
        copy.wait_send()

    @pl.when(y < 3)
    def _():
        h_hop.wait_send()

    @pl.when(y > 0)
    def _():
        c_hop.wait_send()


def on_device(inputs, cotangent, w_qkv, w_out):
    any_space = pl.BlockSpec(memory_space=pl.ANY)
    vmem = pl.BlockSpec(memory_space=pltpu.VMEM)
    dma = pltpu.SemaphoreType.DMA

    def flow():
        return [
            pltpu.VMEM((4, 64, QUARTER), BF16),
            pltpu.VMEM((4, 64, QUARTER), BF16),
            pltpu.VMEM((4, 64, HALF), BF16),
            pltpu.VMEM((4, 64, HALF), BF16),
            pltpu.VMEM((4, 64, HALF), BF16),
            pltpu.VMEM((64, QUARTER), BF16),
            pltpu.VMEM((64, QUARTER), BF16),
            pltpu.VMEM((64, HALF), BF16),
            pltpu.VMEM((64, HALF), BF16),
        ]

    return pl.pallas_call(
        kernel,
        out_shape=(jax.ShapeDtypeStruct((1, 64, QKV), F32), jax.ShapeDtypeStruct((1, 64, D), F32)),
        in_specs=[any_space] * 4,
        out_specs=(vmem, vmem),
        scratch_shapes=[
            pltpu.VMEM((2, D, QKV), BF16),
            pltpu.VMEM((2, D, D), BF16),
            pltpu.VMEM((3, SEQ, D), BF16),
            pltpu.VMEM((2, 2 * SEQ, D), BF16),
            pltpu.VMEM((2, SEQ, QKV), BF16),
            pltpu.VMEM((2, 4, 256, 256), BF16),
            pltpu.VMEM((2, 2 * SEQ, D), BF16),
            pltpu.VMEM((3, 2 * SEQ, D), BF16),
            pltpu.VMEM((2, 2 * SEQ, QKV), BF16),
            pltpu.VMEM((4, 4, 64, COLS), BF16),
            *flow(),
            *flow(),
            dma((4,)),
            dma((4,)),
            dma((4,)),
            dma((4, 4)),
            dma((4, 4)),
            dma((4, 4)),
            dma((4, 4)),
            dma((2,)),
            dma((2,)),
            dma((8,)),
            dma((8,)),
            dma((24,)),
            dma((24,)),
        ],
        compiler_params=pltpu.CompilerParams(
            collective_id=0, has_side_effects=True, vmem_limit_bytes=56 * 2**20
        ),
    )(inputs, cotangent, w_qkv, w_out)


def solution(mesh):
    placed = (
        P("dp", None, None, None, None),
        P("dp", None, None, None, None),
        P("section", None, None),
        P("section", None, None),
    )
    return jax.shard_map(
        on_device,
        mesh=mesh,
        in_specs=placed,
        out_specs=(P("section", "dp", None), P("section", "dp", None)),
        check_vma=False,
    )
```

```python
import functools

import jax
import jax.numpy as jnp
from jax import lax
from jax.experimental import pallas as pl
from jax.experimental.pallas import tpu as pltpu
from jax.sharding import PartitionSpec as P

MESH = pl.DeviceIdType.MESH
F32 = jnp.float32
BF16 = jnp.bfloat16
EPSILON = 1e-05

D = 1024
SEQ = 128
QKV = 1536
COLS = 2560
HALF = 1280
QUARTER = 640
CHUNK = 64


def mm(a, b):
    return jnp.dot(a, b, preferred_element_type=F32)


def mm_nt(a, b):
    return lax.dot_general(a, b, (((1,), (1,)), ((), ())), preferred_element_type=F32)


def mm_tn(a, b):
    return lax.dot_general(a, b, (((0,), (0,)), ((), ())), preferred_element_type=F32)


def block_diagonal(pair, group):
    low = lax.broadcasted_iota(jnp.int32, pair.shape, 1) < 64
    wide = pair.astype(F32)
    rolled = pltpu.roll(wide, 64, 1)
    first, second = (wide, rolled) if group % 2 == 0 else (rolled, wide)
    zero = jnp.zeros_like(wide)
    return jnp.concatenate([jnp.where(low, first, zero), jnp.where(low, zero, second)], axis=0).astype(BF16)


def half_sums(x):
    return (jnp.sum(x[:, :128], axis=1, keepdims=True), jnp.sum(x[:, 128:], axis=1, keepdims=True))


def stack_pairs(x, group):
    at = group * 256
    return jnp.concatenate([x[:, at : at + 128], x[:, at + 128 : at + 256]], axis=0)


def kv_pairs(joined, group):
    at = (group // 2) * 128
    return joined[:, D + at : D + at + 128], joined[:, D + 256 + at : D + 256 + at + 128]


def attention_forward(joined, probs_ref, att_ref, layer):
    rows = lax.broadcasted_iota(jnp.int32, (256, 256), 0) & 127
    cols = lax.broadcasted_iota(jnp.int32, (256, 256), 1) & 127
    causal = rows >= cols
    for group in range(4):
        queries = stack_pairs(joined, group)
        keys, values = kv_pairs(joined, group)
        scores = mm_nt(queries, block_diagonal(keys, group)) * 0.125
        exponent = jnp.where(causal, jnp.exp(scores), 0.0)
        left, right = half_sums(exponent)
        probs = jnp.concatenate([exponent[:, :128] / left, exponent[:, 128:] / right], axis=1).astype(BF16)
        probs_ref[layer, group] = probs
        mixed = mm(probs, block_diagonal(values, group)).astype(BF16)
        at = group * 256
        att_ref[layer, 0:SEQ, at : at + 128] = mixed[:128]
        att_ref[layer, 0:SEQ, at + 128 : at + 256] = mixed[128:]


def attention_backward(joined, d_attention, probs_ref, dj_ref, layer):
    d_keys, d_values = [], []
    for group in range(4):
        queries = stack_pairs(joined, group)
        d_heads = stack_pairs(d_attention, group)
        keys, values = kv_pairs(joined, group)
        probs = probs_ref[layer, group]
        d_probs = mm_nt(d_heads, block_diagonal(values, group))
        wide = probs.astype(F32)
        left, right = half_sums(wide * d_probs)
        centred = jnp.concatenate([d_probs[:, :128] - left, d_probs[:, 128:] - right], axis=1)
        d_scores = (wide * centred * 0.125).astype(BF16)
        d_queries = mm(d_scores, block_diagonal(keys, group)).astype(BF16)
        at = group * 256
        dj_ref[layer, 0:SEQ, at : at + 128] = d_queries[:128]
        dj_ref[layer, 0:SEQ, at + 128 : at + 256] = d_queries[128:]
        d_keys.append(mm_tn(d_scores, queries))
        d_values.append(mm_tn(probs, d_heads))
    low = lax.broadcasted_iota(jnp.int32, (128, 128), 1) < 64

    def merged(even, odd):
        first = even[:128] + pltpu.roll(even[128:], 64, 1)
        second = pltpu.roll(odd[:128], 64, 1) + odd[128:]
        return jnp.where(low, first, second).astype(BF16)

    for pair in range(2):
        at = D + pair * 128
        dj_ref[layer, 0:SEQ, at : at + 128] = merged(d_keys[2 * pair], d_keys[2 * pair + 1])
        dj_ref[layer, 0:SEQ, at + 256 : at + 384] = merged(d_values[2 * pair], d_values[2 * pair + 1])


def inverse_norm(wide):
    return lax.rsqrt(jnp.mean(wide * wide, axis=-1, keepdims=True) + EPSILON)


def kernel(
    inputs_ref, cotangent_ref, wq_ref, wo_ref,
    gq_ref, go_ref,
    wq, wo, entry, passed, hidden, normed, joined, probs, att, upstream, dj, grads,
    z_a1, z_b1, z_m2, z_p2, z_r, z_sa1, z_sb1, z_sm2, z_sp2,
    x_a1, x_b1, x_m2, x_p2, x_r, x_sa1, x_sb1, x_sm2, x_sp2,
    load_sem, flip_send, flip_recv, spread_send, spread_recv, core_send, core_recv,
    entry_send, entry_recv, hop_send, hop_recv, share_send, share_recv, sum_send, sum_recv,
):
    section, dp = lax.axis_index("section"), lax.axis_index("dp")
    y, x_hi = lax.div(section, 2), lax.rem(section, 2)
    z, x_lo, core = lax.div(dp, 4), lax.rem(lax.div(dp, 2), 2), lax.rem(dp, 2)
    x = 2 * x_hi + x_lo

    def place(y, x, z, core):
        return (2 * y + lax.div(x, 2), 4 * z + 2 * lax.rem(x, 2) + core)

    core_dev = place(y, x, z, 1 - core)
    xp_dev, xm_dev = place(y, lax.rem(x + 1, 4), z, core), place(y, lax.rem(x + 3, 4), z, core)
    zp_dev, zm_dev = place(y, x, lax.rem(z + 1, 4), core), place(y, x, lax.rem(z + 3, 4), core)
    yp_dev, ym_dev = place(lax.rem(y + 1, 4), x, z, core), place(lax.rem(y + 3, 4), x, z, core)
    flip_dev = place(y, 3 - x, z, core)
    side_dev = place(y, 2 * x_hi + 1 - x_lo, z, core)
    up_across_dev, down_across_dev = place(lax.rem(y + 1, 4), 3 - x, z, core), place(lax.rem(y + 3, 4), 3 - x, z, core)

    def remote(src, dst, send_sem, recv_sem, device):
        return pltpu.make_async_remote_copy(
            src_ref=src, dst_ref=dst, send_sem=send_sem, recv_sem=recv_sem, device_id=device, device_id_type=MESH
        )

    sent = []

    def go(copy):
        copy.start()
        sent.append(copy)

    loads = [
        pltpu.make_async_copy(wq_ref.at[0], wq.at[x_hi], load_sem.at[0]),
        pltpu.make_async_copy(wo_ref.at[0], wo.at[x_hi], load_sem.at[1]),
    ]
    load_in = pltpu.make_async_copy(inputs_ref.at[0, 0, 0], hidden.at[0], load_sem.at[2])
    load_cot = pltpu.make_async_copy(cotangent_ref.at[0, 0, 0], upstream.at[2, 0:SEQ], load_sem.at[3])
    load_entry = [pltpu.make_async_copy(inputs_ref.at[0, s, 0], entry.at[s], load_sem.at[4 + s]) for s in range(2)]
    for copy in loads:
        copy.start()

    near, far = x_hi == 0, x_hi == 1

    @pl.when((y == 0) & near)
    def _():
        load_entry[0].start()
        load_entry[1].start()
        load_in.start()

    @pl.when((y == 3) & near)
    def _():
        load_cot.start()

    barrier = pltpu.get_barrier_semaphore()
    for device in (core_dev, xp_dev, xm_dev, zp_dev, zm_dev, yp_dev, ym_dev, up_across_dev, down_across_dev):
        pl.semaphore_signal(barrier, inc=1, device_id=device, device_id_type=MESH)
    pl.semaphore_wait(barrier, 9)

    in_hop = remote(inputs_ref.at[0, 1, 0], hidden.at[0], hop_send.at[2], hop_recv.at[2], side_dev)
    cot_hop = remote(cotangent_ref.at[0, 1, 0], upstream.at[2, 0:SEQ], hop_send.at[3], hop_recv.at[3], side_dev)

    @pl.when((y == 0) & far)
    def _():
        in_hop.start()

    @pl.when((y == 3) & far)
    def _():
        cot_hop.start()

    h_hop = remote(hidden.at[2], hidden.at[0], hop_send.at[0], hop_recv.at[0], yp_dev)
    c_hop = remote(upstream.at[0, 0:SEQ], upstream.at[2, 0:SEQ], hop_send.at[1], hop_recv.at[1], ym_dev)

    def run_forward(h, weights, layer):
        wide = h.astype(F32)
        inverse = inverse_norm(wide)
        normed[layer, 0:SEQ] = (wide * inverse).astype(BF16)
        joined[layer] = (mm(h, wq[weights]) * inverse).astype(BF16)
        attention_forward(joined[layer], probs, att, layer)
        return (wide + mm_nt(att[layer, 0:SEQ], wo[weights])).astype(BF16)

    across = [remote(passed.at[s], entry.at[s], entry_send.at[s], entry_recv.at[s], flip_dev) for s in range(2)]
    onward = [
        remote(passed.at[0], hidden.at[0], entry_send.at[0], hop_recv.at[0], up_across_dev),
        remote(passed.at[1], hidden.at[0], entry_send.at[1], hop_recv.at[0], yp_dev),
    ]

    @pl.when(y == 0)
    def _():
        for copy in loads:
            copy.wait()

        def first_pass(s, carry):
            for k in range(2):
                @pl.when((s == k) & near)
                def _():
                    load_entry[k].wait()

                @pl.when((s == k) & far)
                def _():
                    across[k].wait_recv()

            passed[s] = run_forward(entry[s], x_hi, 0)
            for k in range(2):
                @pl.when((s == k) & near)
                def _():
                    across[k].start()

                @pl.when((s == k) & far)
                def _():
                    onward[k].start()

            return carry

        lax.fori_loop(0, 2, first_pass, 0)

        @pl.when(near)
        def _():
            for copy in across:
                copy.wait_send()

        @pl.when(far)
        def _():
            for copy in onward:
                copy.wait_send()

    other = 1 - x_hi
    piece = lax.rem(z + 2 * x_lo, 4)
    pieces = [lax.rem(piece + k, 4) for k in range(4)]

    def chunk_rows(which, half, part):
        return pl.ds(pl.multiple_of(which * 256 + half * 128 + (part % 2) * CHUNK, CHUNK), CHUNK)

    def chunk(buf_q, buf_o, slot, which, half, part):
        rows = chunk_rows(which, half, part)
        return (buf_q if part < 2 else buf_o).at[slot, rows]

    for part in range(4):
        src = chunk(wq_ref, wo_ref, 0, pieces[2], core, part)
        go(remote(src, chunk(wq, wo, x_hi, pieces[2], core, part), flip_send.at[part], flip_recv.at[part], flip_dev))

    def await_flip(part):
        block = chunk(wq, wo, other, pieces[0], core, part)
        remote(block, block, flip_send.at[part], flip_recv.at[part], flip_dev).wait_recv()

    def spread(part):
        block = chunk(wq, wo, other, pieces[0], core, part)
        for slot, device in ((1, zm_dev), (2, side_dev), (3, zp_dev)):
            go(remote(block, block, spread_send.at[part, slot], spread_recv.at[part, slot], device))

    def to_core(part, k):
        block = chunk(wq, wo, other, pieces[k], core, part)
        go(remote(block, block, core_send.at[part, k], core_recv.at[part, k], core_dev))

    def gather_rest(part):
        for k in (1, 2, 3):
            block = chunk(wq, wo, other, pieces[k], core, part)
            remote(block, block, spread_send.at[part, k], spread_recv.at[part, k], side_dev).wait_recv()
            to_core(part, k)

    for part in range(4):
        await_flip(part)
        spread(part)
        to_core(part, 0)
        if part > 0:
            gather_rest(part - 1)
    gather_rest(3)
    for part in range(4):
        for k in range(4):
            block = chunk(wq, wo, other, pieces[k], 1 - core, part)
            remote(block, block, core_send.at[part, k], core_recv.at[part, k], core_dev).wait_recv()

    @pl.when(y > 0)
    def _():
        for copy in loads:
            copy.wait()

    @pl.when((y == 0) & near)
    def _():
        load_in.wait()

    @pl.when((y == 0) & far)
    def _():
        in_hop.wait()

    @pl.when(y > 0)
    def _():
        h_hop.wait_recv()

    def forward(layer, carry):
        hidden[layer + 1] = run_forward(hidden[layer], layer, layer)
        return carry

    lax.fori_loop(0, 2, forward, 0)

    @pl.when((y > 0) & (y < 3))
    def _():
        h_hop.start()

    def share(buf, slot, number):
        go(remote(buf.at[slot, 0:SEQ], buf.at[slot, SEQ : 2 * SEQ], share_send.at[number], share_recv.at[number], core_dev))

    shared = [(normed, 0), (normed, 1), (att, 0), (att, 1), (upstream, 2), (upstream, 1), (dj, 1), (dj, 0)]
    for number in range(4):
        share(*shared[number], number)

    @pl.when((y == 3) & near)
    def _():
        load_cot.wait()

    @pl.when((y == 3) & far)
    def _():
        cot_hop.wait()

    @pl.when(y < 3)
    def _():
        c_hop.wait_recv()

    def backward(step, carry):
        layer = 1 - step
        c = upstream[layer + 1, 0:SEQ]
        d_attention = mm(c, wo[layer]).astype(BF16)
        attention_backward(joined[layer], d_attention, probs, dj, layer)
        d_normed = mm_nt(dj[layer, 0:SEQ], wq[layer])
        wide = hidden[layer].astype(F32)
        inverse = inverse_norm(wide)
        scaled = wide * inverse
        along = jnp.mean(d_normed * scaled, axis=-1, keepdims=True)
        upstream[layer, 0:SEQ] = (c.astype(F32) + inverse * (d_normed - scaled * along)).astype(BF16)
        return carry

    lax.fori_loop(0, 2, backward, 0)

    @pl.when(y > 0)
    def _():
        c_hop.start()

    for number in range(4, 8):
        share(*shared[number], number)
    for number, (buf, slot) in enumerate(shared):
        remote(
            buf.at[slot, 0:SEQ], buf.at[slot, SEQ : 2 * SEQ], share_send.at[number], share_recv.at[number], core_dev
        ).wait_recv()

    low = lax.broadcasted_iota(jnp.int32, (2 * SEQ, 128), 1) < 64

    def own_columns(block):
        def tile(k):
            return block[:, 128 * k : 128 * k + 128].astype(F32)

        tiles = []
        for lo in range(2):
            for pair in range(2):
                a, b = tile(4 * pair + lo), tile(4 * pair + 2 + lo)
                first = jnp.where(core == 0, a, pltpu.roll(a, 64, 1))
                second = jnp.where(core == 0, pltpu.roll(b, 64, 1), b)
                tiles.append(jnp.where(low, first, second).astype(BF16))
        return jnp.concatenate(tiles, axis=1)

    for layer in (1, 0):
        left = own_columns(normed[layer])
        for lo in range(2):
            part = mm_tn(left[:, 256 * lo : 256 * lo + 256], dj[layer]).astype(BF16)
            grads[2 * layer + lo, :, :, 0:QKV] = part.reshape(4, 64, QKV)
        left = own_columns(upstream[layer + 1])
        for lo in range(2):
            part = mm_tn(left[:, 256 * lo : 256 * lo + 256], att[layer]).astype(BF16)
            grads[2 * layer + lo, :, :, QKV:COLS] = part.reshape(4, 64, D)

    def ring_sum(view, position, plus, minus, bufs, sems):
        a1, b1, m2, p2, alpha, beta = bufs
        opposite, after, before = (lax.rem(position + k, 4) for k in (2, 1, 3))
        s, r = sum_send.at, sum_recv.at

        def first():
            go(remote(view(opposite, 0), a1, s[sems], r[sems], plus))
            go(remote(view(opposite, 1), b1, s[sems + 1], r[sems + 1], minus))
            go(remote(view(after, 1), m2.at[beta], s[sems + 2], r[sems + 2], plus))
            go(remote(view(before, 0), p2.at[alpha], s[sems + 3], r[sems + 3], minus))

        def second():
            mine = view(after, 0)
            remote(mine, a1, s[sems], r[sems], plus).wait_recv()
            mine[...] = (mine[...].astype(F32) + a1[...].astype(F32)).astype(BF16)
            go(remote(mine, m2.at[alpha], s[sems + 4], r[sems + 4], plus))
            mine = view(before, 1)
            remote(mine, b1, s[sems + 1], r[sems + 1], minus).wait_recv()
            mine[...] = (mine[...].astype(F32) + b1[...].astype(F32)).astype(BF16)
            go(remote(mine, p2.at[beta], s[sems + 5], r[sems + 5], minus))

        def last():
            remote(view(after, 1), m2.at[beta], s[sems + 2], r[sems + 2], plus).wait_recv()
            remote(view(before, 0), p2.at[alpha], s[sems + 3], r[sems + 3], minus).wait_recv()
            remote(view(after, 0), m2.at[alpha], s[sems + 4], r[sems + 4], plus).wait_recv()
            remote(view(before, 1), p2.at[beta], s[sems + 5], r[sems + 5], minus).wait_recv()

        return first, second, last

    def halves(offset):
        return [pl.ds(offset, QUARTER), pl.ds(offset + QUARTER, QUARTER)]

    z_cols, x_cols, own_cols = halves(0), halves(HALF), halves(0)
    wide_at = [(slice(None), slice(None), cols) for cols in own_cols]
    flat_at = [(slice(None), cols) for cols in own_cols]
    z_big = ring_sum(
        lambda t, k: grads.at[:, t, :, z_cols[k]], z, zp_dev, zm_dev, (z_a1, z_b1, z_m2, z_p2, *wide_at), 0
    )
    x_big = ring_sum(
        lambda t, k: grads.at[t, :, :, x_cols[k]], x, xp_dev, xm_dev, (x_a1, x_b1, x_m2, x_p2, *wide_at), 6
    )
    z_small = ring_sum(
        lambda t, k: z_r.at[t, :, own_cols[k]], x, xp_dev, xm_dev, (z_sa1, z_sb1, z_sm2, z_sp2, *flat_at), 12
    )
    x_small = ring_sum(
        lambda t, k: x_r.at[t, :, own_cols[k]], z, zp_dev, zm_dev, (x_sa1, x_sb1, x_sm2, x_sp2, *flat_at), 18
    )
    z_big[0]()
    x_big[0]()
    z_big[1]()
    x_big[1]()
    z_big[2]()
    z_r[...] = (grads[:, z, :, 0:HALF].astype(F32) + z_m2[...].astype(F32) + z_p2[...].astype(F32)).astype(BF16)
    z_small[0]()
    x_big[2]()
    x_r[...] = (grads[x, :, :, HALF:COLS].astype(F32) + x_m2[...].astype(F32) + x_p2[...].astype(F32)).astype(BF16)
    x_small[0]()
    z_small[1]()
    x_small[1]()
    z_small[2]()
    gq_ref[0, :, 0:HALF] = z_r[x].astype(F32) + z_sm2[...].astype(F32) + z_sp2[...].astype(F32)
    x_small[2]()
    total = x_r[z].astype(F32) + x_sm2[...].astype(F32) + x_sp2[...].astype(F32)
    gq_ref[0, :, HALF:QKV] = total[:, : QKV - HALF]
    go_ref[0] = total[:, QKV - HALF :]

    for copy in sent:
        copy.wait_send()

    @pl.when((y > 0) & (y < 3))
    def _():
        h_hop.wait_send()

    @pl.when(y > 0)
    def _():
        c_hop.wait_send()


def on_device(inputs, cotangent, w_qkv, w_out):
    any_space = pl.BlockSpec(memory_space=pl.ANY)
    vmem = pl.BlockSpec(memory_space=pltpu.VMEM)
    dma = pltpu.SemaphoreType.DMA

    def flow():
        return [
            pltpu.VMEM((4, 64, QUARTER), BF16),
            pltpu.VMEM((4, 64, QUARTER), BF16),
            pltpu.VMEM((4, 64, HALF), BF16),
            pltpu.VMEM((4, 64, HALF), BF16),
            pltpu.VMEM((4, 64, HALF), BF16),
            pltpu.VMEM((64, QUARTER), BF16),
            pltpu.VMEM((64, QUARTER), BF16),
            pltpu.VMEM((64, HALF), BF16),
            pltpu.VMEM((64, HALF), BF16),
        ]

    return pl.pallas_call(
        kernel,
        out_shape=(jax.ShapeDtypeStruct((1, 64, QKV), F32), jax.ShapeDtypeStruct((1, 64, D), F32)),
        in_specs=[any_space] * 4,
        out_specs=(vmem, vmem),
        scratch_shapes=[
            pltpu.VMEM((2, D, QKV), BF16),
            pltpu.VMEM((2, D, D), BF16),
            pltpu.VMEM((2, SEQ, D), BF16),
            pltpu.VMEM((2, SEQ, D), BF16),
            pltpu.VMEM((3, SEQ, D), BF16),
            pltpu.VMEM((2, 2 * SEQ, D), BF16),
            pltpu.VMEM((2, SEQ, QKV), BF16),
            pltpu.VMEM((2, 4, 256, 256), BF16),
            pltpu.VMEM((2, 2 * SEQ, D), BF16),
            pltpu.VMEM((3, 2 * SEQ, D), BF16),
            pltpu.VMEM((2, 2 * SEQ, QKV), BF16),
            pltpu.VMEM((4, 4, 64, COLS), BF16),
            *flow(),
            *flow(),
            dma((6,)),
            dma((4,)),
            dma((4,)),
            dma((4, 4)),
            dma((4, 4)),
            dma((4, 4)),
            dma((4, 4)),
            dma((2,)),
            dma((2,)),
            dma((4,)),
            dma((4,)),
            dma((8,)),
            dma((8,)),
            dma((24,)),
            dma((24,)),
        ],
        compiler_params=pltpu.CompilerParams(
            collective_id=0, has_side_effects=True, vmem_limit_bytes=56 * 2**20
        ),
    )(inputs, cotangent, w_qkv, w_out)


def solution(mesh):
    placed = (
        P("dp", None, None, None, None),
        P("dp", None, None, None, None),
        P("section", None, None),
        P("section", None, None),
    )
    return jax.shard_map(
        on_device,
        mesh=mesh,
        in_specs=placed,
        out_specs=(P("section", "dp", None), P("section", "dp", None)),
        check_vma=False,
    )
```

```python
import functools

import jax
import jax.numpy as jnp
from jax import lax
from jax.experimental import pallas as pl
from jax.experimental.pallas import tpu as pltpu
from jax.sharding import PartitionSpec as P

MESH = pl.DeviceIdType.MESH
F32 = jnp.float32
BF16 = jnp.bfloat16
EPSILON = 1e-05

D = 1024
SEQ = 128
QKV = 1536
COLS = 2560
HALF = 768
QUARTER = 384
WIDE = 512
CHUNK = 64


def mm(a, b):
    return jnp.dot(a, b, preferred_element_type=F32)


def mm_nt(a, b):
    return lax.dot_general(a, b, (((1,), (1,)), ((), ())), preferred_element_type=F32)


def mm_tn(a, b):
    return lax.dot_general(a, b, (((0,), (0,)), ((), ())), preferred_element_type=F32)


def block_diagonal(pair, group):
    low = lax.broadcasted_iota(jnp.int32, pair.shape, 1) < 64
    wide = pair.astype(F32)
    rolled = pltpu.roll(wide, 64, 1)
    first, second = (wide, rolled) if group % 2 == 0 else (rolled, wide)
    zero = jnp.zeros_like(wide)
    return jnp.concatenate([jnp.where(low, first, zero), jnp.where(low, zero, second)], axis=0).astype(BF16)


def half_sums(x):
    return (jnp.sum(x[:, :128], axis=1, keepdims=True), jnp.sum(x[:, 128:], axis=1, keepdims=True))


def stack_pairs(x, group):
    at = group * 256
    return jnp.concatenate([x[:, at : at + 128], x[:, at + 128 : at + 256]], axis=0)


def kv_pairs(joined, group):
    at = (group // 2) * 128
    return joined[:, D + at : D + at + 128], joined[:, D + 256 + at : D + 256 + at + 128]


def attention_forward(joined, probs_ref, att_ref, layer):
    rows = lax.broadcasted_iota(jnp.int32, (256, 256), 0) & 127
    cols = lax.broadcasted_iota(jnp.int32, (256, 256), 1) & 127
    causal = rows >= cols
    for group in range(4):
        queries = stack_pairs(joined, group)
        keys, values = kv_pairs(joined, group)
        scores = mm_nt(queries, block_diagonal(keys, group)) * 0.125
        exponent = jnp.where(causal, jnp.exp(scores), 0.0)
        left, right = half_sums(exponent)
        probs = jnp.concatenate([exponent[:, :128] * (1.0 / left), exponent[:, 128:] * (1.0 / right)], axis=1).astype(BF16)
        probs_ref[layer, group] = probs
        mixed = mm(probs, block_diagonal(values, group)).astype(BF16)
        at = group * 256
        att_ref[:, at : at + 128] = mixed[:128]
        att_ref[:, at + 128 : at + 256] = mixed[128:]


def attention_backward(joined, d_attention, probs_ref, dj_ref, layer):
    d_keys, d_values = [], []
    for group in range(4):
        queries = stack_pairs(joined, group)
        d_heads = stack_pairs(d_attention, group)
        keys, values = kv_pairs(joined, group)
        probs = probs_ref[layer, group]
        d_probs = mm_nt(d_heads, block_diagonal(values, group))
        wide = probs.astype(F32)
        left, right = half_sums(wide * d_probs)
        centred = jnp.concatenate([d_probs[:, :128] - left, d_probs[:, 128:] - right], axis=1)
        d_scores = (wide * centred * 0.125).astype(BF16)
        d_queries = mm(d_scores, block_diagonal(keys, group)).astype(BF16)
        at = group * 256
        dj_ref[layer, 0:SEQ, at : at + 128] = d_queries[:128]
        dj_ref[layer, 0:SEQ, at + 128 : at + 256] = d_queries[128:]
        d_keys.append(mm_tn(d_scores, queries))
        d_values.append(mm_tn(probs, d_heads))
    low = lax.broadcasted_iota(jnp.int32, (128, 128), 1) < 64

    def merged(even, odd):
        first = even[:128] + pltpu.roll(even[128:], 64, 1)
        second = pltpu.roll(odd[:128], 64, 1) + odd[128:]
        return jnp.where(low, first, second).astype(BF16)

    for pair in range(2):
        at = D + pair * 128
        dj_ref[layer, 0:SEQ, at : at + 128] = merged(d_keys[2 * pair], d_keys[2 * pair + 1])
        dj_ref[layer, 0:SEQ, at + 256 : at + 384] = merged(d_values[2 * pair], d_values[2 * pair + 1])


def inverse_norm(wide):
    return lax.rsqrt(jnp.mean(wide * wide, axis=-1, keepdims=True) + EPSILON)


def kernel(
    inputs_ref, cotangent_ref, wq_ref, wo_ref,
    out_ref,
    wq, wo, wqt, entry, passed, hidden, normed, joined, probs, att, upstream, dj, c_pack, c_all, grads, grads_out,
    z_a1, z_b1, z_m2, z_p2, z_r, z_sa1, z_sb1, z_sm2, z_sp2,
    x_a1, x_b1, x_m2, x_p2, x_r, x_sa1, x_sb1, x_sm2, x_sp2,
    o_a1, o_b1, o_m2, o_p2,
    load_sem, flip_send, flip_recv, spread_send, spread_recv, core_send, core_recv,
    entry_send, entry_recv, hop_send, hop_recv, share_send, share_recv,
    att_send, att_recv, att_core_send, att_core_recv, c_send, c_recv, sum_send, sum_recv,
):
    section, dp = lax.axis_index("section"), lax.axis_index("dp")
    y, x_hi = lax.div(section, 2), lax.rem(section, 2)
    z, x_lo, core = lax.div(dp, 4), lax.rem(lax.div(dp, 2), 2), lax.rem(dp, 2)
    x = 2 * x_hi + x_lo
    slot = 2 * z + core

    def place(y, x, z, core):
        return (2 * y + lax.div(x, 2), 4 * z + 2 * lax.rem(x, 2) + core)

    core_dev = place(y, x, z, 1 - core)
    xp_dev, xm_dev = place(y, lax.rem(x + 1, 4), z, core), place(y, lax.rem(x + 3, 4), z, core)
    zp_dev, zm_dev = place(y, x, lax.rem(z + 1, 4), core), place(y, x, lax.rem(z + 3, 4), core)
    yp_dev, ym_dev = place(lax.rem(y + 1, 4), x, z, core), place(lax.rem(y + 3, 4), x, z, core)
    column = [[place(y, x, lax.rem(z + k, 4), c) for c in (core, 1 - core)] for k in range(4)]
    flip_dev = place(y, 3 - x, z, core)
    side_dev = place(y, 2 * x_hi + 1 - x_lo, z, core)
    up_across_dev, down_across_dev = place(lax.rem(y + 1, 4), 3 - x, z, core), place(lax.rem(y + 3, 4), 3 - x, z, core)

    def remote(src, dst, send_sem, recv_sem, device):
        return pltpu.make_async_remote_copy(
            src_ref=src, dst_ref=dst, send_sem=send_sem, recv_sem=recv_sem, device_id=device, device_id_type=MESH
        )

    sent = []

    def go(copy):
        copy.start()
        sent.append(copy)

    loads = [
        pltpu.make_async_copy(wq_ref.at[0], wq.at[x_hi], load_sem.at[0]),
        pltpu.make_async_copy(wo_ref.at[0], wo.at[x_hi], load_sem.at[1]),
    ]
    load_in = pltpu.make_async_copy(inputs_ref.at[0, 0, 0], hidden.at[0], load_sem.at[2])
    load_cot = pltpu.make_async_copy(cotangent_ref.at[0, 0, 0], upstream.at[2], load_sem.at[3])
    load_entry = [pltpu.make_async_copy(inputs_ref.at[0, s, 0], entry.at[s], load_sem.at[4 + s]) for s in range(2)]
    for copy in loads:
        copy.start()

    near, far = x_hi == 0, x_hi == 1

    @pl.when((y == 0) & near)
    def _():
        load_entry[0].start()
        load_entry[1].start()
        load_in.start()

    @pl.when((y == 3) & near)
    def _():
        load_cot.start()

    barrier = pltpu.get_barrier_semaphore()
    ring = [column[k][c] for k in range(4) for c in range(2) if (k, c) != (0, 0)]
    for device in (*ring, xp_dev, xm_dev, yp_dev, ym_dev, up_across_dev, down_across_dev):
        pl.semaphore_signal(barrier, inc=1, device_id=device, device_id_type=MESH)
    pl.semaphore_wait(barrier, 13)

    in_hop = remote(inputs_ref.at[0, 1, 0], hidden.at[0], hop_send.at[2], hop_recv.at[2], side_dev)
    cot_hop = remote(cotangent_ref.at[0, 1, 0], upstream.at[2], hop_send.at[3], hop_recv.at[3], side_dev)

    @pl.when((y == 0) & far)
    def _():
        in_hop.start()

    @pl.when((y == 3) & far)
    def _():
        cot_hop.start()

    h_hop = remote(hidden.at[2], hidden.at[0], hop_send.at[0], hop_recv.at[0], yp_dev)
    c_hop = remote(upstream.at[0], upstream.at[2], hop_send.at[1], hop_recv.at[1], ym_dev)

    def run_forward(h, weights, layer):
        wide = h.astype(F32)
        inverse = inverse_norm(wide)
        normed[layer, 0:SEQ] = (wide * inverse).astype(BF16)
        joined[layer] = (mm(h, wq[weights]) * inverse).astype(BF16)
        attention_forward(joined[layer], probs, att.at[layer, slot], layer)
        return (wide + mm_nt(att[layer, slot], wo[weights])).astype(BF16)

    across = [remote(passed.at[s], entry.at[s], entry_send.at[s], entry_recv.at[s], flip_dev) for s in range(2)]
    onward = [
        remote(passed.at[0], hidden.at[0], entry_send.at[0], hop_recv.at[0], up_across_dev),
        remote(passed.at[1], hidden.at[0], entry_send.at[1], hop_recv.at[0], yp_dev),
    ]

    @pl.when(y == 0)
    def _():
        for copy in loads:
            copy.wait()

        def first_pass(s, carry):
            for k in range(2):
                @pl.when((s == k) & near)
                def _():
                    load_entry[k].wait()

                @pl.when((s == k) & far)
                def _():
                    across[k].wait_recv()

            passed[s] = run_forward(entry[s], x_hi, 0)
            for k in range(2):
                @pl.when((s == k) & near)
                def _():
                    across[k].start()

                @pl.when((s == k) & far)
                def _():
                    onward[k].start()

            return carry

        lax.fori_loop(0, 2, first_pass, 0)

        @pl.when(near)
        def _():
            for copy in across:
                copy.wait_send()

        @pl.when(far)
        def _():
            for copy in onward:
                copy.wait_send()

    other = 1 - x_hi
    piece = lax.rem(z + 2 * x_lo, 4)
    pieces = [lax.rem(piece + k, 4) for k in range(4)]

    def chunk_rows(which, half, part):
        return pl.ds(pl.multiple_of(which * 256 + half * 128 + (part % 2) * CHUNK, CHUNK), CHUNK)

    def chunk(buf_q, buf_o, slot, which, half, part):
        rows = chunk_rows(which, half, part)
        return (buf_q if part < 2 else buf_o).at[slot, rows]

    for part in range(4):
        src = chunk(wq_ref, wo_ref, 0, pieces[2], core, part)
        go(remote(src, chunk(wq, wo, x_hi, pieces[2], core, part), flip_send.at[part], flip_recv.at[part], flip_dev))

    def await_flip(part):
        block = chunk(wq, wo, other, pieces[0], core, part)
        remote(block, block, flip_send.at[part], flip_recv.at[part], flip_dev).wait_recv()

    def spread(part):
        block = chunk(wq, wo, other, pieces[0], core, part)
        for slot, device in ((1, zm_dev), (2, side_dev), (3, zp_dev)):
            go(remote(block, block, spread_send.at[part, slot], spread_recv.at[part, slot], device))

    def to_core(part, k):
        block = chunk(wq, wo, other, pieces[k], core, part)
        go(remote(block, block, core_send.at[part, k], core_recv.at[part, k], core_dev))

    def gather_rest(part):
        for k in (1, 2, 3):
            block = chunk(wq, wo, other, pieces[k], core, part)
            remote(block, block, spread_send.at[part, k], spread_recv.at[part, k], side_dev).wait_recv()
            to_core(part, k)

    for part in range(4):
        await_flip(part)
        spread(part)
        to_core(part, 0)
        if part > 0:
            gather_rest(part - 1)
    gather_rest(3)
    for part in range(4):
        for k in range(4):
            block = chunk(wq, wo, other, pieces[k], 1 - core, part)
            remote(block, block, core_send.at[part, k], core_recv.at[part, k], core_dev).wait_recv()

    def transpose_weights():
        def one(k, carry):
            layer, cols = lax.div(k, 6), pl.ds(pl.multiple_of(lax.rem(k, 6) * 256, 256), 256)
            wqt[layer, cols] = wq[layer, :, cols].T
            return carry

        lax.fori_loop(0, 12, one, 0)

    @pl.when(y > 0)
    def _():
        for copy in loads:
            copy.wait()

    @pl.when(y >= 2)
    def _():
        transpose_weights()

    @pl.when((y == 0) & near)
    def _():
        load_in.wait()

    @pl.when((y == 0) & far)
    def _():
        in_hop.wait()

    @pl.when(y > 0)
    def _():
        h_hop.wait_recv()

    def forward(layer, carry):
        hidden[layer + 1] = run_forward(hidden[layer], layer, layer)
        return carry

    lax.fori_loop(0, 2, forward, 0)

    @pl.when((y > 0) & (y < 3))
    def _():
        h_hop.start()

    def share(buf, layer, number):
        return remote(
            buf.at[layer, 0:SEQ], buf.at[layer, SEQ : 2 * SEQ], share_send.at[number], share_recv.at[number], core_dev
        )

    shares = [share(normed, 0, 0), share(normed, 1, 1), share(dj, 0, 2), share(dj, 1, 3)]
    sent.extend(shares)

    def att_copy(layer, k, to_core=False):
        if to_core:
            block = att.at[layer, 2 * lax.rem(z + 4 - k, 4) + core]
            return remote(block, block, att_core_send.at[layer, k], att_core_recv.at[layer, k], core_dev)
        block = att.at[layer, slot]
        return remote(block, block, att_send.at[layer, k], att_recv.at[layer, k], column[k][0])

    spread_att = [att_copy(layer, k) for layer in (1, 0) for k in (1, 3, 2)]
    core_att = [att_copy(layer, k, True) for layer in (1, 0) for k in (0, 1, 3, 2)]
    sent.extend(spread_att + core_att)

    def send_attention():
        shares[0].start()
        shares[1].start()
        for copy in spread_att:
            copy.start()

    def pass_attention():
        for layer in (1, 0):
            for k in (0, 1, 3, 2):
                if k:
                    block = att.at[layer, 2 * lax.rem(z + 4 - k, 4) + core]
                    remote(block, block, att_send.at[layer, k], att_recv.at[layer, k], core_dev).wait_recv()
                att_copy(layer, k, True).start()

    def await_attention(layer):
        for k in range(4):
            block = att.at[layer, 2 * lax.rem(z + 4 - k, 4) + 1 - core]
            remote(block, block, att_core_send.at[layer, k], att_core_recv.at[layer, k], core_dev).wait_recv()

    def c_copy(layer, k, c):
        source = c_pack.at[layer, core if c == 0 else 1 - core, lax.rem(z + k, 4)]
        return remote(source, c_all.at[layer, slot], c_send.at[layer, 2 * k + c], c_recv.at[layer, 2 * k + c], column[k][c])

    def send_c(layer):
        low = lax.broadcasted_iota(jnp.int32, (SEQ, 128), 1) < 64
        for to in range(4):
            a = upstream[layer + 1, :, 256 * to : 256 * to + 128].astype(F32)
            b = upstream[layer + 1, :, 256 * to + 128 : 256 * to + 256].astype(F32)
            c_pack[layer, 0, to] = jnp.where(low, a, pltpu.roll(b, 64, 1)).astype(BF16)
            c_pack[layer, 1, to] = jnp.where(low, pltpu.roll(a, 64, 1), b).astype(BF16)
        c_all[layer, slot] = c_pack[layer, core, z]
        for k in (1, 3, 2, 0):
            for c in range(2):
                if (k, c) != (0, 0):
                    c_copy(layer, k, c).start()

    def await_c(layer):
        for k in range(4):
            for c in range(2):
                if (k, c) != (0, 0):
                    block = c_all.at[layer, 2 * lax.rem(z + 4 - k, 4) + (core if c == 0 else 1 - core)]
                    remote(
                        block, block, c_send.at[layer, 2 * k + c], c_recv.at[layer, 2 * k + c], core_dev
                    ).wait_recv()

    sent.extend(c_copy(layer, k, c) for layer in range(2) for k in range(4) for c in range(2) if (k, c) != (0, 0))

    @pl.when(y < 3)
    def _():
        send_attention()

    @pl.when(y < 2)
    def _():
        transpose_weights()
        pass_attention()

    @pl.when((y == 3) & near)
    def _():
        load_cot.wait()

    @pl.when((y == 3) & far)
    def _():
        cot_hop.wait()

    @pl.when(y < 3)
    def _():
        c_hop.wait_recv()

    def run_backward(layer):
        c = upstream[layer + 1]
        d_attention = mm(c, wo[layer]).astype(BF16)
        attention_backward(joined[layer], d_attention, probs, dj, layer)

        @pl.when((layer > 0) | (y > 0))
        def _():
            d_normed = mm(dj[layer, 0:SEQ], wqt[layer])
            wide = hidden[layer].astype(F32)
            inverse = inverse_norm(wide)
            scaled = wide * inverse
            along = jnp.mean(d_normed * scaled, axis=-1, keepdims=True)
            upstream[layer] = (
                upstream[layer + 1].astype(F32) + inverse * (d_normed - scaled * along)
            ).astype(BF16)

    def backward(step, carry):
        layer = 1 - step

        @pl.when(y == 0)
        def _():
            send_c(layer)

        run_backward(layer)
        share(dj, layer, 2 + layer).start()
        return carry

    lax.fori_loop(0, 2, backward, 0)

    @pl.when(y > 0)
    def _():
        c_hop.start()

    @pl.when(y == 3)
    def _():
        send_attention()

    low = lax.broadcasted_iota(jnp.int32, (2 * SEQ, 128), 1) < 64

    def own_columns(block):
        def tile(k):
            return block[:, 128 * k : 128 * k + 128].astype(F32)

        tiles = []
        for lo in range(2):
            for pair in range(2):
                a, b = tile(4 * pair + lo), tile(4 * pair + 2 + lo)
                first = jnp.where(core == 0, a, pltpu.roll(a, 64, 1))
                second = jnp.where(core == 0, pltpu.roll(b, 64, 1), b)
                tiles.append(jnp.where(low, first, second).astype(BF16))
        return jnp.concatenate(tiles, axis=1)

    def gradient(layer):
        left = own_columns(normed[layer])
        for lo in range(2):
            part = mm_tn(left[:, 256 * lo : 256 * lo + 256], dj[layer]).astype(BF16)
            grads[2 * layer + lo] = part.reshape(4, 64, QKV)

    def gradient_out(layer):
        await_c(layer)
        await_attention(layer)
        part = mm_tn(c_all[layer].reshape(8 * SEQ, 128), att[layer].reshape(8 * SEQ, D)).astype(BF16)
        grads_out[2 * layer : 2 * layer + 2] = part.reshape(2, 64, D)

    def ring_sum(view, position, plus, minus, bufs, sems, layers=None):
        a1, b1, m2, p2, alpha, beta = bufs
        opposite, after, before = (lax.rem(position + k, 4) for k in (2, 1, 3))
        s, r = sum_send.at, sum_recv.at
        copies = [
            remote(view(opposite, 0), a1, s[sems], r[sems], plus),
            remote(view(opposite, 1), b1, s[sems + 1], r[sems + 1], minus),
            remote(view(after, 1), m2.at[beta], s[sems + 2], r[sems + 2], plus),
            remote(view(before, 0), p2.at[alpha], s[sems + 3], r[sems + 3], minus),
            remote(view(after, 0), m2.at[alpha], s[sems + 4], r[sems + 4], plus),
            remote(view(before, 1), p2.at[beta], s[sems + 5], r[sems + 5], minus),
        ]
        sent.extend(copies)

        def only(stage, target):
            if stage is None:
                return lambda body: body()
            return pl.when(layers(target) == stage)

        def first(stage=None):
            @only(stage, opposite)
            def _():
                copies[0].start()
                copies[1].start()

            @only(stage, after)
            def _():
                copies[2].start()

            @only(stage, before)
            def _():
                copies[3].start()

        def second(stage=None):
            @only(stage, after)
            def _():
                mine = view(after, 0)
                copies[0].wait_recv()
                mine[...] = (mine[...].astype(F32) + a1[...].astype(F32)).astype(BF16)
                copies[4].start()

            @only(stage, before)
            def _():
                mine = view(before, 1)
                copies[1].wait_recv()
                mine[...] = (mine[...].astype(F32) + b1[...].astype(F32)).astype(BF16)
                copies[5].start()

        def last():
            for copy in copies[2:]:
                copy.wait_recv()

        return first, second, last

    def halves(offset):
        return [pl.ds(offset, QUARTER), pl.ds(offset + QUARTER, QUARTER)]

    z_cols, x_cols, own_cols = halves(0), halves(HALF), halves(0)
    wide_at = [(slice(None), slice(None), cols) for cols in own_cols]
    flat_at = [(slice(None), cols) for cols in own_cols]

    def z_ring(layer):
        pair = pl.ds(2 * layer, 2)
        bufs = (z_a1.at[pair], z_b1.at[pair], z_m2.at[pair], z_p2.at[pair], *wide_at)
        return ring_sum(lambda t, k: grads.at[pair, t, :, z_cols[k]], z, zp_dev, zm_dev, bufs, 24 if layer else 0)

    z_big = [z_ring(0), z_ring(1)]
    def layer_of(target):
        return lax.div(target, 2)

    x_big = ring_sum(
        lambda t, k: grads.at[t, :, :, x_cols[k]], x, xp_dev, xm_dev, (x_a1, x_b1, x_m2, x_p2, *wide_at), 6, layer_of
    )
    z_small = ring_sum(
        lambda t, k: z_r.at[t, :, own_cols[k]], x, xp_dev, xm_dev, (z_sa1, z_sb1, z_sm2, z_sp2, *flat_at), 12, layer_of
    )
    x_small = ring_sum(
        lambda t, k: x_r.at[t, :, own_cols[k]], z, zp_dev, zm_dev, (x_sa1, x_sb1, x_sm2, x_sp2, *flat_at), 18
    )
    out_at = [(slice(None), pl.ds(0, WIDE)), (slice(None), pl.ds(WIDE, WIDE))]
    o_ring = ring_sum(
        lambda t, k: grads_out.at[t, :, pl.ds(k * WIDE, WIDE)], x, xp_dev, xm_dev, (o_a1, o_b1, o_m2, o_p2, *out_at), 30
    )

    def sum_z(layer):
        pair = slice(2 * layer, 2 * layer + 2)
        z_r[pair] = (grads[pair, z, :, 0:HALF].astype(F32) + z_m2[pair].astype(F32) + z_p2[pair].astype(F32)).astype(BF16)

    shares[1].wait_recv()
    shares[3].wait_recv()
    gradient(1)
    z_big[1][0]()
    x_big[0](1)
    shares[0].wait_recv()
    shares[2].wait_recv()
    gradient(0)
    z_big[0][0]()
    x_big[0](0)

    @pl.when(y > 0)
    def _():
        send_c(1)
        send_c(0)

    @pl.when(y >= 2)
    def _():
        pass_attention()

    gradient_out(1)
    gradient_out(0)
    o_ring[0]()
    z_big[1][1]()
    x_big[1](1)
    z_big[0][1]()
    x_big[1](0)
    z_big[1][2]()
    sum_z(1)
    z_small[0](1)
    o_ring[1]()
    z_big[0][2]()
    sum_z(0)
    z_small[0](0)
    x_big[2]()
    x_r[...] = (grads[x, :, :, HALF:QKV].astype(F32) + x_m2[...].astype(F32) + x_p2[...].astype(F32)).astype(BF16)
    x_small[0]()
    z_small[1](1)
    z_small[1](0)
    x_small[1]()
    o_ring[2]()
    out_ref[:, QKV:COLS] = grads_out[x].astype(F32) + o_m2[...].astype(F32) + o_p2[...].astype(F32)
    z_small[2]()
    out_ref[:, 0:HALF] = z_r[x].astype(F32) + z_sm2[...].astype(F32) + z_sp2[...].astype(F32)
    x_small[2]()
    out_ref[:, HALF:QKV] = x_r[z].astype(F32) + x_sm2[...].astype(F32) + x_sp2[...].astype(F32)

    for copy in sent:
        copy.wait_send()

    @pl.when((y > 0) & (y < 3))
    def _():
        h_hop.wait_send()

    @pl.when(y > 0)
    def _():
        c_hop.wait_send()


def on_device(inputs, cotangent, w_qkv, w_out):
    any_space = pl.BlockSpec(memory_space=pl.ANY)
    vmem = pl.BlockSpec(memory_space=pltpu.VMEM)
    dma = pltpu.SemaphoreType.DMA

    def flow():
        return [
            pltpu.VMEM((4, 64, QUARTER), BF16),
            pltpu.VMEM((4, 64, QUARTER), BF16),
            pltpu.VMEM((4, 64, HALF), BF16),
            pltpu.VMEM((4, 64, HALF), BF16),
            pltpu.VMEM((4, 64, HALF), BF16),
            pltpu.VMEM((64, QUARTER), BF16),
            pltpu.VMEM((64, QUARTER), BF16),
            pltpu.VMEM((64, HALF), BF16),
            pltpu.VMEM((64, HALF), BF16),
        ]

    total = pl.pallas_call(
        kernel,
        out_shape=jax.ShapeDtypeStruct((64, COLS), F32),
        in_specs=[any_space] * 4,
        out_specs=vmem,
        scratch_shapes=[
            pltpu.VMEM((2, D, QKV), BF16),
            pltpu.VMEM((2, D, D), BF16),
            pltpu.VMEM((2, QKV, D), BF16),
            pltpu.VMEM((2, SEQ, D), BF16),
            pltpu.VMEM((2, SEQ, D), BF16),
            pltpu.VMEM((3, SEQ, D), BF16),
            pltpu.VMEM((2, 2 * SEQ, D), BF16),
            pltpu.VMEM((2, SEQ, QKV), BF16),
            pltpu.VMEM((2, 4, 256, 256), BF16),
            pltpu.VMEM((2, 8, SEQ, D), BF16),
            pltpu.VMEM((3, SEQ, D), BF16),
            pltpu.VMEM((2, 2 * SEQ, QKV), BF16),
            pltpu.VMEM((2, 2, 4, SEQ, 128), BF16),
            pltpu.VMEM((2, 8, SEQ, 128), BF16),
            pltpu.VMEM((4, 4, 64, QKV), BF16),
            pltpu.VMEM((4, 64, D), BF16),
            *flow(),
            *flow(),
            pltpu.VMEM((64, WIDE), BF16),
            pltpu.VMEM((64, WIDE), BF16),
            pltpu.VMEM((64, D), BF16),
            pltpu.VMEM((64, D), BF16),
            dma((6,)),
            dma((4,)),
            dma((4,)),
            dma((4, 4)),
            dma((4, 4)),
            dma((4, 4)),
            dma((4, 4)),
            dma((2,)),
            dma((2,)),
            dma((4,)),
            dma((4,)),
            dma((4,)),
            dma((4,)),
            dma((2, 4)),
            dma((2, 4)),
            dma((2, 4)),
            dma((2, 4)),
            dma((2, 8)),
            dma((2, 8)),
            dma((36,)),
            dma((36,)),
        ],
        compiler_params=pltpu.CompilerParams(
            collective_id=0, has_side_effects=True, vmem_limit_bytes=56 * 2**20
        ),
    )(inputs, cotangent, w_qkv, w_out)
    return (total[None, :, :QKV], total[None, :, QKV:])


def solution(mesh):
    placed = (
        P("dp", None, None, None, None),
        P("dp", None, None, None, None),
        P("section", None, None),
        P("section", None, None),
    )
    return jax.shard_map(
        on_device,
        mesh=mesh,
        in_specs=placed,
        out_specs=(P("section", "dp", None), P("section", "dp", None)),
        check_vma=False,
    )
```

```python
import functools

import jax
import jax.numpy as jnp
from jax import lax
from jax.experimental import pallas as pl
from jax.experimental.pallas import tpu as pltpu
from jax.sharding import PartitionSpec as P

MESH = pl.DeviceIdType.MESH
F32 = jnp.float32
BF16 = jnp.bfloat16
EPSILON = 1e-05

D = 1024
SEQ = 128
QKV = 1536
COLS = 2560
HALF = 768
QUARTER = 384
WIDE = 512
PARTS = [("q", k, 32) for k in range(4)] + [("o", k, 64) for k in range(2)]


def mm(a, b):
    return jnp.dot(a, b, preferred_element_type=F32)


def mm_nt(a, b):
    return lax.dot_general(a, b, (((1,), (1,)), ((), ())), preferred_element_type=F32)


def mm_tn(a, b):
    return lax.dot_general(a, b, (((0,), (0,)), ((), ())), preferred_element_type=F32)


def block_diagonal(pair, group):
    low = lax.broadcasted_iota(jnp.int32, pair.shape, 1) < 64
    wide = pair.astype(F32)
    rolled = pltpu.roll(wide, 64, 1)
    first, second = (wide, rolled) if group % 2 == 0 else (rolled, wide)
    zero = jnp.zeros_like(wide)
    return jnp.concatenate([jnp.where(low, first, zero), jnp.where(low, zero, second)], axis=0).astype(BF16)


def half_sums(x):
    return (jnp.sum(x[:, :128], axis=1, keepdims=True), jnp.sum(x[:, 128:], axis=1, keepdims=True))


def stack_pairs(x, group):
    at = group * 256
    return jnp.concatenate([x[:, at : at + 128], x[:, at + 128 : at + 256]], axis=0)


def kv_pairs(joined, group):
    at = (group // 2) * 128
    return joined[:, D + at : D + at + 128], joined[:, D + 256 + at : D + 256 + at + 128]


def attention_forward(joined, probs_ref, att_ref, layer):
    rows = lax.broadcasted_iota(jnp.int32, (256, 256), 0) & 127
    cols = lax.broadcasted_iota(jnp.int32, (256, 256), 1) & 127
    causal = rows >= cols
    for group in range(4):
        queries = stack_pairs(joined, group)
        keys, values = kv_pairs(joined, group)
        scores = mm_nt(queries, block_diagonal(keys, group)) * 0.125
        exponent = jnp.where(causal, jnp.exp(scores), 0.0)
        left, right = half_sums(exponent)
        probs = jnp.concatenate([exponent[:, :128] * (1.0 / left), exponent[:, 128:] * (1.0 / right)], axis=1).astype(BF16)
        probs_ref[layer, group] = probs
        mixed = mm(probs, block_diagonal(values, group)).astype(BF16)
        at = group * 256
        att_ref[:, at : at + 128] = mixed[:128]
        att_ref[:, at + 128 : at + 256] = mixed[128:]


def attention_backward(joined, d_attention, probs_ref, dj_ref, carried, layer, half):
    at = 64 * half
    rows = pl.ds(at, 64)
    early, late = slice(0, 64), slice(64, 128)
    d_keys, d_values = [], []
    for group in range(4):
        queries = stack_pairs(joined[at : at + 64], group)
        d_heads = stack_pairs(d_attention, group)
        keys, values = kv_pairs(joined, group)
        probs = jnp.concatenate(
            [probs_ref[layer, group, at : at + 64], probs_ref[layer, group, 128 + at : 192 + at]], axis=0
        )
        d_probs = mm_nt(d_heads, block_diagonal(values, group))
        wide = probs.astype(F32)
        left, right = half_sums(wide * d_probs)
        centred = jnp.concatenate([d_probs[:, :128] - left, d_probs[:, 128:] - right], axis=1)
        d_scores = (wide * centred * 0.125).astype(BF16)
        d_queries = mm(d_scores, block_diagonal(keys, group)).astype(BF16)
        lane = group * 256
        dj_ref[layer, rows, lane : lane + 128] = d_queries[:64]
        dj_ref[layer, rows, lane + 128 : lane + 256] = d_queries[64:]
        d_keys.append(mm_tn(d_scores, queries))
        d_values.append(mm_tn(probs, d_heads))
    low = lax.broadcasted_iota(jnp.int32, (128, 128), 1) < 64

    def merged(even, odd):
        first = even[:128] + pltpu.roll(even[128:], 64, 1)
        second = pltpu.roll(odd[:128], 64, 1) + odd[128:]
        return jnp.where(low, first, second)

    for number, parts in ((0, d_keys), (1, d_values)):
        for pair in range(2):
            total = merged(parts[2 * pair], parts[2 * pair + 1])
            lane = D + 256 * number + 128 * pair
            if half:
                carried[layer, number, pair] = total[early]
                dj_ref[layer, rows, lane : lane + 128] = total[late].astype(BF16)
            else:
                dj_ref[layer, rows, lane : lane + 128] = (total[early] + carried[layer, number, pair]).astype(BF16)


def inverse_norm(wide):
    return lax.rsqrt(jnp.mean(wide * wide, axis=-1, keepdims=True) + EPSILON)


def kernel(
    inputs_ref, cotangent_ref, wq_ref, wo_ref,
    out_ref,
    wq, wo, wqt, entry, passed, hidden, normed, joined, probs, att, upstream, dj, carried, c_pack, c_all, grads, grads_out,
    z_a1, z_b1, z_m2, z_p2, z_r, z_sa1, z_sb1, z_sm2, z_sp2,
    x_a1, x_b1, x_m2, x_p2, x_r, x_sa1, x_sb1, x_sm2, x_sp2,
    o_a1, o_b1, o_m2, o_p2,
    load_sem, flip_send, flip_recv, spread_send, spread_recv, core_send, core_recv,
    entry_send, entry_recv, hop_send, hop_recv, share_send, share_recv,
    att_send, att_recv, att_core_send, att_core_recv, c_send, c_recv, sum_send, sum_recv,
):
    section, dp = lax.axis_index("section"), lax.axis_index("dp")
    y, x_hi = lax.div(section, 2), lax.rem(section, 2)
    z, x_lo, core = lax.div(dp, 4), lax.rem(lax.div(dp, 2), 2), lax.rem(dp, 2)
    x = 2 * x_hi + x_lo
    slot = 2 * z + core

    def place(y, x, z, core):
        return (2 * y + lax.div(x, 2), 4 * z + 2 * lax.rem(x, 2) + core)

    core_dev = place(y, x, z, 1 - core)
    xp_dev, xm_dev = place(y, lax.rem(x + 1, 4), z, core), place(y, lax.rem(x + 3, 4), z, core)
    zp_dev, zm_dev = place(y, x, lax.rem(z + 1, 4), core), place(y, x, lax.rem(z + 3, 4), core)
    yp_dev, ym_dev = place(lax.rem(y + 1, 4), x, z, core), place(lax.rem(y + 3, 4), x, z, core)
    column = [[place(y, x, lax.rem(z + k, 4), c) for c in (core, 1 - core)] for k in range(4)]
    flip_dev = place(y, 3 - x, z, core)
    side_dev = place(y, 2 * x_hi + 1 - x_lo, z, core)
    up_across_dev, down_across_dev = place(lax.rem(y + 1, 4), 3 - x, z, core), place(lax.rem(y + 3, 4), 3 - x, z, core)

    def remote(src, dst, send_sem, recv_sem, device):
        return pltpu.make_async_remote_copy(
            src_ref=src, dst_ref=dst, send_sem=send_sem, recv_sem=recv_sem, device_id=device, device_id_type=MESH
        )

    sent = []

    def go(copy):
        copy.start()
        sent.append(copy)

    loads = [
        pltpu.make_async_copy(wq_ref.at[0], wq.at[x_hi], load_sem.at[0]),
        pltpu.make_async_copy(wo_ref.at[0], wo.at[x_hi], load_sem.at[1]),
    ]
    load_in = pltpu.make_async_copy(inputs_ref.at[0, 0, 0], hidden.at[0], load_sem.at[2])
    load_cot = pltpu.make_async_copy(cotangent_ref.at[0, 0, 0], upstream.at[2], load_sem.at[3])
    load_entry = [pltpu.make_async_copy(inputs_ref.at[0, s, 0], entry.at[s], load_sem.at[4 + s]) for s in range(2)]
    for copy in loads:
        copy.start()

    near, far = x_hi == 0, x_hi == 1

    @pl.when((y == 0) & near)
    def _():
        load_entry[0].start()
        load_entry[1].start()
        load_in.start()

    @pl.when((y == 3) & near)
    def _():
        load_cot.start()

    barrier = pltpu.get_barrier_semaphore()
    ring = [column[k][c] for k in range(4) for c in range(2) if (k, c) != (0, 0)]
    for device in (*ring, xp_dev, xm_dev, yp_dev, ym_dev, up_across_dev, down_across_dev):
        pl.semaphore_signal(barrier, inc=1, device_id=device, device_id_type=MESH)
    pl.semaphore_wait(barrier, 13)

    in_hop = remote(inputs_ref.at[0, 1, 0], hidden.at[0], hop_send.at[2], hop_recv.at[2], side_dev)
    cot_hop = remote(cotangent_ref.at[0, 1, 0], upstream.at[2], hop_send.at[3], hop_recv.at[3], side_dev)

    @pl.when((y == 0) & far)
    def _():
        in_hop.start()

    @pl.when((y == 3) & far)
    def _():
        cot_hop.start()

    h_hop = remote(hidden.at[2], hidden.at[0], hop_send.at[0], hop_recv.at[0], yp_dev)
    c_hop = [
        remote(
            upstream.at[0, 64 * half : 64 * half + 64], upstream.at[2, 64 * half : 64 * half + 64],
            hop_send.at[(1, 4)[half]], hop_recv.at[(1, 4)[half]], ym_dev,
        )
        for half in range(2)
    ]

    def run_forward(h, weights, layer):
        wide = h.astype(F32)
        inverse = inverse_norm(wide)
        normed[layer, 0:SEQ] = (wide * inverse).astype(BF16)
        joined[layer] = (mm(h, wq[weights]) * inverse).astype(BF16)
        attention_forward(joined[layer], probs, att.at[layer, slot], layer)
        return (wide + mm_nt(att[layer, slot], wo[weights])).astype(BF16)

    across = [remote(passed.at[s], entry.at[s], entry_send.at[s], entry_recv.at[s], flip_dev) for s in range(2)]
    onward = [
        remote(passed.at[0], hidden.at[0], entry_send.at[0], hop_recv.at[0], up_across_dev),
        remote(passed.at[1], hidden.at[0], entry_send.at[1], hop_recv.at[0], yp_dev),
    ]

    @pl.when(y == 0)
    def _():
        for copy in loads:
            copy.wait()

        def first_pass(s, carry):
            for k in range(2):
                @pl.when((s == k) & near)
                def _():
                    load_entry[k].wait()

                @pl.when((s == k) & far)
                def _():
                    across[k].wait_recv()

            passed[s] = run_forward(entry[s], x_hi, 0)
            for k in range(2):
                @pl.when((s == k) & near)
                def _():
                    across[k].start()

                @pl.when((s == k) & far)
                def _():
                    onward[k].start()

            return carry

        lax.fori_loop(0, 2, first_pass, 0)

        @pl.when(near)
        def _():
            for copy in across:
                copy.wait_send()

        @pl.when(far)
        def _():
            for copy in onward:
                copy.wait_send()

    other = 1 - x_hi
    piece = lax.rem(z + 2 * x_lo, 4)
    pieces = [lax.rem(piece + k, 4) for k in range(4)]

    def chunk(buf, slot, which, half, part):
        name, k, rows = part
        at = (half * 4 + which) * 128 + k * rows
        return buf[name].at[slot, pl.ds(pl.multiple_of(at, rows), rows)]

    held, given = {"q": wq, "o": wo}, {"q": wq_ref, "o": wo_ref}

    def flip_copy(i, block, source=None):
        return remote(block if source is None else source, block, flip_send.at[i], flip_recv.at[i], flip_dev)

    for i, part in enumerate(PARTS):
        go(flip_copy(i, chunk(held, x_hi, pieces[2], core, part), chunk(given, 0, pieces[2], core, part)))

    def spread(i, part):
        flip_copy(i, chunk(held, other, pieces[0], core, part)).wait_recv()
        block = chunk(held, other, pieces[0], core, part)
        for k, device in ((1, zm_dev), (2, side_dev), (3, zp_dev)):
            go(remote(block, block, spread_send.at[i, k], spread_recv.at[i, k], device))

    def core_copy(i, part, half):
        name, k, rows = part
        block = held[name].at[other].reshape(8, 128, held[name].shape[2])
        block = block.at[pl.ds(half * 4, 4), pl.ds(k * rows, rows)]
        return remote(block, block, core_send.at[i], core_recv.at[i], core_dev)

    def gather_rest(i, part):
        for k in (1, 2, 3):
            block = chunk(held, other, pieces[k], core, part)
            remote(block, block, spread_send.at[i, k], spread_recv.at[i, k], side_dev).wait_recv()
        go(core_copy(i, part, core))

    for i, part in enumerate(PARTS):
        spread(i, part)
        if i > 0:
            gather_rest(i - 1, PARTS[i - 1])
    gather_rest(len(PARTS) - 1, PARTS[-1])
    for i, part in enumerate(PARTS):
        core_copy(i, part, 1 - core).wait_recv()

    def transpose_weights():
        def one(k, carry):
            layer, cols = lax.div(k, 6), pl.ds(pl.multiple_of(lax.rem(k, 6) * 256, 256), 256)
            wqt[layer, cols] = wq[layer, :, cols].T
            return carry

        lax.fori_loop(0, 12, one, 0)

    @pl.when(y > 0)
    def _():
        for copy in loads:
            copy.wait()

    @pl.when(y >= 2)
    def _():
        transpose_weights()

    @pl.when((y == 0) & near)
    def _():
        load_in.wait()

    @pl.when((y == 0) & far)
    def _():
        in_hop.wait()

    @pl.when(y > 0)
    def _():
        h_hop.wait_recv()

    def forward(layer, carry):
        hidden[layer + 1] = run_forward(hidden[layer], layer, layer)
        return carry

    lax.fori_loop(0, 2, forward, 0)

    @pl.when((y > 0) & (y < 3))
    def _():
        h_hop.start()

    def share(buf, layer, number):
        return remote(
            buf.at[layer, 0:SEQ], buf.at[layer, SEQ : 2 * SEQ], share_send.at[number], share_recv.at[number], core_dev
        )

    shares = [share(normed, 0, 0), share(normed, 1, 1), share(dj, 0, 2), share(dj, 1, 3)]
    sent.extend(shares)

    def att_copy(layer, k, to_core=False):
        if to_core:
            block = att.at[layer, 2 * lax.rem(z + 4 - k, 4) + core]
            return remote(block, block, att_core_send.at[layer, k], att_core_recv.at[layer, k], core_dev)
        block = att.at[layer, slot]
        return remote(block, block, att_send.at[layer, k], att_recv.at[layer, k], column[k][0])

    spread_att = [att_copy(layer, k) for layer in (1, 0) for k in (1, 3, 2)]
    core_att = [att_copy(layer, k, True) for layer in (1, 0) for k in (0, 1, 3, 2)]
    sent.extend(spread_att + core_att)

    def send_attention():
        shares[0].start()
        shares[1].start()
        for copy in spread_att:
            copy.start()

    def pass_attention():
        for layer in (1, 0):
            for k in (0, 1, 3, 2):
                if k:
                    block = att.at[layer, 2 * lax.rem(z + 4 - k, 4) + core]
                    remote(block, block, att_send.at[layer, k], att_recv.at[layer, k], core_dev).wait_recv()
                att_copy(layer, k, True).start()

    def await_attention(layer):
        for k in range(4):
            block = att.at[layer, 2 * lax.rem(z + 4 - k, 4) + 1 - core]
            remote(block, block, att_core_send.at[layer, k], att_core_recv.at[layer, k], core_dev).wait_recv()

    def c_copy(layer, k, c):
        source = c_pack.at[layer, core if c == 0 else 1 - core, lax.rem(z + k, 4)]
        return remote(source, c_all.at[layer, slot], c_send.at[layer, 2 * k + c], c_recv.at[layer, 2 * k + c], column[k][c])

    def send_c(layer):
        low = lax.broadcasted_iota(jnp.int32, (SEQ, 128), 1) < 64
        for to in range(4):
            a = upstream[layer + 1, :, 256 * to : 256 * to + 128].astype(F32)
            b = upstream[layer + 1, :, 256 * to + 128 : 256 * to + 256].astype(F32)
            c_pack[layer, 0, to] = jnp.where(low, a, pltpu.roll(b, 64, 1)).astype(BF16)
            c_pack[layer, 1, to] = jnp.where(low, pltpu.roll(a, 64, 1), b).astype(BF16)
        c_all[layer, slot] = c_pack[layer, core, z]
        for k in (1, 3, 2, 0):
            for c in range(2):
                if (k, c) != (0, 0):
                    c_copy(layer, k, c).start()

    def await_c(layer):
        for k in range(4):
            for c in range(2):
                if (k, c) != (0, 0):
                    block = c_all.at[layer, 2 * lax.rem(z + 4 - k, 4) + (core if c == 0 else 1 - core)]
                    remote(
                        block, block, c_send.at[layer, 2 * k + c], c_recv.at[layer, 2 * k + c], core_dev
                    ).wait_recv()

    sent.extend(c_copy(layer, k, c) for layer in range(2) for k in range(4) for c in range(2) if (k, c) != (0, 0))

    @pl.when(y < 3)
    def _():
        send_attention()

    @pl.when(y < 2)
    def _():
        transpose_weights()
        pass_attention()

    @pl.when((y == 3) & near)
    def _():
        load_cot.wait()

    @pl.when((y == 3) & far)
    def _():
        cot_hop.wait()

    def run_backward(layer, half):
        rows = pl.ds(64 * half, 64)
        d_attention = mm(upstream[layer + 1, rows], wo[layer]).astype(BF16)
        attention_backward(joined[layer], d_attention, probs, dj, carried, layer, half)

        @pl.when((layer > 0) | (y > 0))
        def _():
            d_normed = mm(dj[layer, rows], wqt[layer])
            wide = hidden[layer, rows].astype(F32)
            inverse = inverse_norm(wide)
            scaled = wide * inverse
            along = jnp.mean(d_normed * scaled, axis=-1, keepdims=True)
            upstream[layer, rows] = (
                upstream[layer + 1, rows].astype(F32) + inverse * (d_normed - scaled * along)
            ).astype(BF16)

    for half in (1, 0):
        @pl.when(y < 3)
        def _():
            c_hop[half].wait_recv()

        def backward(step, carry):
            layer = 1 - step
            if half == 0:
                @pl.when(y == 0)
                def _():
                    send_c(layer)

            run_backward(layer, half)
            if half == 0:
                share(dj, layer, 2 + layer).start()
            return carry

        lax.fori_loop(0, 2, backward, 0)

        @pl.when(y > 0)
        def _():
            c_hop[half].start()

    @pl.when(y == 3)
    def _():
        send_attention()

    low = lax.broadcasted_iota(jnp.int32, (2 * SEQ, 128), 1) < 64

    def own_columns(block):
        def tile(k):
            return block[:, 128 * k : 128 * k + 128].astype(F32)

        tiles = []
        for lo in range(2):
            for pair in range(2):
                a, b = tile(4 * pair + lo), tile(4 * pair + 2 + lo)
                first = jnp.where(core == 0, a, pltpu.roll(a, 64, 1))
                second = jnp.where(core == 0, pltpu.roll(b, 64, 1), b)
                tiles.append(jnp.where(low, first, second).astype(BF16))
        return jnp.concatenate(tiles, axis=1)

    def gradient(layer):
        left = own_columns(normed[layer])
        for lo in range(2):
            part = mm_tn(left[:, 256 * lo : 256 * lo + 256], dj[layer]).astype(BF16)
            grads[2 * layer + lo] = part.reshape(4, 64, QKV)

    def gradient_out(layer):
        await_c(layer)
        await_attention(layer)
        part = mm_tn(c_all[layer].reshape(8 * SEQ, 128), att[layer].reshape(8 * SEQ, D)).astype(BF16)
        grads_out[2 * layer : 2 * layer + 2] = part.reshape(2, 64, D)

    def ring_sum(view, position, plus, minus, bufs, sems, layers=None):
        a1, b1, m2, p2, alpha, beta = bufs
        opposite, after, before = (lax.rem(position + k, 4) for k in (2, 1, 3))
        s, r = sum_send.at, sum_recv.at
        copies = [
            remote(view(opposite, 0), a1, s[sems], r[sems], plus),
            remote(view(opposite, 1), b1, s[sems + 1], r[sems + 1], minus),
            remote(view(after, 1), m2.at[beta], s[sems + 2], r[sems + 2], plus),
            remote(view(before, 0), p2.at[alpha], s[sems + 3], r[sems + 3], minus),
            remote(view(after, 0), m2.at[alpha], s[sems + 4], r[sems + 4], plus),
            remote(view(before, 1), p2.at[beta], s[sems + 5], r[sems + 5], minus),
        ]
        sent.extend(copies)

        def only(stage, target):
            if stage is None:
                return lambda body: body()
            return pl.when(layers(target) == stage)

        def first(stage=None):
            @only(stage, opposite)
            def _():
                copies[0].start()
                copies[1].start()

            @only(stage, after)
            def _():
                copies[2].start()

            @only(stage, before)
            def _():
                copies[3].start()

        def second(stage=None):
            @only(stage, after)
            def _():
                mine = view(after, 0)
                copies[0].wait_recv()
                mine[...] = (mine[...].astype(F32) + a1[...].astype(F32)).astype(BF16)
                copies[4].start()

            @only(stage, before)
            def _():
                mine = view(before, 1)
                copies[1].wait_recv()
                mine[...] = (mine[...].astype(F32) + b1[...].astype(F32)).astype(BF16)
                copies[5].start()

        def last():
            for copy in copies[2:]:
                copy.wait_recv()

        return first, second, last

    def halves(offset):
        return [pl.ds(offset, QUARTER), pl.ds(offset + QUARTER, QUARTER)]

    z_cols, x_cols, own_cols = halves(0), halves(HALF), halves(0)
    wide_at = [(slice(None), slice(None), cols) for cols in own_cols]
    flat_at = [(slice(None), cols) for cols in own_cols]

    def z_ring(layer):
        pair = pl.ds(2 * layer, 2)
        bufs = (z_a1.at[pair], z_b1.at[pair], z_m2.at[pair], z_p2.at[pair], *wide_at)
        return ring_sum(lambda t, k: grads.at[pair, t, :, z_cols[k]], z, zp_dev, zm_dev, bufs, 24 if layer else 0)

    z_big = [z_ring(0), z_ring(1)]
    def layer_of(target):
        return lax.div(target, 2)

    x_big = ring_sum(
        lambda t, k: grads.at[t, :, :, x_cols[k]], x, xp_dev, xm_dev, (x_a1, x_b1, x_m2, x_p2, *wide_at), 6, layer_of
    )
    z_small = ring_sum(
        lambda t, k: z_r.at[t, :, own_cols[k]], x, xp_dev, xm_dev, (z_sa1, z_sb1, z_sm2, z_sp2, *flat_at), 12, layer_of
    )
    x_small = ring_sum(
        lambda t, k: x_r.at[t, :, own_cols[k]], z, zp_dev, zm_dev, (x_sa1, x_sb1, x_sm2, x_sp2, *flat_at), 18
    )
    out_at = [(slice(None), pl.ds(0, WIDE)), (slice(None), pl.ds(WIDE, WIDE))]
    o_ring = ring_sum(
        lambda t, k: grads_out.at[t, :, pl.ds(k * WIDE, WIDE)], x, xp_dev, xm_dev, (o_a1, o_b1, o_m2, o_p2, *out_at), 30
    )

    def sum_z(layer):
        pair = slice(2 * layer, 2 * layer + 2)
        z_r[pair] = (grads[pair, z, :, 0:HALF].astype(F32) + z_m2[pair].astype(F32) + z_p2[pair].astype(F32)).astype(BF16)

    shares[1].wait_recv()
    shares[3].wait_recv()
    gradient(1)
    z_big[1][0]()
    x_big[0](1)
    shares[0].wait_recv()
    shares[2].wait_recv()
    gradient(0)
    z_big[0][0]()
    x_big[0](0)

    @pl.when(y > 0)
    def _():
        send_c(1)
        send_c(0)

    @pl.when(y >= 2)
    def _():
        pass_attention()

    gradient_out(1)
    gradient_out(0)
    o_ring[0]()
    z_big[1][1]()
    x_big[1](1)
    z_big[0][1]()
    x_big[1](0)
    z_big[1][2]()
    sum_z(1)
    z_small[0](1)
    o_ring[1]()
    z_big[0][2]()
    sum_z(0)
    z_small[0](0)
    x_big[2]()
    x_r[...] = (grads[x, :, :, HALF:QKV].astype(F32) + x_m2[...].astype(F32) + x_p2[...].astype(F32)).astype(BF16)
    x_small[0]()
    z_small[1](1)
    z_small[1](0)
    x_small[1]()
    o_ring[2]()
    out_ref[:, QKV:COLS] = grads_out[x].astype(F32) + o_m2[...].astype(F32) + o_p2[...].astype(F32)
    z_small[2]()
    out_ref[:, 0:HALF] = z_r[x].astype(F32) + z_sm2[...].astype(F32) + z_sp2[...].astype(F32)
    x_small[2]()
    out_ref[:, HALF:QKV] = x_r[z].astype(F32) + x_sm2[...].astype(F32) + x_sp2[...].astype(F32)

    for copy in sent:
        copy.wait_send()

    @pl.when((y > 0) & (y < 3))
    def _():
        h_hop.wait_send()

    @pl.when(y > 0)
    def _():
        c_hop[0].wait_send()
        c_hop[1].wait_send()


def split_columns(total_ref, gq_ref, go_ref):
    gq_ref[0] = total_ref[:, :QKV]
    go_ref[0] = total_ref[:, QKV:]


def on_device(inputs, cotangent, w_qkv, w_out):
    any_space = pl.BlockSpec(memory_space=pl.ANY)
    vmem = pl.BlockSpec(memory_space=pltpu.VMEM)
    dma = pltpu.SemaphoreType.DMA

    def flow():
        return [
            pltpu.VMEM((4, 64, QUARTER), BF16),
            pltpu.VMEM((4, 64, QUARTER), BF16),
            pltpu.VMEM((4, 64, HALF), BF16),
            pltpu.VMEM((4, 64, HALF), BF16),
            pltpu.VMEM((4, 64, HALF), BF16),
            pltpu.VMEM((64, QUARTER), BF16),
            pltpu.VMEM((64, QUARTER), BF16),
            pltpu.VMEM((64, HALF), BF16),
            pltpu.VMEM((64, HALF), BF16),
        ]

    total = pl.pallas_call(
        kernel,
        out_shape=jax.ShapeDtypeStruct((64, COLS), F32),
        in_specs=[any_space] * 4,
        out_specs=vmem,
        scratch_shapes=[
            pltpu.VMEM((2, D, QKV), BF16),
            pltpu.VMEM((2, D, D), BF16),
            pltpu.VMEM((2, QKV, D), BF16),
            pltpu.VMEM((2, SEQ, D), BF16),
            pltpu.VMEM((2, SEQ, D), BF16),
            pltpu.VMEM((3, SEQ, D), BF16),
            pltpu.VMEM((2, 2 * SEQ, D), BF16),
            pltpu.VMEM((2, SEQ, QKV), BF16),
            pltpu.VMEM((2, 4, 256, 256), BF16),
            pltpu.VMEM((2, 8, SEQ, D), BF16),
            pltpu.VMEM((3, SEQ, D), BF16),
            pltpu.VMEM((2, 2 * SEQ, QKV), BF16),
            pltpu.VMEM((2, 2, 2, 64, 128), F32),
            pltpu.VMEM((2, 2, 4, SEQ, 128), BF16),
            pltpu.VMEM((2, 8, SEQ, 128), BF16),
            pltpu.VMEM((4, 4, 64, QKV), BF16),
            pltpu.VMEM((4, 64, D), BF16),
            *flow(),
            *flow(),
            pltpu.VMEM((64, WIDE), BF16),
            pltpu.VMEM((64, WIDE), BF16),
            pltpu.VMEM((64, D), BF16),
            pltpu.VMEM((64, D), BF16),
            dma((6,)),
            dma((len(PARTS),)),
            dma((len(PARTS),)),
            dma((len(PARTS), 4)),
            dma((len(PARTS), 4)),
            dma((len(PARTS),)),
            dma((len(PARTS),)),
            dma((2,)),
            dma((2,)),
            dma((5,)),
            dma((5,)),
            dma((4,)),
            dma((4,)),
            dma((2, 4)),
            dma((2, 4)),
            dma((2, 4)),
            dma((2, 4)),
            dma((2, 8)),
            dma((2, 8)),
            dma((36,)),
            dma((36,)),
        ],
        compiler_params=pltpu.CompilerParams(
            collective_id=0, has_side_effects=True, vmem_limit_bytes=56 * 2**20
        ),
    )(inputs, cotangent, w_qkv, w_out)
    return pl.pallas_call(
        split_columns,
        out_shape=(jax.ShapeDtypeStruct((1, 64, QKV), F32), jax.ShapeDtypeStruct((1, 64, D), F32)),
    )(total)


def solution(mesh):
    placed = (
        P("dp", None, None, None, None),
        P("dp", None, None, None, None),
        P("section", None, None),
        P("section", None, None),
    )
    return jax.shard_map(
        on_device,
        mesh=mesh,
        in_specs=placed,
        out_specs=(P("section", "dp", None), P("section", "dp", None)),
        check_vma=False,
    )
```

```python
import functools

import jax
import jax.numpy as jnp
from jax import lax
from jax.experimental import pallas as pl
from jax.experimental.pallas import tpu as pltpu
from jax.sharding import PartitionSpec as P

MESH = pl.DeviceIdType.MESH
F32 = jnp.float32
BF16 = jnp.bfloat16
EPSILON = 1e-05

D = 1024
SEQ = 128
QKV = 1536
COLS = 2560
HALF = 768
QUARTER = 384
WIDE = 512
PARTS = [("q", k, 32) for k in range(4)] + [("o", k, 64) for k in range(2)]


def mm(a, b):
    return jnp.dot(a, b, preferred_element_type=F32)


def mm_nt(a, b):
    return lax.dot_general(a, b, (((1,), (1,)), ((), ())), preferred_element_type=F32)


def mm_tn(a, b):
    return lax.dot_general(a, b, (((0,), (0,)), ((), ())), preferred_element_type=F32)


def block_diagonal(pair, group):
    low = lax.broadcasted_iota(jnp.int32, pair.shape, 1) < 64
    wide = pair.astype(F32)
    rolled = pltpu.roll(wide, 64, 1)
    first, second = (wide, rolled) if group % 2 == 0 else (rolled, wide)
    zero = jnp.zeros_like(wide)
    return jnp.concatenate([jnp.where(low, first, zero), jnp.where(low, zero, second)], axis=0).astype(BF16)


def stack_pairs(x, group):
    at = group * 256
    blocks = []
    for start in range(0, x.shape[0], 64):
        blocks += [x[start : start + 64, at : at + 128], x[start : start + 64, at + 128 : at + 256]]
    return jnp.concatenate(blocks, axis=0)


def head_sums(x):
    return (jnp.sum(x[:128], axis=0, keepdims=True), jnp.sum(x[128:], axis=0, keepdims=True))


def kv_pairs(joined, group):
    at = (group // 2) * 128
    return joined[:, D + at : D + at + 128], joined[:, D + 256 + at : D + 256 + at + 128]


def attention_forward(joined, probs_ref, keys_ref, values_ref, att_ref, layer):
    key = lax.broadcasted_iota(jnp.int32, (256, 256), 0) & 127
    column = lax.broadcasted_iota(jnp.int32, (256, 256), 1)
    causal = key <= (column & 63) + 64 * lax.shift_right_logical(column, 7)
    for group in range(4):
        queries = stack_pairs(joined, group)
        keys, values = (block_diagonal(pair, group) for pair in kv_pairs(joined, group))
        keys_ref[layer, group] = keys
        values_ref[layer, group] = values
        scores = mm_nt(keys, queries) * 0.125
        exponent = jnp.where(causal, jnp.exp(scores), 0.0)
        first, second = head_sums(exponent)
        probs = jnp.concatenate([exponent[:128] * (1.0 / first), exponent[128:] * (1.0 / second)], axis=0).astype(BF16)
        probs_ref[layer, group] = probs
        mixed = mm_tn(probs, values).astype(BF16)
        at = group * 256
        for half in range(2):
            rows = slice(64 * half, 64 * half + 64)
            att_ref[rows, at : at + 128] = mixed[128 * half : 128 * half + 64]
            att_ref[rows, at + 128 : at + 256] = mixed[128 * half + 64 : 128 * half + 128]


def attention_backward(joined, d_attention, probs_ref, keys_ref, values_ref, dj_ref, carried, layer, half):
    rows = pl.ds(64 * half, 64)
    early, late = slice(0, 64), slice(64, 128)
    d_keys, d_values = [], []
    for group in range(4):
        queries = stack_pairs(joined, group)
        d_heads = stack_pairs(d_attention, group)
        probs = probs_ref[layer, group, :, 128 * half : 128 * half + 128]
        d_probs = mm_nt(values_ref[layer, group], d_heads)
        wide = probs.astype(F32)
        first, second = head_sums(wide * d_probs)
        centred = jnp.concatenate([d_probs[:128] - first, d_probs[128:] - second], axis=0)
        d_scores = (wide * centred * 0.125).astype(BF16)
        d_keys.append(mm(d_scores, queries))
        d_values.append(mm(probs, d_heads))
        d_queries = mm_tn(d_scores, keys_ref[layer, group]).astype(BF16)
        lane = group * 256
        dj_ref[layer, rows, lane : lane + 128] = d_queries[:64]
        dj_ref[layer, rows, lane + 128 : lane + 256] = d_queries[64:]
    low = lax.broadcasted_iota(jnp.int32, (128, 128), 1) < 64

    def merged(even, odd):
        first = even[:128] + pltpu.roll(even[128:], 64, 1)
        second = pltpu.roll(odd[:128], 64, 1) + odd[128:]
        return jnp.where(low, first, second)

    for number, parts in ((0, d_keys), (1, d_values)):
        for pair in range(2):
            total = merged(parts[2 * pair], parts[2 * pair + 1])
            lane = D + 256 * number + 128 * pair
            if half:
                carried[layer, number, pair] = total[early]
                dj_ref[layer, rows, lane : lane + 128] = total[late].astype(BF16)
            else:
                dj_ref[layer, rows, lane : lane + 128] = (total[early] + carried[layer, number, pair]).astype(BF16)


def inverse_norm(wide):
    return lax.rsqrt(jnp.mean(wide * wide, axis=-1, keepdims=True) + EPSILON)


def kernel(
    inputs_ref, cotangent_ref, wq_ref, wo_ref,
    out_ref,
    wq, wo, wqt, entry, passed, hidden, normed, joined, probs, keys, values, att, upstream, dj, carried, c_pack, c_all, grads, grads_out,
    z_a1, z_b1, z_m2, z_p2, z_r, z_sa1, z_sb1, z_sm2, z_sp2,
    x_a1, x_b1, x_m2, x_p2, x_r, x_sa1, x_sb1, x_sm2, x_sp2,
    o_a1, o_b1, o_m2, o_p2,
    load_sem, flip_send, flip_recv, spread_send, spread_recv, core_send, core_recv,
    entry_send, entry_recv, hop_send, hop_recv, share_send, share_recv,
    att_send, att_recv, att_core_send, att_core_recv, c_send, c_recv, sum_send, sum_recv,
):
    section, dp = lax.axis_index("section"), lax.axis_index("dp")
    y, x_hi = lax.div(section, 2), lax.rem(section, 2)
    z, x_lo, core = lax.div(dp, 4), lax.rem(lax.div(dp, 2), 2), lax.rem(dp, 2)
    x = 2 * x_hi + x_lo
    slot = 2 * z + core

    def place(y, x, z, core):
        return (2 * y + lax.div(x, 2), 4 * z + 2 * lax.rem(x, 2) + core)

    core_dev = place(y, x, z, 1 - core)
    xp_dev, xm_dev = place(y, lax.rem(x + 1, 4), z, core), place(y, lax.rem(x + 3, 4), z, core)
    zp_dev, zm_dev = place(y, x, lax.rem(z + 1, 4), core), place(y, x, lax.rem(z + 3, 4), core)
    yp_dev, ym_dev = place(lax.rem(y + 1, 4), x, z, core), place(lax.rem(y + 3, 4), x, z, core)
    column = [[place(y, x, lax.rem(z + k, 4), c) for c in (core, 1 - core)] for k in range(4)]
    flip_dev = place(y, 3 - x, z, core)
    side_dev = place(y, 2 * x_hi + 1 - x_lo, z, core)
    up_across_dev, down_across_dev = place(lax.rem(y + 1, 4), 3 - x, z, core), place(lax.rem(y + 3, 4), 3 - x, z, core)

    def remote(src, dst, send_sem, recv_sem, device):
        return pltpu.make_async_remote_copy(
            src_ref=src, dst_ref=dst, send_sem=send_sem, recv_sem=recv_sem, device_id=device, device_id_type=MESH
        )

    sent = []

    def go(copy):
        copy.start()
        sent.append(copy)

    loads = [
        pltpu.make_async_copy(wq_ref.at[0], wq.at[x_hi], load_sem.at[0]),
        pltpu.make_async_copy(wo_ref.at[0], wo.at[x_hi], load_sem.at[1]),
    ]
    load_in = pltpu.make_async_copy(inputs_ref.at[0, 0, 0], hidden.at[0], load_sem.at[2])
    load_cot = pltpu.make_async_copy(cotangent_ref.at[0, 0, 0], upstream.at[2], load_sem.at[3])
    load_entry = [pltpu.make_async_copy(inputs_ref.at[0, s, 0], entry.at[s], load_sem.at[4 + s]) for s in range(2)]
    for copy in loads:
        copy.start()

    near, far = x_hi == 0, x_hi == 1

    @pl.when((y == 0) & near)
    def _():
        load_entry[0].start()
        load_entry[1].start()
        load_in.start()

    @pl.when((y == 3) & near)
    def _():
        load_cot.start()

    barrier = pltpu.get_barrier_semaphore()
    ring = [column[k][c] for k in range(4) for c in range(2) if (k, c) != (0, 0)]
    for device in (*ring, xp_dev, xm_dev, yp_dev, ym_dev, up_across_dev, down_across_dev):
        pl.semaphore_signal(barrier, inc=1, device_id=device, device_id_type=MESH)
    pl.semaphore_wait(barrier, 13)

    in_hop = remote(inputs_ref.at[0, 1, 0], hidden.at[0], hop_send.at[2], hop_recv.at[2], side_dev)
    cot_hop = remote(cotangent_ref.at[0, 1, 0], upstream.at[2], hop_send.at[3], hop_recv.at[3], side_dev)

    @pl.when((y == 0) & far)
    def _():
        in_hop.start()

    @pl.when((y == 3) & far)
    def _():
        cot_hop.start()

    h_hop = remote(hidden.at[2], hidden.at[0], hop_send.at[0], hop_recv.at[0], yp_dev)
    c_hop = [
        remote(
            upstream.at[0, 64 * half : 64 * half + 64], upstream.at[2, 64 * half : 64 * half + 64],
            hop_send.at[(1, 4)[half]], hop_recv.at[(1, 4)[half]], ym_dev,
        )
        for half in range(2)
    ]

    def run_forward(h, weights, layer):
        wide = h.astype(F32)
        inverse = inverse_norm(wide)
        normed[layer, 0:SEQ] = (wide * inverse).astype(BF16)
        joined[layer] = (mm(h, wq[weights]) * inverse).astype(BF16)
        attention_forward(joined[layer], probs, keys, values, att.at[layer, slot], layer)
        return (wide + mm_nt(att[layer, slot], wo[weights])).astype(BF16)

    across = [remote(passed.at[s], entry.at[s], entry_send.at[s], entry_recv.at[s], flip_dev) for s in range(2)]
    onward = [
        remote(passed.at[0], hidden.at[0], entry_send.at[0], hop_recv.at[0], up_across_dev),
        remote(passed.at[1], hidden.at[0], entry_send.at[1], hop_recv.at[0], yp_dev),
    ]

    @pl.when(y == 0)
    def _():
        for copy in loads:
            copy.wait()

        def first_pass(s, carry):
            for k in range(2):
                @pl.when((s == k) & near)
                def _():
                    load_entry[k].wait()

                @pl.when((s == k) & far)
                def _():
                    across[k].wait_recv()

            passed[s] = run_forward(entry[s], x_hi, 0)
            for k in range(2):
                @pl.when((s == k) & near)
                def _():
                    across[k].start()

                @pl.when((s == k) & far)
                def _():
                    onward[k].start()

            return carry

        lax.fori_loop(0, 2, first_pass, 0)

        @pl.when(near)
        def _():
            for copy in across:
                copy.wait_send()

        @pl.when(far)
        def _():
            for copy in onward:
                copy.wait_send()

    other = 1 - x_hi
    piece = lax.rem(z + 2 * x_lo, 4)
    pieces = [lax.rem(piece + k, 4) for k in range(4)]

    def chunk(buf, slot, which, half, part):
        name, k, rows = part
        at = (half * 4 + which) * 128 + k * rows
        return buf[name].at[slot, pl.ds(pl.multiple_of(at, rows), rows)]

    held, given = {"q": wq, "o": wo}, {"q": wq_ref, "o": wo_ref}

    def flip_copy(i, block, source=None):
        return remote(block if source is None else source, block, flip_send.at[i], flip_recv.at[i], flip_dev)

    for i, part in enumerate(PARTS):
        go(flip_copy(i, chunk(held, x_hi, pieces[2], core, part), chunk(given, 0, pieces[2], core, part)))

    def spread(i, part):
        flip_copy(i, chunk(held, other, pieces[0], core, part)).wait_recv()
        block = chunk(held, other, pieces[0], core, part)
        for k, device in ((1, zm_dev), (2, side_dev), (3, zp_dev)):
            go(remote(block, block, spread_send.at[i, k], spread_recv.at[i, k], device))

    def core_copy(i, part, half):
        name, k, rows = part
        block = held[name].at[other].reshape(8, 128, held[name].shape[2])
        block = block.at[pl.ds(half * 4, 4), pl.ds(k * rows, rows)]
        return remote(block, block, core_send.at[i], core_recv.at[i], core_dev)

    def gather_rest(i, part):
        for k in (1, 2, 3):
            block = chunk(held, other, pieces[k], core, part)
            remote(block, block, spread_send.at[i, k], spread_recv.at[i, k], side_dev).wait_recv()
        go(core_copy(i, part, core))

    for i, part in enumerate(PARTS):
        spread(i, part)
        if i > 0:
            gather_rest(i - 1, PARTS[i - 1])
    gather_rest(len(PARTS) - 1, PARTS[-1])
    for i, part in enumerate(PARTS):
        core_copy(i, part, 1 - core).wait_recv()

    def transpose_weights():
        def one(k, carry):
            layer, cols = lax.div(k, 6), pl.ds(pl.multiple_of(lax.rem(k, 6) * 256, 256), 256)
            wqt[layer, cols] = wq[layer, :, cols].T
            return carry

        lax.fori_loop(0, 12, one, 0)

    @pl.when(y > 0)
    def _():
        for copy in loads:
            copy.wait()

    @pl.when(y >= 2)
    def _():
        transpose_weights()

    @pl.when((y == 0) & near)
    def _():
        load_in.wait()

    @pl.when((y == 0) & far)
    def _():
        in_hop.wait()

    @pl.when(y > 0)
    def _():
        h_hop.wait_recv()

    def forward(layer, carry):
        hidden[layer + 1] = run_forward(hidden[layer], layer, layer)
        return carry

    lax.fori_loop(0, 2, forward, 0)

    @pl.when((y > 0) & (y < 3))
    def _():
        h_hop.start()

    def share(buf, layer, number):
        return remote(
            buf.at[layer, 0:SEQ], buf.at[layer, SEQ : 2 * SEQ], share_send.at[number], share_recv.at[number], core_dev
        )

    shares = [share(dj, 0, 0), share(dj, 1, 1)]
    share_normed = remote(
        normed.at[:, 0:SEQ], normed.at[:, SEQ : 2 * SEQ], share_send.at[2], share_recv.at[2], core_dev
    )
    sent.extend(shares)

    def att_block(k, half):
        return att.at[:, 2 * lax.rem(z + 4 - k, 4) + half]

    def att_copy(k):
        return remote(att_block(0, core), att_block(0, core), att_send.at[k], att_recv.at[k], column[k][0])

    def core_att(k):
        return remote(att_block(k, core), att_block(k, core), att_core_send.at[k], att_core_recv.at[k], core_dev)

    def send_attention():
        share_normed.start()
        for k in (1, 3, 2):
            att_copy(k).start()

    def pass_attention():
        core_att(0).start()
        for k in (1, 3, 2):
            remote(att_block(k, core), att_block(k, core), att_send.at[k], att_recv.at[k], core_dev).wait_recv()
            core_att(k).start()

    def await_attention():
        for k in range(4):
            block = att_block(k, 1 - core)
            remote(block, block, att_core_send.at[k], att_core_recv.at[k], core_dev).wait_recv()

    early = sent[: -len(shares)]
    del sent[: len(early)]

    def settle():
        for copy in early:
            copy.wait_send()
        share_normed.wait_send()
        for k in (1, 3, 2):
            att_copy(k).wait_send()
        for k in range(4):
            core_att(k).wait_send()

    def c_copy(layer, k, c):
        source = c_pack.at[layer, core if c == 0 else 1 - core, lax.rem(z + k, 4)]
        return remote(source, c_all.at[layer, slot], c_send.at[layer, 2 * k + c], c_recv.at[layer, 2 * k + c], column[k][c])

    def send_c(layer):
        low = lax.broadcasted_iota(jnp.int32, (SEQ, 128), 1) < 64
        for to in range(4):
            a = upstream[layer + 1, :, 256 * to : 256 * to + 128].astype(F32)
            b = upstream[layer + 1, :, 256 * to + 128 : 256 * to + 256].astype(F32)
            c_pack[layer, 0, to] = jnp.where(low, a, pltpu.roll(b, 64, 1)).astype(BF16)
            c_pack[layer, 1, to] = jnp.where(low, pltpu.roll(a, 64, 1), b).astype(BF16)
        c_all[layer, slot] = c_pack[layer, core, z]
        for k in (1, 3, 2, 0):
            for c in range(2):
                if (k, c) != (0, 0):
                    c_copy(layer, k, c).start()

    def await_c(layer):
        for k in range(4):
            for c in range(2):
                if (k, c) != (0, 0):
                    block = c_all.at[layer, 2 * lax.rem(z + 4 - k, 4) + (core if c == 0 else 1 - core)]
                    remote(
                        block, block, c_send.at[layer, 2 * k + c], c_recv.at[layer, 2 * k + c], core_dev
                    ).wait_recv()

    sent.extend(c_copy(layer, k, c) for layer in range(2) for k in range(4) for c in range(2) if (k, c) != (0, 0))

    send_attention()

    @pl.when(y < 2)
    def _():
        transpose_weights()
        pass_attention()
        await_attention()
        share_normed.wait_recv()
        settle()

    @pl.when((y == 3) & near)
    def _():
        load_cot.wait()

    @pl.when((y == 3) & far)
    def _():
        cot_hop.wait()

    def run_backward(layer, half):
        rows = pl.ds(64 * half, 64)
        d_attention = mm(upstream[layer + 1, rows], wo[layer]).astype(BF16)
        attention_backward(joined[layer, rows], d_attention, probs, keys, values, dj, carried, layer, half)

        @pl.when((layer > 0) | (y > 0))
        def _():
            d_normed = mm(dj[layer, rows], wqt[layer])
            wide = hidden[layer, rows].astype(F32)
            inverse = inverse_norm(wide)
            scaled = wide * inverse
            along = jnp.mean(d_normed * scaled, axis=-1, keepdims=True)
            upstream[layer, rows] = (
                upstream[layer + 1, rows].astype(F32) + inverse * (d_normed - scaled * along)
            ).astype(BF16)

    for half in (1, 0):
        @pl.when(y < 3)
        def _():
            c_hop[half].wait_recv()

        def backward(step, carry):
            layer = 1 - step
            if half == 0:
                @pl.when(y == 0)
                def _():
                    send_c(layer)

            run_backward(layer, half)
            if half == 0:
                share(dj, layer, layer).start()
            return carry

        lax.fori_loop(0, 2, backward, 0)

        @pl.when(y > 0)
        def _():
            c_hop[half].start()

    @pl.when(y > 0)
    def _():
        send_c(1)
        send_c(0)

    @pl.when(y >= 2)
    def _():
        share_normed.wait_recv()

    low = lax.broadcasted_iota(jnp.int32, (2 * SEQ, 128), 1) < 64

    def own_columns(block):
        def tile(k):
            return block[:, 128 * k : 128 * k + 128].astype(F32)

        tiles = []
        for lo in range(2):
            for pair in range(2):
                a, b = tile(4 * pair + lo), tile(4 * pair + 2 + lo)
                first = jnp.where(core == 0, a, pltpu.roll(a, 64, 1))
                second = jnp.where(core == 0, pltpu.roll(b, 64, 1), b)
                tiles.append(jnp.where(low, first, second).astype(BF16))
        return jnp.concatenate(tiles, axis=1)

    def gradient(layer):
        left = own_columns(normed[layer])
        for lo in range(2):
            part = mm_tn(left[:, 256 * lo : 256 * lo + 256], dj[layer]).astype(BF16)
            grads[2 * layer + lo] = part.reshape(4, 64, QKV)

    def gradient_out(layer):
        await_c(layer)
        part = mm_tn(c_all[layer].reshape(8 * SEQ, 128), att[layer].reshape(8 * SEQ, D)).astype(BF16)
        grads_out[2 * layer : 2 * layer + 2] = part.reshape(2, 64, D)

    def ring_sum(view, position, plus, minus, bufs, sems, layers=None):
        a1, b1, m2, p2, alpha, beta = bufs
        opposite, after, before = (lax.rem(position + k, 4) for k in (2, 1, 3))
        s, r = sum_send.at, sum_recv.at
        copies = [
            remote(view(opposite, 0), a1, s[sems], r[sems], plus),
            remote(view(opposite, 1), b1, s[sems + 1], r[sems + 1], minus),
            remote(view(after, 1), m2.at[beta], s[sems + 2], r[sems + 2], plus),
            remote(view(before, 0), p2.at[alpha], s[sems + 3], r[sems + 3], minus),
            remote(view(after, 0), m2.at[alpha], s[sems + 4], r[sems + 4], plus),
            remote(view(before, 1), p2.at[beta], s[sems + 5], r[sems + 5], minus),
        ]
        sent.extend(copies)

        def only(stage, target):
            if stage is None:
                return lambda body: body()
            return pl.when(layers(target) == stage)

        def first(stage=None):
            @only(stage, opposite)
            def _():
                copies[0].start()
                copies[1].start()

            @only(stage, after)
            def _():
                copies[2].start()

            @only(stage, before)
            def _():
                copies[3].start()

        def second(stage=None):
            @only(stage, after)
            def _():
                mine = view(after, 0)
                copies[0].wait_recv()
                mine[...] = (mine[...].astype(F32) + a1[...].astype(F32)).astype(BF16)
                copies[4].start()

            @only(stage, before)
            def _():
                mine = view(before, 1)
                copies[1].wait_recv()
                mine[...] = (mine[...].astype(F32) + b1[...].astype(F32)).astype(BF16)
                copies[5].start()

        def last():
            for copy in copies[2:]:
                copy.wait_recv()

        return first, second, last

    def halves(offset):
        return [pl.ds(offset, QUARTER), pl.ds(offset + QUARTER, QUARTER)]

    z_cols, x_cols, own_cols = halves(0), halves(HALF), halves(0)
    wide_at = [(slice(None), slice(None), cols) for cols in own_cols]
    flat_at = [(slice(None), cols) for cols in own_cols]

    def z_ring(layer):
        pair = pl.ds(2 * layer, 2)
        bufs = (z_a1.at[pair], z_b1.at[pair], z_m2.at[pair], z_p2.at[pair], *wide_at)
        return ring_sum(lambda t, k: grads.at[pair, t, :, z_cols[k]], z, zp_dev, zm_dev, bufs, 24 if layer else 0)

    z_big = [z_ring(0), z_ring(1)]
    def layer_of(target):
        return lax.div(target, 2)

    x_big = ring_sum(
        lambda t, k: grads.at[t, :, :, x_cols[k]], x, xp_dev, xm_dev, (x_a1, x_b1, x_m2, x_p2, *wide_at), 6, layer_of
    )
    z_small = ring_sum(
        lambda t, k: z_r.at[t, :, own_cols[k]], x, xp_dev, xm_dev, (z_sa1, z_sb1, z_sm2, z_sp2, *flat_at), 12, layer_of
    )
    x_small = ring_sum(
        lambda t, k: x_r.at[t, :, own_cols[k]], z, zp_dev, zm_dev, (x_sa1, x_sb1, x_sm2, x_sp2, *flat_at), 18
    )
    out_at = [(slice(None), pl.ds(0, WIDE)), (slice(None), pl.ds(WIDE, WIDE))]
    o_ring = ring_sum(
        lambda t, k: grads_out.at[t, :, pl.ds(k * WIDE, WIDE)], x, xp_dev, xm_dev, (o_a1, o_b1, o_m2, o_p2, *out_at), 30
    )

    def sum_z(layer):
        pair = slice(2 * layer, 2 * layer + 2)
        z_r[pair] = (grads[pair, z, :, 0:HALF].astype(F32) + z_m2[pair].astype(F32) + z_p2[pair].astype(F32)).astype(BF16)

    shares[1].wait_recv()
    gradient(1)
    z_big[1][0]()
    x_big[0](1)
    shares[0].wait_recv()
    gradient(0)
    z_big[0][0]()
    x_big[0](0)

    @pl.when(y >= 2)
    def _():
        pass_attention()
        await_attention()

    gradient_out(1)
    gradient_out(0)
    o_ring[0]()
    z_big[1][1]()
    x_big[1](1)
    z_big[0][1]()
    x_big[1](0)
    z_big[1][2]()
    sum_z(1)
    z_small[0](1)
    o_ring[1]()
    z_big[0][2]()
    sum_z(0)
    z_small[0](0)
    x_big[2]()
    x_r[...] = (grads[x, :, :, HALF:QKV].astype(F32) + x_m2[...].astype(F32) + x_p2[...].astype(F32)).astype(BF16)
    x_small[0]()
    z_small[1](1)
    z_small[1](0)
    x_small[1]()
    o_ring[2]()
    out_ref[:, QKV:COLS] = grads_out[x].astype(F32) + o_m2[...].astype(F32) + o_p2[...].astype(F32)
    z_small[2]()
    out_ref[:, 0:HALF] = z_r[x].astype(F32) + z_sm2[...].astype(F32) + z_sp2[...].astype(F32)
    x_small[2]()
    out_ref[:, HALF:QKV] = x_r[z].astype(F32) + x_sm2[...].astype(F32) + x_sp2[...].astype(F32)

    @pl.when(y >= 2)
    def _():
        settle()

    for copy in sent:
        copy.wait_send()

    @pl.when((y > 0) & (y < 3))
    def _():
        h_hop.wait_send()

    @pl.when(y > 0)
    def _():
        c_hop[0].wait_send()
        c_hop[1].wait_send()


def split_columns(total_ref, gq_ref, go_ref):
    gq_ref[0] = total_ref[:, :QKV]
    go_ref[0] = total_ref[:, QKV:]


def on_device(inputs, cotangent, w_qkv, w_out):
    any_space = pl.BlockSpec(memory_space=pl.ANY)
    vmem = pl.BlockSpec(memory_space=pltpu.VMEM)
    dma = pltpu.SemaphoreType.DMA

    def flow():
        return [
            pltpu.VMEM((4, 64, QUARTER), BF16),
            pltpu.VMEM((4, 64, QUARTER), BF16),
            pltpu.VMEM((4, 64, HALF), BF16),
            pltpu.VMEM((4, 64, HALF), BF16),
            pltpu.VMEM((4, 64, HALF), BF16),
            pltpu.VMEM((64, QUARTER), BF16),
            pltpu.VMEM((64, QUARTER), BF16),
            pltpu.VMEM((64, HALF), BF16),
            pltpu.VMEM((64, HALF), BF16),
        ]

    total = pl.pallas_call(
        kernel,
        out_shape=jax.ShapeDtypeStruct((64, COLS), F32),
        in_specs=[any_space] * 4,
        out_specs=vmem,
        scratch_shapes=[
            pltpu.VMEM((2, D, QKV), BF16),
            pltpu.VMEM((2, D, D), BF16),
            pltpu.VMEM((2, QKV, D), BF16),
            pltpu.VMEM((2, SEQ, D), BF16),
            pltpu.VMEM((2, SEQ, D), BF16),
            pltpu.VMEM((3, SEQ, D), BF16),
            pltpu.VMEM((2, 2 * SEQ, D), BF16),
            pltpu.VMEM((2, SEQ, QKV), BF16),
            pltpu.VMEM((2, 4, 256, 256), BF16),
            pltpu.VMEM((2, 4, 256, 128), BF16),
            pltpu.VMEM((2, 4, 256, 128), BF16),
            pltpu.VMEM((2, 8, SEQ, D), BF16),
            pltpu.VMEM((3, SEQ, D), BF16),
            pltpu.VMEM((2, 2 * SEQ, QKV), BF16),
            pltpu.VMEM((2, 2, 2, 64, 128), F32),
            pltpu.VMEM((2, 2, 4, SEQ, 128), BF16),
            pltpu.VMEM((2, 8, SEQ, 128), BF16),
            pltpu.VMEM((4, 4, 64, QKV), BF16),
            pltpu.VMEM((4, 64, D), BF16),
            *flow(),
            *flow(),
            pltpu.VMEM((64, WIDE), BF16),
            pltpu.VMEM((64, WIDE), BF16),
            pltpu.VMEM((64, D), BF16),
            pltpu.VMEM((64, D), BF16),
            dma((6,)),
            dma((len(PARTS),)),
            dma((len(PARTS),)),
            dma((len(PARTS), 4)),
            dma((len(PARTS), 4)),
            dma((len(PARTS),)),
            dma((len(PARTS),)),
            dma((2,)),
            dma((2,)),
            dma((5,)),
            dma((5,)),
            dma((4,)),
            dma((4,)),
            dma((4,)),
            dma((4,)),
            dma((4,)),
            dma((4,)),
            dma((2, 8)),
            dma((2, 8)),
            dma((36,)),
            dma((36,)),
        ],
        compiler_params=pltpu.CompilerParams(
            collective_id=0, has_side_effects=True, vmem_limit_bytes=56 * 2**20
        ),
    )(inputs, cotangent, w_qkv, w_out)
    return pl.pallas_call(
        split_columns,
        out_shape=(jax.ShapeDtypeStruct((1, 64, QKV), F32), jax.ShapeDtypeStruct((1, 64, D), F32)),
    )(total)


def solution(mesh):
    placed = (
        P("dp", None, None, None, None),
        P("dp", None, None, None, None),
        P("section", None, None),
        P("section", None, None),
    )
    return jax.shard_map(
        on_device,
        mesh=mesh,
        in_specs=placed,
        out_specs=(P("section", "dp", None), P("section", "dp", None)),
        check_vma=False,
    )
```

```python
import functools

import jax
import jax.numpy as jnp
from jax import lax
from jax.experimental import pallas as pl
from jax.experimental.pallas import tpu as pltpu
from jax.sharding import PartitionSpec as P

MESH = pl.DeviceIdType.MESH
F32 = jnp.float32
BF16 = jnp.bfloat16
EPSILON = 1e-05

D = 1024
SEQ = 128
QKV = 1536
COLS = 2560
Z_CUT = (512, 384)
X_CUT = (256, 384)
HALF = sum(Z_CUT)
WIDE = 512
PARTS = [("q", k, 32) for k in range(4)] + [("o", k, 64) for k in range(2)]


def mm(a, b):
    return jnp.dot(a, b, preferred_element_type=F32)


def mm_nt(a, b):
    return lax.dot_general(a, b, (((1,), (1,)), ((), ())), preferred_element_type=F32)


def mm_tn(a, b):
    return lax.dot_general(a, b, (((0,), (0,)), ((), ())), preferred_element_type=F32)


def block_diagonal(pair, group):
    low = lax.broadcasted_iota(jnp.int32, pair.shape, 1) < 64
    wide = pair.astype(F32)
    rolled = pltpu.roll(wide, 64, 1)
    first, second = (wide, rolled) if group % 2 == 0 else (rolled, wide)
    zero = jnp.zeros_like(wide)
    return jnp.concatenate([jnp.where(low, first, zero), jnp.where(low, zero, second)], axis=0).astype(BF16)


def stack_pairs(x, group):
    at = group * 256
    blocks = []
    for start in range(0, x.shape[0], 64):
        blocks += [x[start : start + 64, at : at + 128], x[start : start + 64, at + 128 : at + 256]]
    return jnp.concatenate(blocks, axis=0)


def head_sums(x):
    return (jnp.sum(x[:128], axis=0, keepdims=True), jnp.sum(x[128:], axis=0, keepdims=True))


def kv_pairs(joined, group):
    at = (group // 2) * 128
    return joined[:, D + at : D + at + 128], joined[:, D + 256 + at : D + 256 + at + 128]


def attention_forward(joined, probs_ref, keys_ref, values_ref, att_ref, layer):
    key = lax.broadcasted_iota(jnp.int32, (256, 256), 0) & 127
    column = lax.broadcasted_iota(jnp.int32, (256, 256), 1)
    causal = key <= (column & 63) + 64 * lax.shift_right_logical(column, 7)
    for group in range(4):
        queries = stack_pairs(joined, group)
        keys, values = (block_diagonal(pair, group) for pair in kv_pairs(joined, group))
        keys_ref[layer, group] = keys
        values_ref[layer, group] = values
        scores = mm_nt(keys, queries) * 0.125
        exponent = jnp.where(causal, jnp.exp(scores), 0.0)
        first, second = head_sums(exponent)
        probs = jnp.concatenate([exponent[:128] * (1.0 / first), exponent[128:] * (1.0 / second)], axis=0).astype(BF16)
        probs_ref[layer, group] = probs
        mixed = mm_tn(probs, values).astype(BF16)
        at = group * 256
        for half in range(2):
            rows = slice(64 * half, 64 * half + 64)
            att_ref[rows, at : at + 128] = mixed[128 * half : 128 * half + 64]
            att_ref[rows, at + 128 : at + 256] = mixed[128 * half + 64 : 128 * half + 128]


def attention_backward(joined, d_attention, probs_ref, keys_ref, values_ref, dj_ref, carried, layer, half):
    rows = pl.ds(pl.multiple_of(64 * half, 64), 64)
    lanes = pl.ds(pl.multiple_of(128 * half, 128), 128)
    d_keys, d_values = [], []
    for group in range(4):
        queries = stack_pairs(joined, group)
        d_heads = stack_pairs(d_attention, group)
        probs = probs_ref[layer, group, :, lanes]
        d_probs = mm_nt(values_ref[layer, group], d_heads)
        wide = probs.astype(F32)
        first, second = head_sums(wide * d_probs)
        centred = jnp.concatenate([d_probs[:128] - first, d_probs[128:] - second], axis=0)
        d_scores = (wide * centred * 0.125).astype(BF16)
        d_keys.append(mm(d_scores, queries))
        d_values.append(mm(probs, d_heads))
        d_queries = mm_tn(d_scores, keys_ref[layer, group]).astype(BF16)
        lane = group * 256
        dj_ref[layer, rows, lane : lane + 128] = d_queries[:64]
        dj_ref[layer, rows, lane + 128 : lane + 256] = d_queries[64:]
    low = lax.broadcasted_iota(jnp.int32, (128, 128), 1) < 64

    def merged(even, odd):
        first = even[:128] + pltpu.roll(even[128:], 64, 1)
        second = pltpu.roll(odd[:128], 64, 1) + odd[128:]
        return jnp.where(low, first, second)

    for number, parts in ((0, d_keys), (1, d_values)):
        for pair in range(2):
            total = merged(parts[2 * pair], parts[2 * pair + 1])
            lane = D + 256 * number + 128 * pair
            ours = jnp.where(half == 1, total[64:], total[:64] + carried[layer, number, pair])
            dj_ref[layer, rows, lane : lane + 128] = ours.astype(BF16)
            carried[layer, number, pair] = total[:64]


def inverse_norm(wide):
    return lax.rsqrt(jnp.mean(wide * wide, axis=-1, keepdims=True) + EPSILON)


def kernel(
    inputs_ref, cotangent_ref, wq_ref, wo_ref,
    out_ref,
    wq, wo, wqt, wot, entry, passed, hidden, normed, joined, probs, keys, values, att, upstream, dj, carried, c_all, grads, grads_out,
    z_a1, z_b1, z_m2, z_p2, z_r, z_sa1, z_sb1, z_sm2, z_sp2,
    x_a1, x_b1, x_m2, x_p2, x_r, x_sa1, x_sb1, x_sm2, x_sp2,
    o_a1, o_b1, o_m2, o_p2,
    load_sem, flip_send, flip_recv, spread_send, spread_recv, core_send, core_recv,
    entry_send, entry_recv, hop_send, hop_recv, c_hop_send, c_hop_recv, share_send, share_recv,
    att_send, att_recv, att_core_send, att_core_recv, c_send, c_recv, sum_send, sum_recv,
):
    section, dp = lax.axis_index("section"), lax.axis_index("dp")
    y, x_hi = lax.div(section, 2), lax.rem(section, 2)
    z, x_lo, core = lax.div(dp, 4), lax.rem(lax.div(dp, 2), 2), lax.rem(dp, 2)
    x = 2 * x_hi + x_lo
    slot = 2 * z + core

    def place(y, x, z, core):
        return (2 * y + lax.div(x, 2), 4 * z + 2 * lax.rem(x, 2) + core)

    core_dev = place(y, x, z, 1 - core)
    xp_dev, xm_dev = place(y, lax.rem(x + 1, 4), z, core), place(y, lax.rem(x + 3, 4), z, core)
    zp_dev, zm_dev = place(y, x, lax.rem(z + 1, 4), core), place(y, x, lax.rem(z + 3, 4), core)
    yp_dev, ym_dev = place(lax.rem(y + 1, 4), x, z, core), place(lax.rem(y + 3, 4), x, z, core)
    column = [[place(y, x, lax.rem(z + k, 4), c) for c in (core, 1 - core)] for k in range(4)]
    flip_dev = place(y, 3 - x, z, core)
    side_dev = place(y, 2 * x_hi + 1 - x_lo, z, core)
    up_across_dev, down_across_dev = place(lax.rem(y + 1, 4), 3 - x, z, core), place(lax.rem(y + 3, 4), 3 - x, z, core)

    def remote(src, dst, send_sem, recv_sem, device):
        return pltpu.make_async_remote_copy(
            src_ref=src, dst_ref=dst, send_sem=send_sem, recv_sem=recv_sem, device_id=device, device_id_type=MESH
        )

    sent = []

    def go(copy):
        copy.start()
        sent.append(copy)

    loads = [
        pltpu.make_async_copy(wq_ref.at[0], wq.at[x_hi], load_sem.at[0]),
        pltpu.make_async_copy(wo_ref.at[0], wo.at[x_hi], load_sem.at[1]),
    ]
    load_in = pltpu.make_async_copy(inputs_ref.at[0, 0, 0], hidden.at[0], load_sem.at[2])
    load_cot = pltpu.make_async_copy(cotangent_ref.at[0, 0, 0], upstream.at[2], load_sem.at[3])
    load_entry = [pltpu.make_async_copy(inputs_ref.at[0, s, 0], entry.at[s], load_sem.at[4 + s]) for s in range(2)]
    for copy in loads:
        copy.start()

    near, far = x_hi == 0, x_hi == 1

    @pl.when((y == 0) & near)
    def _():
        load_entry[0].start()
        load_entry[1].start()
        load_in.start()

    @pl.when((y == 3) & near)
    def _():
        load_cot.start()

    barrier = pltpu.get_barrier_semaphore()
    ring = [column[k][c] for k in range(4) for c in range(2) if (k, c) != (0, 0)]
    for device in (*ring, xp_dev, xm_dev, yp_dev, ym_dev, up_across_dev, down_across_dev):
        pl.semaphore_signal(barrier, inc=1, device_id=device, device_id_type=MESH)
    pl.semaphore_wait(barrier, 13)

    in_hop = remote(inputs_ref.at[0, 1, 0], hidden.at[0], hop_send.at[2], hop_recv.at[2], side_dev)
    cot_hop = remote(cotangent_ref.at[0, 1, 0], upstream.at[2], hop_send.at[3], hop_recv.at[3], side_dev)

    @pl.when((y == 0) & far)
    def _():
        in_hop.start()

    @pl.when((y == 3) & far)
    def _():
        cot_hop.start()

    h_hop = remote(hidden.at[2], hidden.at[0], hop_send.at[0], hop_recv.at[0], yp_dev)
    def run_forward(h, weights, layer, turned=False):
        wide = h.astype(F32)
        inverse = inverse_norm(wide)
        normed[layer, 0:SEQ] = (wide * inverse).astype(BF16)
        joined[layer] = (mm(h, wq[weights]) * inverse).astype(BF16)
        attention_forward(joined[layer], probs, keys, values, att.at[layer, slot], layer)
        update = mm(att[layer, slot], wot[weights]) if turned else mm_nt(att[layer, slot], wo[weights])
        return (wide + update).astype(BF16)

    other = 1 - x_hi
    piece = lax.rem(z + 2 * x_lo, 4)
    pieces = [lax.rem(piece + k, 4) for k in range(4)]

    def chunk(buf, slot, which, half, part):
        name, k, rows = part
        at = (half * 4 + which) * 128 + k * rows
        return buf[name].at[slot, pl.ds(pl.multiple_of(at, rows), rows)]

    held, given = {"q": wq, "o": wo}, {"q": wq_ref, "o": wo_ref}

    def flip_copy(i, block, source=None):
        return remote(block if source is None else source, block, flip_send.at[i], flip_recv.at[i], flip_dev)

    flips = [
        flip_copy(i, chunk(held, x_hi, pieces[2], core, part), chunk(given, 0, pieces[2], core, part))
        for i, part in enumerate(PARTS)
    ]
    sent.extend(flips)

    @pl.when((y == 0) & far)
    def _():
        for copy in flips:
            copy.start()

    across = [remote(passed.at[s], entry.at[s], entry_send.at[s], entry_recv.at[s], flip_dev) for s in range(2)]
    onward = [
        remote(passed.at[0], hidden.at[0], entry_send.at[0], hop_recv.at[0], up_across_dev),
        remote(passed.at[1], hidden.at[0], entry_send.at[1], hop_recv.at[0], yp_dev),
    ]

    @pl.when(y == 0)
    def _():
        for copy in loads:
            copy.wait()

        def first_pass(s, carry):
            for k in range(2):
                @pl.when((s == k) & near)
                def _():
                    load_entry[k].wait()

                @pl.when((s == k) & far)
                def _():
                    across[k].wait_recv()

            passed[s] = run_forward(entry[s], x_hi, 0)
            for k in range(2):
                @pl.when((s == k) & near)
                def _():
                    across[k].start()

                @pl.when((s == k) & far)
                def _():
                    onward[k].start()

            return carry

        lax.fori_loop(0, 2, first_pass, 0)

        @pl.when(near)
        def _():
            for copy in across:
                copy.wait_send()

        @pl.when(far)
        def _():
            for copy in onward:
                copy.wait_send()

    @pl.when((y > 0) | near)
    def _():
        for copy in flips:
            copy.start()

    def spread(i, part):
        flip_copy(i, chunk(held, other, pieces[0], core, part)).wait_recv()
        block = chunk(held, other, pieces[0], core, part)
        for k, device in ((1, zm_dev), (2, side_dev), (3, zp_dev)):
            go(remote(block, block, spread_send.at[i, k], spread_recv.at[i, k], device))

    def core_copy(i, part, half):
        name, k, rows = part
        block = held[name].at[other].reshape(8, 128, held[name].shape[2])
        block = block.at[pl.ds(half * 4, 4), pl.ds(k * rows, rows)]
        return remote(block, block, core_send.at[i], core_recv.at[i], core_dev)

    def gather_rest(i, part):
        for k in (1, 2, 3):
            block = chunk(held, other, pieces[k], core, part)
            remote(block, block, spread_send.at[i, k], spread_recv.at[i, k], side_dev).wait_recv()
        go(core_copy(i, part, core))

    for i, part in enumerate(PARTS):
        spread(i, part)
        if i > 0:
            gather_rest(i - 1, PARTS[i - 1])
    gather_rest(len(PARTS) - 1, PARTS[-1])
    for i, part in enumerate(PARTS):
        core_copy(i, part, 1 - core).wait_recv()

    def transpose_weights():
        def one(k, carry):
            layer, cols = lax.div(k, 6), pl.ds(pl.multiple_of(lax.rem(k, 6) * 256, 256), 256)
            wqt[layer, cols] = wq[layer, :, cols].T
            return carry

        lax.fori_loop(0, 12, one, 0)

    @pl.when(y > 0)
    def _():
        for copy in loads:
            copy.wait()

    @pl.when(y >= 2)
    def _():
        def one(k, carry):
            layer, rows = lax.div(k, 4), pl.ds(pl.multiple_of(lax.rem(k, 4) * 256, 256), 256)
            wot[layer, :, rows] = wo[layer, rows].T
            return carry

        lax.fori_loop(0, 8, one, 0)
        transpose_weights()

    @pl.when((y == 0) & near)
    def _():
        load_in.wait()

    @pl.when((y == 0) & far)
    def _():
        in_hop.wait()

    @pl.when(y > 0)
    def _():
        h_hop.wait_recv()

    def forward(turned, layer, carry):
        hidden[layer + 1] = run_forward(hidden[layer], layer, layer, turned)
        return carry

    @pl.when(y < 2)
    def _():
        lax.fori_loop(0, 2, functools.partial(forward, False), 0)

    @pl.when(y >= 2)
    def _():
        lax.fori_loop(0, 2, functools.partial(forward, True), 0)

    @pl.when((y > 0) & (y < 3))
    def _():
        h_hop.start()

    def share(buf, layer, number):
        return remote(
            buf.at[layer, 0:SEQ], buf.at[layer, SEQ : 2 * SEQ], share_send.at[number], share_recv.at[number], core_dev
        )

    shares = [share(dj, 0, 0), share(dj, 1, 1)]
    share_normed = remote(
        normed.at[:, 0:SEQ], normed.at[:, SEQ : 2 * SEQ], share_send.at[2], share_recv.at[2], core_dev
    )
    sent.extend(shares)

    def att_block(k, half):
        return att.at[:, 2 * lax.rem(z + 4 - k, 4) + half]

    def att_copy(k):
        return remote(att_block(0, core), att_block(0, core), att_send.at[k], att_recv.at[k], column[k][0])

    def core_att(k):
        return remote(att_block(k, core), att_block(k, core), att_core_send.at[k], att_core_recv.at[k], core_dev)

    def send_attention():
        share_normed.start()
        for k in (1, 3, 2):
            att_copy(k).start()

    def pass_attention():
        core_att(0).start()
        for k in (1, 3, 2):
            remote(att_block(k, core), att_block(k, core), att_send.at[k], att_recv.at[k], core_dev).wait_recv()
            core_att(k).start()

    def await_attention():
        for k in range(4):
            block = att_block(k, 1 - core)
            remote(block, block, att_core_send.at[k], att_core_recv.at[k], core_dev).wait_recv()

    early = sent[: -len(shares)]
    del sent[: len(early)]

    def settle():
        for copy in early:
            copy.wait_send()
        share_normed.wait_send()
        for k in (1, 3, 2):
            att_copy(k).wait_send()
        for k in range(4):
            core_att(k).wait_send()

    def c_columns(layer, k):
        return upstream.at[layer + 1, :, pl.ds(pl.multiple_of(256 * lax.rem(z + k, 4), 256), 256)]

    def c_copy(layer, k):
        return remote(c_columns(layer, k), c_all.at[layer, z, core], c_send.at[layer, k], c_recv.at[layer, k], column[k][0])

    def core_c(layer, half):
        block = c_all.at[layer, :, half]
        return remote(block, block, c_send.at[layer, 0], c_recv.at[layer, 0], core_dev)

    def send_c(layer):
        for k in (1, 3, 2):
            c_copy(layer, k).start()

    def pass_c(layer):
        c_all[layer, z, core] = c_columns(layer, 0)[...]
        for k in (1, 3, 2):
            block = c_all.at[layer, lax.rem(z + 4 - k, 4), core]
            remote(block, block, c_send.at[layer, k], c_recv.at[layer, k], core_dev).wait_recv()
        core_c(layer, core).start()

    sent.extend(c_copy(layer, k) for layer in range(2) for k in (1, 3, 2))
    sent.extend(core_c(layer, core) for layer in range(2))

    send_attention()

    @pl.when(y < 2)
    def _():
        transpose_weights()
        pass_attention()
        await_attention()
        share_normed.wait_recv()
        settle()

    @pl.when((y == 3) & near)
    def _():
        load_cot.wait()

    @pl.when((y == 3) & far)
    def _():
        cot_hop.wait()

    def c_half(half):
        rows = pl.ds(pl.multiple_of(64 * half, 64), 64)
        return remote(upstream.at[0, rows], upstream.at[2, rows], c_hop_send.at[half], c_hop_recv.at[half], ym_dev)

    def backward(step, carry):
        half, layer = 1 - lax.div(step, 2), 1 - lax.rem(step, 2)
        rows = pl.ds(pl.multiple_of(64 * half, 64), 64)

        @pl.when((y < 3) & (layer == 1))
        def _():
            c_half(half).wait_recv()

        @pl.when((y == 0) & (half == 0))
        def _():
            send_c(layer)

        d_attention = mm(upstream[layer + 1, rows], wo[layer]).astype(BF16)
        attention_backward(joined[layer, rows], d_attention, probs, keys, values, dj, carried, layer, half)

        @pl.when(half == 0)
        def _():
            share(dj, layer, layer).start()

        @pl.when((layer > 0) | (y > 0))
        def _():
            d_normed = mm(dj[layer, rows], wqt[layer])
            wide = hidden[layer, rows].astype(F32)
            inverse = inverse_norm(wide)
            scaled = wide * inverse
            along = jnp.mean(d_normed * scaled, axis=-1, keepdims=True)
            upstream[layer, rows] = (
                upstream[layer + 1, rows].astype(F32) + inverse * (d_normed - scaled * along)
            ).astype(BF16)

        @pl.when((y > 0) & (layer == 0))
        def _():
            c_half(half).start()

        return carry

    lax.fori_loop(0, 4, backward, 0)

    @pl.when(y > 0)
    def _():
        send_c(1)
        send_c(0)

    @pl.when(y >= 2)
    def _():
        share_normed.wait_recv()

    low = lax.broadcasted_iota(jnp.int32, (2 * SEQ, 128), 1) < 64

    def own_columns(block):
        def tile(k):
            return block[:, 128 * k : 128 * k + 128].astype(F32)

        tiles = []
        for lo in range(2):
            for pair in range(2):
                a, b = tile(4 * pair + lo), tile(4 * pair + 2 + lo)
                first = jnp.where(core == 0, a, pltpu.roll(a, 64, 1))
                second = jnp.where(core == 0, pltpu.roll(b, 64, 1), b)
                tiles.append(jnp.where(low, first, second).astype(BF16))
        return jnp.concatenate(tiles, axis=1)

    def gradient(layer):
        left = own_columns(normed[layer])
        for lo in range(2):
            part = mm_tn(left[:, 256 * lo : 256 * lo + 256], dj[layer]).astype(BF16)
            grads[2 * layer + lo] = part.reshape(4, 64, QKV)

    def gradient_out(layer):
        core_c(layer, 1 - core).wait_recv()
        a = c_all[layer, :, :, :, 0:128].reshape(8 * SEQ, 128).astype(F32)
        b = c_all[layer, :, :, :, 128:256].reshape(8 * SEQ, 128).astype(F32)
        first = jnp.where(core == 0, a, pltpu.roll(a, 64, 1))
        second = jnp.where(core == 0, pltpu.roll(b, 64, 1), b)
        left = jnp.where(lax.broadcasted_iota(jnp.int32, a.shape, 1) < 64, first, second).astype(BF16)
        part = mm_tn(left, att[layer].reshape(8 * SEQ, D)).astype(BF16)
        grads_out[2 * layer : 2 * layer + 2] = part.reshape(2, 64, D)

    def ring_sum(view, position, plus, minus, bufs, sems, layers=None):
        a1, b1, m2, p2, alpha, beta = bufs
        opposite, after, before = (lax.rem(position + k, 4) for k in (2, 1, 3))
        s, r = sum_send.at, sum_recv.at
        copies = [
            remote(view(opposite, 0), a1, s[sems], r[sems], plus),
            remote(view(opposite, 1), b1, s[sems + 1], r[sems + 1], minus),
            remote(view(after, 1), m2.at[beta], s[sems + 2], r[sems + 2], plus),
            remote(view(before, 0), p2.at[alpha], s[sems + 3], r[sems + 3], minus),
            remote(view(after, 0), m2.at[alpha], s[sems + 4], r[sems + 4], plus),
            remote(view(before, 1), p2.at[beta], s[sems + 5], r[sems + 5], minus),
        ]
        sent.extend(copies)

        def only(stage, target):
            if stage is None:
                return lambda body: body()
            return pl.when(layers(target) == stage)

        def first(stage=None):
            @only(stage, opposite)
            def _():
                copies[0].start()
                copies[1].start()

            @only(stage, after)
            def _():
                copies[2].start()

            @only(stage, before)
            def _():
                copies[3].start()

        def second(stage=None):
            @only(stage, after)
            def _():
                mine = view(after, 0)
                copies[0].wait_recv()
                mine[...] = (mine[...].astype(F32) + a1[...].astype(F32)).astype(BF16)
                copies[4].start()

            @only(stage, before)
            def _():
                mine = view(before, 1)
                copies[1].wait_recv()
                mine[...] = (mine[...].astype(F32) + b1[...].astype(F32)).astype(BF16)
                copies[5].start()

        def last():
            for copy in copies[2:]:
                copy.wait_recv()

        return first, second, last

    def cut(offset, widths):
        return [pl.ds(offset, widths[0]), pl.ds(offset + widths[0], widths[1])]

    z_cols, x_cols, z_own, x_own = cut(0, Z_CUT), cut(HALF, X_CUT), cut(0, Z_CUT), cut(0, X_CUT)

    def wide_at(own):
        return [(slice(None), slice(None), cols) for cols in own]

    def flat_at(own):
        return [(slice(None), cols) for cols in own]

    def z_ring(layer):
        pair = pl.ds(2 * layer, 2)
        bufs = (z_a1.at[pair], z_b1.at[pair], z_m2.at[pair], z_p2.at[pair], *wide_at(z_own))
        return ring_sum(lambda t, k: grads.at[pair, t, :, z_cols[k]], z, zp_dev, zm_dev, bufs, 24 if layer else 0)

    z_big = [z_ring(0), z_ring(1)]
    def layer_of(target):
        return lax.div(target, 2)

    x_big = ring_sum(
        lambda t, k: grads.at[t, :, :, x_cols[k]], x, xp_dev, xm_dev, (x_a1, x_b1, x_m2, x_p2, *wide_at(x_own)), 6, layer_of
    )
    z_small = ring_sum(
        lambda t, k: z_r.at[t, :, z_own[k]], x, xp_dev, xm_dev, (z_sa1, z_sb1, z_sm2, z_sp2, *flat_at(z_own)), 12, layer_of
    )
    x_small = ring_sum(
        lambda t, k: x_r.at[t, :, x_own[k]], z, zp_dev, zm_dev, (x_sa1, x_sb1, x_sm2, x_sp2, *flat_at(x_own)), 18
    )
    out_at = [(slice(None), pl.ds(0, WIDE)), (slice(None), pl.ds(WIDE, WIDE))]
    o_ring = ring_sum(
        lambda t, k: grads_out.at[t, :, pl.ds(k * WIDE, WIDE)], x, xp_dev, xm_dev, (o_a1, o_b1, o_m2, o_p2, *out_at), 30
    )

    def sum_z(layer):
        pair = slice(2 * layer, 2 * layer + 2)
        z_r[pair] = (grads[pair, z, :, 0:HALF].astype(F32) + z_m2[pair].astype(F32) + z_p2[pair].astype(F32)).astype(BF16)

    shares[1].wait_recv()
    gradient(1)
    z_big[1][0]()
    x_big[0](1)
    shares[0].wait_recv()
    gradient(0)
    z_big[0][0]()
    x_big[0](0)

    @pl.when(y >= 2)
    def _():
        pass_attention()
        await_attention()

    pass_c(1)
    pass_c(0)
    gradient_out(1)
    gradient_out(0)
    o_ring[0]()
    z_big[1][1]()
    x_big[1](1)
    z_big[0][1]()
    x_big[1](0)
    z_big[1][2]()
    sum_z(1)
    z_small[0](1)
    o_ring[1]()
    z_big[0][2]()
    sum_z(0)
    z_small[0](0)
    x_big[2]()
    x_r[...] = (grads[x, :, :, HALF:QKV].astype(F32) + x_m2[...].astype(F32) + x_p2[...].astype(F32)).astype(BF16)
    x_small[0]()
    z_small[1](1)
    z_small[1](0)
    x_small[1]()
    o_ring[2]()
    out_ref[:, QKV:COLS] = grads_out[x].astype(F32) + o_m2[...].astype(F32) + o_p2[...].astype(F32)
    z_small[2]()
    out_ref[:, 0:HALF] = z_r[x].astype(F32) + z_sm2[...].astype(F32) + z_sp2[...].astype(F32)
    x_small[2]()
    out_ref[:, HALF:QKV] = x_r[z].astype(F32) + x_sm2[...].astype(F32) + x_sp2[...].astype(F32)

    @pl.when(y >= 2)
    def _():
        settle()

    for copy in sent:
        copy.wait_send()

    @pl.when((y > 0) & (y < 3))
    def _():
        h_hop.wait_send()

    @pl.when(y > 0)
    def _():
        c_half(0).wait_send()
        c_half(1).wait_send()


def split_columns(total_ref, gq_ref, go_ref):
    gq_ref[0] = total_ref[:, :QKV]
    go_ref[0] = total_ref[:, QKV:]


def on_device(inputs, cotangent, w_qkv, w_out):
    any_space = pl.BlockSpec(memory_space=pl.ANY)
    vmem = pl.BlockSpec(memory_space=pltpu.VMEM)
    dma = pltpu.SemaphoreType.DMA

    def flow(widths):
        first, second = widths
        both = first + second
        return [
            pltpu.VMEM((4, 64, first), BF16),
            pltpu.VMEM((4, 64, second), BF16),
            pltpu.VMEM((4, 64, both), BF16),
            pltpu.VMEM((4, 64, both), BF16),
            pltpu.VMEM((4, 64, both), BF16),
            pltpu.VMEM((64, first), BF16),
            pltpu.VMEM((64, second), BF16),
            pltpu.VMEM((64, both), BF16),
            pltpu.VMEM((64, both), BF16),
        ]

    total = pl.pallas_call(
        kernel,
        out_shape=jax.ShapeDtypeStruct((64, COLS), F32),
        in_specs=[any_space] * 4,
        out_specs=vmem,
        scratch_shapes=[
            pltpu.VMEM((2, D, QKV), BF16),
            pltpu.VMEM((2, D, D), BF16),
            pltpu.VMEM((2, QKV, D), BF16),
            pltpu.VMEM((2, D, D), BF16),
            pltpu.VMEM((2, SEQ, D), BF16),
            pltpu.VMEM((2, SEQ, D), BF16),
            pltpu.VMEM((3, SEQ, D), BF16),
            pltpu.VMEM((2, 2 * SEQ, D), BF16),
            pltpu.VMEM((2, SEQ, QKV), BF16),
            pltpu.VMEM((2, 4, 256, 256), BF16),
            pltpu.VMEM((2, 4, 256, 128), BF16),
            pltpu.VMEM((2, 4, 256, 128), BF16),
            pltpu.VMEM((2, 8, SEQ, D), BF16),
            pltpu.VMEM((3, SEQ, D), BF16),
            pltpu.VMEM((2, 2 * SEQ, QKV), BF16),
            pltpu.VMEM((2, 2, 2, 64, 128), F32),
            pltpu.VMEM((2, 4, 2, SEQ, 256), BF16),
            pltpu.VMEM((4, 4, 64, QKV), BF16),
            pltpu.VMEM((4, 64, D), BF16),
            *flow(Z_CUT),
            *flow(X_CUT),
            pltpu.VMEM((64, WIDE), BF16),
            pltpu.VMEM((64, WIDE), BF16),
            pltpu.VMEM((64, D), BF16),
            pltpu.VMEM((64, D), BF16),
            dma((6,)),
            dma((len(PARTS),)),
            dma((len(PARTS),)),
            dma((len(PARTS), 4)),
            dma((len(PARTS), 4)),
            dma((len(PARTS),)),
            dma((len(PARTS),)),
            dma((2,)),
            dma((2,)),
            dma((4,)),
            dma((4,)),
            dma((2,)),
            dma((2,)),
            dma((4,)),
            dma((4,)),
            dma((4,)),
            dma((4,)),
            dma((4,)),
            dma((4,)),
            dma((2, 4)),
            dma((2, 4)),
            dma((36,)),
            dma((36,)),
        ],
        compiler_params=pltpu.CompilerParams(
            collective_id=0, has_side_effects=True, vmem_limit_bytes=56 * 2**20
        ),
    )(inputs, cotangent, w_qkv, w_out)
    return pl.pallas_call(
        split_columns,
        out_shape=(jax.ShapeDtypeStruct((1, 64, QKV), F32), jax.ShapeDtypeStruct((1, 64, D), F32)),
    )(total)


def solution(mesh):
    placed = (
        P("dp", None, None, None, None),
        P("dp", None, None, None, None),
        P("section", None, None),
        P("section", None, None),
    )
    return jax.shard_map(
        on_device,
        mesh=mesh,
        in_specs=placed,
        out_specs=(P("section", "dp", None), P("section", "dp", None)),
        check_vma=False,
    )
```

```python
import functools

import jax
import jax.numpy as jnp
from jax import lax
from jax.experimental import pallas as pl
from jax.experimental.pallas import tpu as pltpu
from jax.sharding import PartitionSpec as P

MESH = pl.DeviceIdType.MESH
F32 = jnp.float32
BF16 = jnp.bfloat16
EPSILON = 1e-05

D = 1024
SEQ = 128
QKV = 1536
COLS = 2560
Z_CUT = (512, 384)
X_CUT = (256, 384)
HALF = sum(Z_CUT)
WIDE = 512
PARTS = [("q", k, 32) for k in range(4)] + [("o", k, 64) for k in range(2)]


def mm(a, b):
    return jnp.dot(a, b, preferred_element_type=F32)


def mm_nt(a, b):
    return lax.dot_general(a, b, (((1,), (1,)), ((), ())), preferred_element_type=F32)


def mm_tn(a, b):
    return lax.dot_general(a, b, (((0,), (0,)), ((), ())), preferred_element_type=F32)


def block_diagonal(pair, group):
    low = lax.broadcasted_iota(jnp.int32, pair.shape, 1) < 64
    wide = pair.astype(F32)
    rolled = pltpu.roll(wide, 64, 1)
    first, second = (wide, rolled) if group % 2 == 0 else (rolled, wide)
    zero = jnp.zeros_like(wide)
    return jnp.concatenate([jnp.where(low, first, zero), jnp.where(low, zero, second)], axis=0).astype(BF16)


def stack_pairs(x, group):
    at = group * 256
    blocks = []
    for start in range(0, x.shape[0], 64):
        blocks += [x[start : start + 64, at : at + 128], x[start : start + 64, at + 128 : at + 256]]
    return jnp.concatenate(blocks, axis=0)


def head_sums(x):
    return (jnp.sum(x[:128], axis=0, keepdims=True), jnp.sum(x[128:], axis=0, keepdims=True))


def kv_pairs(joined, group):
    at = (group // 2) * 128
    return joined[:, D + at : D + at + 128], joined[:, D + 256 + at : D + 256 + at + 128]


def attention_forward(joined, probs_ref, keys_ref, values_ref, att_ref, layer):
    key = lax.broadcasted_iota(jnp.int32, (256, 256), 0) & 127
    column = lax.broadcasted_iota(jnp.int32, (256, 256), 1)
    causal = key <= (column & 63) + 64 * lax.shift_right_logical(column, 7)
    for group in range(4):
        queries = stack_pairs(joined, group)
        keys, values = (block_diagonal(pair, group) for pair in kv_pairs(joined, group))
        keys_ref[layer, group] = keys
        values_ref[layer, group] = values
        scores = mm_nt(keys, queries) * 0.125
        exponent = jnp.where(causal, jnp.exp(scores), 0.0)
        first, second = head_sums(exponent)
        probs = jnp.concatenate([exponent[:128] * (1.0 / first), exponent[128:] * (1.0 / second)], axis=0).astype(BF16)
        probs_ref[layer, group] = probs
        mixed = mm_tn(probs, values).astype(BF16)
        at = group * 256
        for half in range(2):
            rows = slice(64 * half, 64 * half + 64)
            att_ref[rows, at : at + 128] = mixed[128 * half : 128 * half + 64]
            att_ref[rows, at + 128 : at + 256] = mixed[128 * half + 64 : 128 * half + 128]


def attention_backward(joined, d_attention, probs_ref, keys_ref, values_ref, dj_ref, carried, layer, half):
    rows = pl.ds(pl.multiple_of(64 * half, 64), 64)
    lanes = pl.ds(pl.multiple_of(128 * half, 128), 128)
    d_keys, d_values = [], []
    for group in range(4):
        queries = stack_pairs(joined, group)
        d_heads = stack_pairs(d_attention, group)
        probs = probs_ref[layer, group, :, lanes]
        d_probs = mm_nt(values_ref[layer, group], d_heads)
        wide = probs.astype(F32)
        first, second = head_sums(wide * d_probs)
        centred = jnp.concatenate([d_probs[:128] - first, d_probs[128:] - second], axis=0)
        d_scores = (wide * centred * 0.125).astype(BF16)
        d_keys.append(mm(d_scores, queries))
        d_values.append(mm(probs, d_heads))
        d_queries = mm_tn(d_scores, keys_ref[layer, group]).astype(BF16)
        lane = group * 256
        dj_ref[layer, rows, lane : lane + 128] = d_queries[:64]
        dj_ref[layer, rows, lane + 128 : lane + 256] = d_queries[64:]
    low = lax.broadcasted_iota(jnp.int32, (128, 128), 1) < 64

    def merged(even, odd):
        first = even[:128] + pltpu.roll(even[128:], 64, 1)
        second = pltpu.roll(odd[:128], 64, 1) + odd[128:]
        return jnp.where(low, first, second)

    for number, parts in ((0, d_keys), (1, d_values)):
        for pair in range(2):
            total = merged(parts[2 * pair], parts[2 * pair + 1])
            lane = D + 256 * number + 128 * pair
            ours = jnp.where(half == 1, total[64:], total[:64] + carried[layer, number, pair])
            dj_ref[layer, rows, lane : lane + 128] = ours.astype(BF16)
            carried[layer, number, pair] = total[:64]


def inverse_norm(wide):
    return lax.rsqrt(jnp.mean(wide * wide, axis=-1, keepdims=True) + EPSILON)


def kernel(
    inputs_ref, cotangent_ref, wq_ref, wo_ref,
    out_ref,
    wq, wo, wqt, wot, entry, passed, hidden, normed, joined, probs, keys, values, att, upstream, dj, carried, c_all, grads, grads_out,
    z_a1, z_b1, z_m2, z_p2, z_r, z_sa1, z_sb1, z_sm2, z_sp2,
    x_a1, x_b1, x_m2, x_p2, x_r, x_sa1, x_sb1, x_sm2, x_sp2,
    o_a1, o_b1, o_m2, o_p2,
    load_sem, flip_send, flip_recv, spread_send, spread_recv, core_send, core_recv,
    entry_send, entry_recv, hop_send, hop_recv, c_hop_send, c_hop_recv, share_send, share_recv,
    att_send, att_recv, att_core_send, att_core_recv, c_send, c_recv, sum_send, sum_recv,
):
    section, dp = lax.axis_index("section"), lax.axis_index("dp")
    y, x_hi = lax.div(section, 2), lax.rem(section, 2)
    z, x_lo, core = lax.div(dp, 4), lax.rem(lax.div(dp, 2), 2), lax.rem(dp, 2)
    x = 2 * x_hi + x_lo
    slot = 2 * z + core

    def place(y, x, z, core):
        return (2 * y + lax.div(x, 2), 4 * z + 2 * lax.rem(x, 2) + core)

    core_dev = place(y, x, z, 1 - core)
    xp_dev, xm_dev = place(y, lax.rem(x + 1, 4), z, core), place(y, lax.rem(x + 3, 4), z, core)
    zp_dev, zm_dev = place(y, x, lax.rem(z + 1, 4), core), place(y, x, lax.rem(z + 3, 4), core)
    yp_dev, ym_dev = place(lax.rem(y + 1, 4), x, z, core), place(lax.rem(y + 3, 4), x, z, core)
    column = [[place(y, x, lax.rem(z + k, 4), c) for c in (core, 1 - core)] for k in range(4)]
    flip_dev = place(y, 3 - x, z, core)
    side_dev = place(y, 2 * x_hi + 1 - x_lo, z, core)
    up_across_dev, down_across_dev = place(lax.rem(y + 1, 4), 3 - x, z, core), place(lax.rem(y + 3, 4), 3 - x, z, core)

    def remote(src, dst, send_sem, recv_sem, device):
        return pltpu.make_async_remote_copy(
            src_ref=src, dst_ref=dst, send_sem=send_sem, recv_sem=recv_sem, device_id=device, device_id_type=MESH
        )

    sent = []

    def go(copy):
        copy.start()
        sent.append(copy)

    loads = [
        pltpu.make_async_copy(wq_ref.at[0], wq.at[x_hi], load_sem.at[0]),
        pltpu.make_async_copy(wo_ref.at[0], wo.at[x_hi], load_sem.at[1]),
    ]
    load_in = pltpu.make_async_copy(inputs_ref.at[0, 0, 0], hidden.at[0], load_sem.at[2])
    load_cot = pltpu.make_async_copy(cotangent_ref.at[0, 0, 0], upstream.at[2], load_sem.at[3])
    load_entry = [pltpu.make_async_copy(inputs_ref.at[0, s, 0], entry.at[s], load_sem.at[4 + s]) for s in range(2)]
    for copy in loads:
        copy.start()

    near, far = x_hi == 0, x_hi == 1

    @pl.when((y == 0) & near)
    def _():
        load_entry[0].start()
        load_entry[1].start()
        load_in.start()

    @pl.when((y == 3) & near)
    def _():
        load_cot.start()

    barrier = pltpu.get_barrier_semaphore()
    for device in (core_dev, xp_dev, xm_dev, zp_dev, zm_dev, yp_dev, ym_dev):
        pl.semaphore_signal(barrier, inc=1, device_id=device, device_id_type=MESH)
    pl.semaphore_wait(barrier, 7)

    in_hop = remote(inputs_ref.at[0, 1, 0], hidden.at[0], hop_send.at[2], hop_recv.at[2], side_dev)
    cot_hop = remote(cotangent_ref.at[0, 1, 0], upstream.at[2], hop_send.at[3], hop_recv.at[3], side_dev)

    @pl.when((y == 0) & far)
    def _():
        in_hop.start()

    @pl.when((y == 3) & far)
    def _():
        cot_hop.start()

    h_hop = remote(hidden.at[2], hidden.at[0], hop_send.at[0], hop_recv.at[0], yp_dev)
    def run_forward(h, weights, layer, turned=False):
        wide = h.astype(F32)
        inverse = inverse_norm(wide)
        normed[layer, 0:SEQ] = (wide * inverse).astype(BF16)
        joined[layer] = (mm(h, wq[weights]) * inverse).astype(BF16)
        attention_forward(joined[layer], probs, keys, values, att.at[layer, slot], layer)
        update = mm(att[layer, slot], wot[weights]) if turned else mm_nt(att[layer, slot], wo[weights])
        return (wide + update).astype(BF16)

    other = 1 - x_hi
    piece = lax.rem(z + 2 * x_lo, 4)
    pieces = [lax.rem(piece + k, 4) for k in range(4)]

    def chunk(buf, slot, which, half, part):
        name, k, rows = part
        at = (half * 4 + which) * 128 + k * rows
        return buf[name].at[slot, pl.ds(pl.multiple_of(at, rows), rows)]

    held, given = {"q": wq, "o": wo}, {"q": wq_ref, "o": wo_ref}

    def flip_copy(i, block, source=None):
        return remote(block if source is None else source, block, flip_send.at[i], flip_recv.at[i], flip_dev)

    flips = [
        flip_copy(i, chunk(held, x_hi, pieces[2], core, part), chunk(given, 0, pieces[2], core, part))
        for i, part in enumerate(PARTS)
    ]
    sent.extend(flips)

    @pl.when((y == 0) & far)
    def _():
        for copy in flips:
            copy.start()

    across = [remote(passed.at[s], entry.at[s], entry_send.at[s], entry_recv.at[s], flip_dev) for s in range(2)]
    onward = [
        remote(passed.at[0], hidden.at[0], entry_send.at[0], hop_recv.at[0], up_across_dev),
        remote(passed.at[1], hidden.at[0], entry_send.at[1], hop_recv.at[0], yp_dev),
    ]

    @pl.when(y == 0)
    def _():
        for copy in loads:
            copy.wait()

        def first_pass(s, carry):
            for k in range(2):
                @pl.when((s == k) & near)
                def _():
                    load_entry[k].wait()

                @pl.when((s == k) & far)
                def _():
                    across[k].wait_recv()

            passed[s] = run_forward(entry[s], x_hi, 0)
            for k in range(2):
                @pl.when((s == k) & near)
                def _():
                    across[k].start()

                @pl.when((s == k) & far)
                def _():
                    onward[k].start()

            return carry

        lax.fori_loop(0, 2, first_pass, 0)

        @pl.when(near)
        def _():
            for copy in across:
                copy.wait_send()

        @pl.when(far)
        def _():
            for copy in onward:
                copy.wait_send()

    @pl.when((y > 0) | near)
    def _():
        for copy in flips:
            copy.start()

    def spread(i, part):
        flip_copy(i, chunk(held, other, pieces[0], core, part)).wait_recv()
        block = chunk(held, other, pieces[0], core, part)
        for k, device in ((1, zm_dev), (2, side_dev), (3, zp_dev)):
            go(remote(block, block, spread_send.at[i, k], spread_recv.at[i, k], device))

    def core_copy(i, part, half):
        name, k, rows = part
        block = held[name].at[other].reshape(8, 128, held[name].shape[2])
        block = block.at[pl.ds(half * 4, 4), pl.ds(k * rows, rows)]
        return remote(block, block, core_send.at[i], core_recv.at[i], core_dev)

    def gather_rest(i, part):
        for k in (1, 2, 3):
            block = chunk(held, other, pieces[k], core, part)
            remote(block, block, spread_send.at[i, k], spread_recv.at[i, k], side_dev).wait_recv()
        go(core_copy(i, part, core))

    for i, part in enumerate(PARTS):
        spread(i, part)
        if i > 0:
            gather_rest(i - 1, PARTS[i - 1])
    gather_rest(len(PARTS) - 1, PARTS[-1])
    for i, part in enumerate(PARTS):
        core_copy(i, part, 1 - core).wait_recv()

    def transpose_weights():
        def one(k, carry):
            layer, cols = lax.div(k, 6), pl.ds(pl.multiple_of(lax.rem(k, 6) * 256, 256), 256)
            wqt[layer, cols] = wq[layer, :, cols].T
            return carry

        lax.fori_loop(0, 12, one, 0)

    @pl.when(y > 0)
    def _():
        for copy in loads:
            copy.wait()

    @pl.when(y >= 2)
    def _():
        def one(k, carry):
            layer, rows = lax.div(k, 4), pl.ds(pl.multiple_of(lax.rem(k, 4) * 256, 256), 256)
            wot[layer, :, rows] = wo[layer, rows].T
            return carry

        lax.fori_loop(0, 8, one, 0)
        transpose_weights()

    @pl.when((y == 0) & near)
    def _():
        load_in.wait()

    @pl.when((y == 0) & far)
    def _():
        in_hop.wait()

    @pl.when(y > 0)
    def _():
        h_hop.wait_recv()

    def forward(turned, layer, carry):
        hidden[layer + 1] = run_forward(hidden[layer], layer, layer, turned)
        return carry

    @pl.when(y < 2)
    def _():
        lax.fori_loop(0, 2, functools.partial(forward, False), 0)

    @pl.when(y >= 2)
    def _():
        lax.fori_loop(0, 2, functools.partial(forward, True), 0)

    @pl.when((y > 0) & (y < 3))
    def _():
        h_hop.start()

    def share(buf, layer, number):
        return remote(
            buf.at[layer, 0:SEQ], buf.at[layer, SEQ : 2 * SEQ], share_send.at[number], share_recv.at[number], core_dev
        )

    shares = [share(dj, 0, 0), share(dj, 1, 1)]
    share_normed = remote(
        normed.at[:, 0:SEQ], normed.at[:, SEQ : 2 * SEQ], share_send.at[2], share_recv.at[2], core_dev
    )
    sent.extend(shares)

    def att_block(k, half):
        return att.at[:, 2 * lax.rem(z + 4 - k, 4) + half]

    def att_copy(k):
        return remote(att_block(0, core), att_block(0, core), att_send.at[k], att_recv.at[k], column[k][0])

    def core_att(k):
        return remote(att_block(k, core), att_block(k, core), att_core_send.at[k], att_core_recv.at[k], core_dev)

    def send_attention():
        share_normed.start()
        for k in (1, 3, 2):
            att_copy(k).start()

    def pass_attention():
        core_att(0).start()
        for k in (1, 3, 2):
            remote(att_block(k, core), att_block(k, core), att_send.at[k], att_recv.at[k], core_dev).wait_recv()
            core_att(k).start()

    def await_attention():
        for k in range(4):
            block = att_block(k, 1 - core)
            remote(block, block, att_core_send.at[k], att_core_recv.at[k], core_dev).wait_recv()

    early = sent[: -len(shares)]
    del sent[: len(early)]

    def settle():
        for copy in early:
            copy.wait_send()
        share_normed.wait_send()
        for k in (1, 3, 2):
            att_copy(k).wait_send()
        for k in range(4):
            core_att(k).wait_send()

    def c_columns(layer, k):
        return upstream.at[layer + 1, :, pl.ds(pl.multiple_of(256 * lax.rem(z + k, 4), 256), 256)]

    def c_copy(layer, k):
        return remote(c_columns(layer, k), c_all.at[layer, z, core], c_send.at[layer, k], c_recv.at[layer, k], column[k][0])

    def core_c(layer, half):
        block = c_all.at[layer, :, half]
        return remote(block, block, c_send.at[layer, 0], c_recv.at[layer, 0], core_dev)

    def send_c(layer):
        for k in (1, 3, 2):
            c_copy(layer, k).start()

    def pass_c(layer):
        c_all[layer, z, core] = c_columns(layer, 0)[...]
        for k in (1, 3, 2):
            block = c_all.at[layer, lax.rem(z + 4 - k, 4), core]
            remote(block, block, c_send.at[layer, k], c_recv.at[layer, k], core_dev).wait_recv()
        core_c(layer, core).start()

    sent.extend(c_copy(layer, k) for layer in range(2) for k in (1, 3, 2))
    sent.extend(core_c(layer, core) for layer in range(2))

    send_attention()

    @pl.when(y < 2)
    def _():
        transpose_weights()
        pass_attention()
        await_attention()
        share_normed.wait_recv()
        settle()

    @pl.when((y == 3) & near)
    def _():
        load_cot.wait()

    @pl.when((y == 3) & far)
    def _():
        cot_hop.wait()

    def c_half(half):
        rows = pl.ds(pl.multiple_of(64 * half, 64), 64)
        return remote(upstream.at[0, rows], upstream.at[2, rows], c_hop_send.at[half], c_hop_recv.at[half], ym_dev)

    def backward(step, carry):
        half, layer = 1 - lax.div(step, 2), 1 - lax.rem(step, 2)
        rows = pl.ds(pl.multiple_of(64 * half, 64), 64)

        @pl.when((y < 3) & (layer == 1))
        def _():
            c_half(half).wait_recv()

        @pl.when((y == 0) & (half == 0))
        def _():
            send_c(layer)

        d_attention = mm(upstream[layer + 1, rows], wo[layer]).astype(BF16)
        attention_backward(joined[layer, rows], d_attention, probs, keys, values, dj, carried, layer, half)

        @pl.when(half == 0)
        def _():
            share(dj, layer, layer).start()

        @pl.when((layer > 0) | (y > 0))
        def _():
            d_normed = mm(dj[layer, rows], wqt[layer])
            wide = hidden[layer, rows].astype(F32)
            inverse = inverse_norm(wide)
            scaled = wide * inverse
            along = jnp.mean(d_normed * scaled, axis=-1, keepdims=True)
            upstream[layer, rows] = (
                upstream[layer + 1, rows].astype(F32) + inverse * (d_normed - scaled * along)
            ).astype(BF16)

        @pl.when((y > 0) & (layer == 0))
        def _():
            c_half(half).start()

        return carry

    lax.fori_loop(0, 4, backward, 0)

    @pl.when(y > 0)
    def _():
        send_c(1)
        send_c(0)

    @pl.when(y >= 2)
    def _():
        share_normed.wait_recv()

    low = lax.broadcasted_iota(jnp.int32, (2 * SEQ, 128), 1) < 64

    def own_columns(block):
        def tile(k):
            return block[:, 128 * k : 128 * k + 128].astype(F32)

        tiles = []
        for lo in range(2):
            for pair in range(2):
                a, b = tile(4 * pair + lo), tile(4 * pair + 2 + lo)
                first = jnp.where(core == 0, a, pltpu.roll(a, 64, 1))
                second = jnp.where(core == 0, pltpu.roll(b, 64, 1), b)
                tiles.append(jnp.where(low, first, second).astype(BF16))
        return jnp.concatenate(tiles, axis=1)

    def gradient(layer):
        left = own_columns(normed[layer])
        for lo in range(2):
            part = mm_tn(left[:, 256 * lo : 256 * lo + 256], dj[layer]).astype(BF16)
            grads[2 * layer + lo] = part.reshape(4, 64, QKV)

    def gradient_out(layer):
        core_c(layer, 1 - core).wait_recv()
        a = c_all[layer, :, :, :, 0:128].reshape(8 * SEQ, 128).astype(F32)
        b = c_all[layer, :, :, :, 128:256].reshape(8 * SEQ, 128).astype(F32)
        first = jnp.where(core == 0, a, pltpu.roll(a, 64, 1))
        second = jnp.where(core == 0, pltpu.roll(b, 64, 1), b)
        left = jnp.where(lax.broadcasted_iota(jnp.int32, a.shape, 1) < 64, first, second).astype(BF16)
        part = mm_tn(left, att[layer].reshape(8 * SEQ, D)).astype(BF16)
        grads_out[2 * layer : 2 * layer + 2] = part.reshape(2, 64, D)

    def ring_sum(view, position, plus, minus, bufs, sems, layers=None):
        a1, b1, m2, p2, alpha, beta = bufs
        opposite, after, before = (lax.rem(position + k, 4) for k in (2, 1, 3))
        s, r = sum_send.at, sum_recv.at
        copies = [
            remote(view(opposite, 0), a1, s[sems], r[sems], plus),
            remote(view(opposite, 1), b1, s[sems + 1], r[sems + 1], minus),
            remote(view(after, 1), m2.at[beta], s[sems + 2], r[sems + 2], plus),
            remote(view(before, 0), p2.at[alpha], s[sems + 3], r[sems + 3], minus),
            remote(view(after, 0), m2.at[alpha], s[sems + 4], r[sems + 4], plus),
            remote(view(before, 1), p2.at[beta], s[sems + 5], r[sems + 5], minus),
        ]
        sent.extend(copies)

        def only(stage, target):
            if stage is None:
                return lambda body: body()
            return pl.when(layers(target) == stage)

        def first(stage=None):
            @only(stage, opposite)
            def _():
                copies[0].start()
                copies[1].start()

            @only(stage, after)
            def _():
                copies[2].start()

            @only(stage, before)
            def _():
                copies[3].start()

        def second(stage=None):
            @only(stage, after)
            def _():
                mine = view(after, 0)
                copies[0].wait_recv()
                mine[...] = (mine[...].astype(F32) + a1[...].astype(F32)).astype(BF16)
                copies[4].start()

            @only(stage, before)
            def _():
                mine = view(before, 1)
                copies[1].wait_recv()
                mine[...] = (mine[...].astype(F32) + b1[...].astype(F32)).astype(BF16)
                copies[5].start()

        def last():
            for copy in copies[2:]:
                copy.wait_recv()

        return first, second, last

    def cut(offset, widths):
        return [pl.ds(offset, widths[0]), pl.ds(offset + widths[0], widths[1])]

    z_cols, x_cols, z_own, x_own = cut(0, Z_CUT), cut(HALF, X_CUT), cut(0, Z_CUT), cut(0, X_CUT)

    def wide_at(own):
        return [(slice(None), slice(None), cols) for cols in own]

    def flat_at(own):
        return [(slice(None), cols) for cols in own]

    def z_ring(layer):
        pair = pl.ds(2 * layer, 2)
        bufs = (z_a1.at[pair], z_b1.at[pair], z_m2.at[pair], z_p2.at[pair], *wide_at(z_own))
        return ring_sum(lambda t, k: grads.at[pair, t, :, z_cols[k]], z, zp_dev, zm_dev, bufs, 24 if layer else 0)

    z_big = [z_ring(0), z_ring(1)]
    def layer_of(target):
        return lax.div(target, 2)

    x_big = ring_sum(
        lambda t, k: grads.at[t, :, :, x_cols[k]], x, xp_dev, xm_dev, (x_a1, x_b1, x_m2, x_p2, *wide_at(x_own)), 6, layer_of
    )
    z_small = ring_sum(
        lambda t, k: z_r.at[t, :, z_own[k]], x, xp_dev, xm_dev, (z_sa1, z_sb1, z_sm2, z_sp2, *flat_at(z_own)), 12, layer_of
    )
    x_small = ring_sum(
        lambda t, k: x_r.at[t, :, x_own[k]], z, zp_dev, zm_dev, (x_sa1, x_sb1, x_sm2, x_sp2, *flat_at(x_own)), 18
    )
    out_at = [(slice(None), pl.ds(0, WIDE)), (slice(None), pl.ds(WIDE, WIDE))]
    o_ring = ring_sum(
        lambda t, k: grads_out.at[t, :, pl.ds(k * WIDE, WIDE)], x, xp_dev, xm_dev, (o_a1, o_b1, o_m2, o_p2, *out_at), 30
    )

    def sum_z(layer):
        pair = slice(2 * layer, 2 * layer + 2)
        z_r[pair] = (grads[pair, z, :, 0:HALF].astype(F32) + z_m2[pair].astype(F32) + z_p2[pair].astype(F32)).astype(BF16)

    shares[1].wait_recv()
    gradient(1)
    z_big[1][0]()
    x_big[0](1)
    shares[0].wait_recv()
    gradient(0)
    z_big[0][0]()
    x_big[0](0)

    @pl.when(y >= 2)
    def _():
        pass_attention()
        await_attention()

    pass_c(1)
    pass_c(0)
    gradient_out(1)
    gradient_out(0)
    o_ring[0]()
    z_big[1][1]()
    x_big[1](1)
    z_big[0][1]()
    x_big[1](0)
    z_big[1][2]()
    sum_z(1)
    z_small[0](1)
    o_ring[1]()
    z_big[0][2]()
    sum_z(0)
    z_small[0](0)
    x_big[2]()
    x_r[...] = (grads[x, :, :, HALF:QKV].astype(F32) + x_m2[...].astype(F32) + x_p2[...].astype(F32)).astype(BF16)
    x_small[0]()
    z_small[1](1)
    z_small[1](0)
    x_small[1]()
    o_ring[2]()
    out_ref[:, QKV:COLS] = grads_out[x].astype(F32) + o_m2[...].astype(F32) + o_p2[...].astype(F32)
    z_small[2]()
    out_ref[:, 0:HALF] = z_r[x].astype(F32) + z_sm2[...].astype(F32) + z_sp2[...].astype(F32)
    x_small[2]()
    out_ref[:, HALF:QKV] = x_r[z].astype(F32) + x_sm2[...].astype(F32) + x_sp2[...].astype(F32)

    @pl.when(y >= 2)
    def _():
        settle()

    for copy in sent:
        copy.wait_send()

    @pl.when((y > 0) & (y < 3))
    def _():
        h_hop.wait_send()

    @pl.when(y > 0)
    def _():
        c_half(0).wait_send()
        c_half(1).wait_send()


def split_columns(total_ref, gq_ref, go_ref):
    gq_ref[0] = total_ref[:, :QKV]
    go_ref[0] = total_ref[:, QKV:]


def on_device(inputs, cotangent, w_qkv, w_out):
    any_space = pl.BlockSpec(memory_space=pl.ANY)
    vmem = pl.BlockSpec(memory_space=pltpu.VMEM)
    dma = pltpu.SemaphoreType.DMA

    def flow(widths):
        first, second = widths
        both = first + second
        return [
            pltpu.VMEM((4, 64, first), BF16),
            pltpu.VMEM((4, 64, second), BF16),
            pltpu.VMEM((4, 64, both), BF16),
            pltpu.VMEM((4, 64, both), BF16),
            pltpu.VMEM((4, 64, both), BF16),
            pltpu.VMEM((64, first), BF16),
            pltpu.VMEM((64, second), BF16),
            pltpu.VMEM((64, both), BF16),
            pltpu.VMEM((64, both), BF16),
        ]

    total = pl.pallas_call(
        kernel,
        out_shape=jax.ShapeDtypeStruct((64, COLS), F32),
        in_specs=[any_space] * 4,
        out_specs=vmem,
        scratch_shapes=[
            pltpu.VMEM((2, D, QKV), BF16),
            pltpu.VMEM((2, D, D), BF16),
            pltpu.VMEM((2, QKV, D), BF16),
            pltpu.VMEM((2, D, D), BF16),
            pltpu.VMEM((2, SEQ, D), BF16),
            pltpu.VMEM((2, SEQ, D), BF16),
            pltpu.VMEM((3, SEQ, D), BF16),
            pltpu.VMEM((2, 2 * SEQ, D), BF16),
            pltpu.VMEM((2, SEQ, QKV), BF16),
            pltpu.VMEM((2, 4, 256, 256), BF16),
            pltpu.VMEM((2, 4, 256, 128), BF16),
            pltpu.VMEM((2, 4, 256, 128), BF16),
            pltpu.VMEM((2, 8, SEQ, D), BF16),
            pltpu.VMEM((3, SEQ, D), BF16),
            pltpu.VMEM((2, 2 * SEQ, QKV), BF16),
            pltpu.VMEM((2, 2, 2, 64, 128), F32),
            pltpu.VMEM((2, 4, 2, SEQ, 256), BF16),
            pltpu.VMEM((4, 4, 64, QKV), BF16),
            pltpu.VMEM((4, 64, D), BF16),
            *flow(Z_CUT),
            *flow(X_CUT),
            pltpu.VMEM((64, WIDE), BF16),
            pltpu.VMEM((64, WIDE), BF16),
            pltpu.VMEM((64, D), BF16),
            pltpu.VMEM((64, D), BF16),
            dma((6,)),
            dma((len(PARTS),)),
            dma((len(PARTS),)),
            dma((len(PARTS), 4)),
            dma((len(PARTS), 4)),
            dma((len(PARTS),)),
            dma((len(PARTS),)),
            dma((2,)),
            dma((2,)),
            dma((4,)),
            dma((4,)),
            dma((2,)),
            dma((2,)),
            dma((4,)),
            dma((4,)),
            dma((4,)),
            dma((4,)),
            dma((4,)),
            dma((4,)),
            dma((2, 4)),
            dma((2, 4)),
            dma((36,)),
            dma((36,)),
        ],
        compiler_params=pltpu.CompilerParams(
            collective_id=0, has_side_effects=True, vmem_limit_bytes=56 * 2**20
        ),
    )(inputs, cotangent, w_qkv, w_out)
    return pl.pallas_call(
        split_columns,
        out_shape=(jax.ShapeDtypeStruct((1, 64, QKV), F32), jax.ShapeDtypeStruct((1, 64, D), F32)),
    )(total)


def solution(mesh):
    placed = (
        P("dp", None, None, None, None),
        P("dp", None, None, None, None),
        P("section", None, None),
        P("section", None, None),
    )
    return jax.shard_map(
        on_device,
        mesh=mesh,
        in_specs=placed,
        out_specs=(P("section", "dp", None), P("section", "dp", None)),
        check_vma=False,
    )
```

```python
import functools

import jax
import jax.numpy as jnp
from jax import lax
from jax.experimental import pallas as pl
from jax.experimental.pallas import tpu as pltpu
from jax.sharding import PartitionSpec as P

MESH = pl.DeviceIdType.MESH
F32 = jnp.float32
BF16 = jnp.bfloat16
EPSILON = 1e-05

D = 1024
SEQ = 128
QKV = 1536
COLS = 2560
Z_CUT = (512, 384)
X_CUT = (256, 384)
HALF = sum(Z_CUT)
WIDE = 512
PARTS = [("q", k, 32) for k in range(4)] + [("o", k, 64) for k in range(2)]


def mm(a, b):
    return jnp.dot(a, b, preferred_element_type=F32)


def mm_nt(a, b):
    return lax.dot_general(a, b, (((1,), (1,)), ((), ())), preferred_element_type=F32)


def mm_tn(a, b):
    return lax.dot_general(a, b, (((0,), (0,)), ((), ())), preferred_element_type=F32)


def block_diagonal(pair, group):
    low = lax.broadcasted_iota(jnp.int32, pair.shape, 1) < 64
    wide = pair.astype(F32)
    rolled = pltpu.roll(wide, 64, 1)
    first, second = (wide, rolled) if group % 2 == 0 else (rolled, wide)
    zero = jnp.zeros_like(wide)
    return jnp.concatenate([jnp.where(low, first, zero), jnp.where(low, zero, second)], axis=0).astype(BF16)


def stack_pairs(x, group):
    at = group * 256
    blocks = []
    for start in range(0, x.shape[0], 64):
        blocks += [x[start : start + 64, at : at + 128], x[start : start + 64, at + 128 : at + 256]]
    return jnp.concatenate(blocks, axis=0)


def head_sums(x):
    return (jnp.sum(x[:128], axis=0, keepdims=True), jnp.sum(x[128:], axis=0, keepdims=True))


def kv_pairs(joined, group):
    at = (group // 2) * 128
    return joined[:, D + at : D + at + 128], joined[:, D + 256 + at : D + 256 + at + 128]


def attention_forward(joined, probs_ref, keys_ref, values_ref, att_ref, layer):
    key = lax.broadcasted_iota(jnp.int32, (256, 256), 0) & 127
    column = lax.broadcasted_iota(jnp.int32, (256, 256), 1)
    causal = key <= (column & 63) + 64 * lax.shift_right_logical(column, 7)
    for group in range(4):
        queries = stack_pairs(joined, group)
        keys, values = (block_diagonal(pair, group) for pair in kv_pairs(joined, group))
        keys_ref[layer, group] = keys
        values_ref[layer, group] = values
        scores = mm_nt(keys, queries) * 0.125
        exponent = jnp.where(causal, jnp.exp(scores), 0.0)
        first, second = head_sums(exponent)
        probs = jnp.concatenate([exponent[:128] * (1.0 / first), exponent[128:] * (1.0 / second)], axis=0).astype(BF16)
        probs_ref[layer, group] = probs
        mixed = mm_tn(probs, values).astype(BF16)
        at = group * 256
        for half in range(2):
            rows = slice(64 * half, 64 * half + 64)
            att_ref[rows, at : at + 128] = mixed[128 * half : 128 * half + 64]
            att_ref[rows, at + 128 : at + 256] = mixed[128 * half + 64 : 128 * half + 128]


def attention_backward(joined, d_attention, probs_ref, keys_ref, values_ref, dj_ref, carried, layer, half):
    rows = pl.ds(pl.multiple_of(64 * half, 64), 64)
    lanes = pl.ds(pl.multiple_of(128 * half, 128), 128)
    d_keys, d_values = [], []
    for group in range(4):
        queries = stack_pairs(joined, group)
        d_heads = stack_pairs(d_attention, group)
        probs = probs_ref[layer, group, :, lanes]
        d_probs = mm_nt(values_ref[layer, group], d_heads)
        wide = probs.astype(F32)
        first, second = head_sums(wide * d_probs)
        centred = jnp.concatenate([d_probs[:128] - first, d_probs[128:] - second], axis=0)
        d_scores = (wide * centred * 0.125).astype(BF16)
        d_keys.append(mm(d_scores, queries))
        d_values.append(mm(probs, d_heads))
        d_queries = mm_tn(d_scores, keys_ref[layer, group]).astype(BF16)
        lane = group * 256
        dj_ref[layer, rows, lane : lane + 128] = d_queries[:64]
        dj_ref[layer, rows, lane + 128 : lane + 256] = d_queries[64:]
    low = lax.broadcasted_iota(jnp.int32, (128, 128), 1) < 64

    def merged(even, odd):
        first = even[:128] + pltpu.roll(even[128:], 64, 1)
        second = pltpu.roll(odd[:128], 64, 1) + odd[128:]
        return jnp.where(low, first, second)

    for number, parts in ((0, d_keys), (1, d_values)):
        for pair in range(2):
            total = merged(parts[2 * pair], parts[2 * pair + 1])
            lane = D + 256 * number + 128 * pair
            ours = jnp.where(half == 1, total[64:], total[:64] + carried[layer, number, pair])
            dj_ref[layer, rows, lane : lane + 128] = ours.astype(BF16)
            carried[layer, number, pair] = total[:64]


def inverse_norm(wide):
    return lax.rsqrt(jnp.mean(wide * wide, axis=-1, keepdims=True) + EPSILON)


def kernel(
    inputs_ref, cotangent_ref, wq_ref, wo_ref,
    out_ref,
    wq, wo, wqt, wot, entry, passed, hidden, normed, joined, probs, keys, values, att, upstream, dj, carried, c_all, grads, grads_out,
    z_a1, z_b1, z_m2, z_p2, z_r, z_sa1, z_sb1, z_sm2, z_sp2,
    x_a1, x_b1, x_m2, x_p2, x_r, x_sa1, x_sb1, x_sm2, x_sp2,
    o_a1, o_b1, o_m2, o_p2,
    load_sem, flip_send, flip_recv, spread_send, spread_recv, core_send, core_recv,
    entry_send, entry_recv, hop_send, hop_recv, c_hop_send, c_hop_recv, share_send, share_recv,
    att_send, att_recv, att_core_send, att_core_recv, c_send, c_recv, sum_send, sum_recv,
):
    section, dp = lax.axis_index("section"), lax.axis_index("dp")
    y, x_hi = lax.div(section, 2), lax.rem(section, 2)
    z, x_lo, core = lax.div(dp, 4), lax.rem(lax.div(dp, 2), 2), lax.rem(dp, 2)
    x = 2 * x_hi + x_lo
    slot = 2 * z + core

    def place(y, x, z, core):
        return (2 * y + lax.div(x, 2), 4 * z + 2 * lax.rem(x, 2) + core)

    core_dev = place(y, x, z, 1 - core)
    xp_dev, xm_dev = place(y, lax.rem(x + 1, 4), z, core), place(y, lax.rem(x + 3, 4), z, core)
    zp_dev, zm_dev = place(y, x, lax.rem(z + 1, 4), core), place(y, x, lax.rem(z + 3, 4), core)
    yp_dev, ym_dev = place(lax.rem(y + 1, 4), x, z, core), place(lax.rem(y + 3, 4), x, z, core)
    column = [[place(y, x, lax.rem(z + k, 4), c) for c in (core, 1 - core)] for k in range(4)]
    flip_dev = place(y, 3 - x, z, core)
    side_dev = place(y, 2 * x_hi + 1 - x_lo, z, core)
    up_across_dev, down_across_dev = place(lax.rem(y + 1, 4), 3 - x, z, core), place(lax.rem(y + 3, 4), 3 - x, z, core)

    def remote(src, dst, send_sem, recv_sem, device):
        return pltpu.make_async_remote_copy(
            src_ref=src, dst_ref=dst, send_sem=send_sem, recv_sem=recv_sem, device_id=device, device_id_type=MESH
        )

    sent = []

    def go(copy):
        copy.start()
        sent.append(copy)

    loads = [
        pltpu.make_async_copy(wq_ref.at[0], wq.at[x_hi], load_sem.at[0]),
        pltpu.make_async_copy(wo_ref.at[0], wo.at[x_hi], load_sem.at[1]),
    ]
    load_in = pltpu.make_async_copy(inputs_ref.at[0, 0, 0], hidden.at[0], load_sem.at[2])
    load_cot = pltpu.make_async_copy(cotangent_ref.at[0, 0, 0], upstream.at[2], load_sem.at[3])
    load_entry = [pltpu.make_async_copy(inputs_ref.at[0, s, 0], entry.at[s], load_sem.at[4 + s]) for s in range(2)]
    for copy in loads:
        copy.start()

    near, far = x_hi == 0, x_hi == 1

    @pl.when((y == 0) & near)
    def _():
        load_entry[0].start()
        load_entry[1].start()
        load_in.start()

    @pl.when((y == 3) & near)
    def _():
        load_cot.start()

    barrier = pltpu.get_barrier_semaphore()
    for device in (core_dev, xp_dev, xm_dev, zp_dev, zm_dev, yp_dev, ym_dev):
        pl.semaphore_signal(barrier, inc=1, device_id=device, device_id_type=MESH)
    pl.semaphore_wait(barrier, 7)

    in_hop = remote(inputs_ref.at[0, 1, 0], hidden.at[0], hop_send.at[2], hop_recv.at[2], side_dev)
    cot_hop = remote(cotangent_ref.at[0, 1, 0], upstream.at[2], hop_send.at[3], hop_recv.at[3], side_dev)

    @pl.when((y == 0) & far)
    def _():
        in_hop.start()

    @pl.when((y == 3) & far)
    def _():
        cot_hop.start()

    h_hop = remote(hidden.at[2], hidden.at[0], hop_send.at[0], hop_recv.at[0], yp_dev)
    def attend(h, weights, layer):
        wide = h.astype(F32)
        inverse = inverse_norm(wide)
        normed[layer, 0:SEQ] = (wide * inverse).astype(BF16)
        joined[layer] = (mm(h, wq[weights]) * inverse).astype(BF16)
        attention_forward(joined[layer], probs, keys, values, att.at[layer, slot], layer)

    def project(h, weights, layer, turned):
        update = mm(att[layer, slot], wot[weights]) if turned else mm_nt(att[layer, slot], wo[weights])
        return (h.astype(F32) + update).astype(BF16)

    def run_forward(h, weights, layer, turned=False):
        attend(h, weights, layer)
        return project(h, weights, layer, turned)

    other = 1 - x_hi
    piece = lax.rem(z + 2 * x_lo, 4)
    pieces = [lax.rem(piece + k, 4) for k in range(4)]

    def chunk(buf, slot, which, half, part):
        name, k, rows = part
        at = (half * 4 + which) * 128 + k * rows
        return buf[name].at[slot, pl.ds(pl.multiple_of(at, rows), rows)]

    held, given = {"q": wq, "o": wo}, {"q": wq_ref, "o": wo_ref}

    def flip_copy(i, block, source=None):
        return remote(block if source is None else source, block, flip_send.at[i], flip_recv.at[i], flip_dev)

    flips = [
        flip_copy(i, chunk(held, x_hi, pieces[2], core, part), chunk(given, 0, pieces[2], core, part))
        for i, part in enumerate(PARTS)
    ]
    sent.extend(flips)

    @pl.when((y == 0) & far)
    def _():
        for copy in flips:
            copy.start()

    across = [remote(passed.at[s], entry.at[s], entry_send.at[s], entry_recv.at[s], flip_dev) for s in range(2)]
    onward = [
        remote(passed.at[0], hidden.at[0], entry_send.at[0], hop_recv.at[0], up_across_dev),
        remote(passed.at[1], hidden.at[0], entry_send.at[1], hop_recv.at[0], yp_dev),
    ]

    @pl.when(y == 0)
    def _():
        for copy in loads:
            copy.wait()

        def first_pass(s, carry):
            for k in range(2):
                @pl.when((s == k) & near)
                def _():
                    load_entry[k].wait()

                @pl.when((s == k) & far)
                def _():
                    across[k].wait_recv()

            passed[s] = run_forward(entry[s], x_hi, 0)
            for k in range(2):
                @pl.when((s == k) & near)
                def _():
                    across[k].start()

                @pl.when((s == k) & far)
                def _():
                    onward[k].start()

            return carry

        lax.fori_loop(0, 2, first_pass, 0)

        @pl.when(near)
        def _():
            for copy in across:
                copy.wait_send()

        @pl.when(far)
        def _():
            for copy in onward:
                copy.wait_send()

    @pl.when((y > 0) | near)
    def _():
        for copy in flips:
            copy.start()

    def spread(i, part):
        flip_copy(i, chunk(held, other, pieces[0], core, part)).wait_recv()
        block = chunk(held, other, pieces[0], core, part)
        for k, device in ((1, zm_dev), (2, side_dev), (3, zp_dev)):
            go(remote(block, block, spread_send.at[i, k], spread_recv.at[i, k], device))

    def core_copy(i, part, half):
        name, k, rows = part
        block = held[name].at[other].reshape(8, 128, held[name].shape[2])
        block = block.at[pl.ds(half * 4, 4), pl.ds(k * rows, rows)]
        return remote(block, block, core_send.at[i], core_recv.at[i], core_dev)

    def gather_rest(i, part):
        for k in (1, 2, 3):
            block = chunk(held, other, pieces[k], core, part)
            remote(block, block, spread_send.at[i, k], spread_recv.at[i, k], side_dev).wait_recv()
        go(core_copy(i, part, core))

    def await_core(name):
        for i, part in enumerate(PARTS):
            if part[0] == name:
                core_copy(i, part, 1 - core).wait_recv()

    @pl.when(y > 0)
    def _():
        for copy in loads:
            copy.wait()

    for i, part in enumerate(PARTS):
        spread(i, part)
        if i > 0:
            gather_rest(i - 1, PARTS[i - 1])

    gather_rest(len(PARTS) - 1, PARTS[-1])
    await_core("q")

    @pl.when(y == 1)
    def _():
        h_hop.wait_recv()
        attend(hidden[0], 0, 0)

    await_core("o")

    def transpose_weights():
        def one(k, carry):
            layer, cols = lax.div(k, 6), pl.ds(pl.multiple_of(lax.rem(k, 6) * 256, 256), 256)
            wqt[layer, cols] = wq[layer, :, cols].T
            return carry

        lax.fori_loop(0, 12, one, 0)

    @pl.when(y >= 2)
    def _():
        def one(k, carry):
            layer, rows = lax.div(k, 4), pl.ds(pl.multiple_of(lax.rem(k, 4) * 256, 256), 256)
            wot[layer, :, rows] = wo[layer, rows].T
            return carry

        lax.fori_loop(0, 8, one, 0)
        transpose_weights()

    @pl.when((y == 0) & near)
    def _():
        load_in.wait()

    @pl.when((y == 0) & far)
    def _():
        in_hop.wait()

    @pl.when(y >= 2)
    def _():
        h_hop.wait_recv()

    def forward(turned, layer, carry):
        if turned:
            attend(hidden[layer], layer, layer)
        else:
            pl.when((y == 0) | (layer > 0))(lambda: attend(hidden[layer], layer, layer))
        hidden[layer + 1] = project(hidden[layer], layer, layer, turned)
        return carry

    @pl.when(y < 2)
    def _():
        lax.fori_loop(0, 2, functools.partial(forward, False), 0)

    @pl.when(y >= 2)
    def _():
        lax.fori_loop(0, 2, functools.partial(forward, True), 0)

    @pl.when((y > 0) & (y < 3))
    def _():
        h_hop.start()

    def share(buf, layer, number):
        return remote(
            buf.at[layer, 0:SEQ], buf.at[layer, SEQ : 2 * SEQ], share_send.at[number], share_recv.at[number], core_dev
        )

    shares = [share(dj, 0, 0), share(dj, 1, 1)]
    share_normed = remote(
        normed.at[:, 0:SEQ], normed.at[:, SEQ : 2 * SEQ], share_send.at[2], share_recv.at[2], core_dev
    )
    sent.extend(shares)

    def att_block(k, half):
        return att.at[:, 2 * lax.rem(z + 4 - k, 4) + half]

    def att_copy(k):
        return remote(att_block(0, core), att_block(0, core), att_send.at[k], att_recv.at[k], column[k][0])

    def core_att(k):
        return remote(att_block(k, core), att_block(k, core), att_core_send.at[k], att_core_recv.at[k], core_dev)

    def send_attention():
        share_normed.start()
        for k in (1, 3, 2):
            att_copy(k).start()

    def pass_attention():
        core_att(0).start()
        for k in (1, 3, 2):
            remote(att_block(k, core), att_block(k, core), att_send.at[k], att_recv.at[k], core_dev).wait_recv()
            core_att(k).start()

    def await_attention():
        for k in range(4):
            block = att_block(k, 1 - core)
            remote(block, block, att_core_send.at[k], att_core_recv.at[k], core_dev).wait_recv()

    early = sent[: -len(shares)]
    del sent[: len(early)]

    def settle():
        for copy in early:
            copy.wait_send()
        share_normed.wait_send()
        for k in (1, 3, 2):
            att_copy(k).wait_send()
        for k in range(4):
            core_att(k).wait_send()

    def c_columns(layer, k):
        return upstream.at[layer + 1, :, pl.ds(pl.multiple_of(256 * lax.rem(z + k, 4), 256), 256)]

    def c_copy(layer, k):
        return remote(c_columns(layer, k), c_all.at[layer, z, core], c_send.at[layer, k], c_recv.at[layer, k], column[k][0])

    def core_c(layer, half):
        block = c_all.at[layer, :, half]
        return remote(block, block, c_send.at[layer, 0], c_recv.at[layer, 0], core_dev)

    def send_c(layer):
        for k in (1, 3, 2):
            c_copy(layer, k).start()

    def pass_c(layer):
        c_all[layer, z, core] = c_columns(layer, 0)[...]
        for k in (1, 3, 2):
            block = c_all.at[layer, lax.rem(z + 4 - k, 4), core]
            remote(block, block, c_send.at[layer, k], c_recv.at[layer, k], core_dev).wait_recv()
        core_c(layer, core).start()

    sent.extend(c_copy(layer, k) for layer in range(2) for k in (1, 3, 2))
    sent.extend(core_c(layer, core) for layer in range(2))

    send_attention()

    @pl.when(y < 2)
    def _():
        transpose_weights()
        pass_attention()
        await_attention()
        share_normed.wait_recv()
        settle()

    @pl.when((y == 3) & near)
    def _():
        load_cot.wait()

    @pl.when((y == 3) & far)
    def _():
        cot_hop.wait()

    def c_half(half):
        rows = pl.ds(pl.multiple_of(64 * half, 64), 64)
        return remote(upstream.at[0, rows], upstream.at[2, rows], c_hop_send.at[half], c_hop_recv.at[half], ym_dev)

    def backward(step, carry):
        half, layer = 1 - lax.div(step, 2), 1 - lax.rem(step, 2)
        rows = pl.ds(pl.multiple_of(64 * half, 64), 64)

        @pl.when((y < 3) & (layer == 1))
        def _():
            c_half(half).wait_recv()

        @pl.when((y == 0) & (half == 0))
        def _():
            send_c(layer)

        d_attention = mm(upstream[layer + 1, rows], wo[layer]).astype(BF16)
        attention_backward(joined[layer, rows], d_attention, probs, keys, values, dj, carried, layer, half)

        @pl.when(half == 0)
        def _():
            share(dj, layer, layer).start()

        @pl.when((layer > 0) | (y > 0))
        def _():
            d_normed = mm(dj[layer, rows], wqt[layer])
            wide = hidden[layer, rows].astype(F32)
            inverse = inverse_norm(wide)
            scaled = wide * inverse
            along = jnp.mean(d_normed * scaled, axis=-1, keepdims=True)
            upstream[layer, rows] = (
                upstream[layer + 1, rows].astype(F32) + inverse * (d_normed - scaled * along)
            ).astype(BF16)

        @pl.when((y > 0) & (layer == 0))
        def _():
            c_half(half).start()

        return carry

    lax.fori_loop(0, 4, backward, 0)

    @pl.when(y > 0)
    def _():
        send_c(1)
        send_c(0)

    @pl.when(y >= 2)
    def _():
        share_normed.wait_recv()

    low = lax.broadcasted_iota(jnp.int32, (2 * SEQ, 128), 1) < 64

    def own_columns(block):
        def tile(k):
            return block[:, 128 * k : 128 * k + 128].astype(F32)

        tiles = []
        for lo in range(2):
            for pair in range(2):
                a, b = tile(4 * pair + lo), tile(4 * pair + 2 + lo)
                first = jnp.where(core == 0, a, pltpu.roll(a, 64, 1))
                second = jnp.where(core == 0, pltpu.roll(b, 64, 1), b)
                tiles.append(jnp.where(low, first, second).astype(BF16))
        return jnp.concatenate(tiles, axis=1)

    def gradient(layer):
        left = own_columns(normed[layer])
        for lo in range(2):
            part = mm_tn(left[:, 256 * lo : 256 * lo + 256], dj[layer]).astype(BF16)
            grads[2 * layer + lo] = part.reshape(4, 64, QKV)

    def gradient_out(layer):
        core_c(layer, 1 - core).wait_recv()
        a = c_all[layer, :, :, :, 0:128].reshape(8 * SEQ, 128).astype(F32)
        b = c_all[layer, :, :, :, 128:256].reshape(8 * SEQ, 128).astype(F32)
        first = jnp.where(core == 0, a, pltpu.roll(a, 64, 1))
        second = jnp.where(core == 0, pltpu.roll(b, 64, 1), b)
        left = jnp.where(lax.broadcasted_iota(jnp.int32, a.shape, 1) < 64, first, second).astype(BF16)
        part = mm_tn(left, att[layer].reshape(8 * SEQ, D)).astype(BF16)
        grads_out[2 * layer : 2 * layer + 2] = part.reshape(2, 64, D)

    def ring_sum(view, position, plus, minus, bufs, sems, layers=None):
        a1, b1, m2, p2, alpha, beta = bufs
        opposite, after, before = (lax.rem(position + k, 4) for k in (2, 1, 3))
        s, r = sum_send.at, sum_recv.at
        copies = [
            remote(view(opposite, 0), a1, s[sems], r[sems], plus),
            remote(view(opposite, 1), b1, s[sems + 1], r[sems + 1], minus),
            remote(view(after, 1), m2.at[beta], s[sems + 2], r[sems + 2], plus),
            remote(view(before, 0), p2.at[alpha], s[sems + 3], r[sems + 3], minus),
            remote(view(after, 0), m2.at[alpha], s[sems + 4], r[sems + 4], plus),
            remote(view(before, 1), p2.at[beta], s[sems + 5], r[sems + 5], minus),
        ]
        sent.extend(copies)

        def only(stage, target):
            if stage is None:
                return lambda body: body()
            return pl.when(layers(target) == stage)

        def first(stage=None):
            @only(stage, opposite)
            def _():
                copies[0].start()
                copies[1].start()

            @only(stage, after)
            def _():
                copies[2].start()

            @only(stage, before)
            def _():
                copies[3].start()

        def second(stage=None):
            @only(stage, after)
            def _():
                mine = view(after, 0)
                copies[0].wait_recv()
                mine[...] = (mine[...].astype(F32) + a1[...].astype(F32)).astype(BF16)
                copies[4].start()

            @only(stage, before)
            def _():
                mine = view(before, 1)
                copies[1].wait_recv()
                mine[...] = (mine[...].astype(F32) + b1[...].astype(F32)).astype(BF16)
                copies[5].start()

        def last():
            for copy in copies[2:]:
                copy.wait_recv()

        return first, second, last

    def cut(offset, widths):
        return [pl.ds(offset, widths[0]), pl.ds(offset + widths[0], widths[1])]

    z_cols, x_cols, z_own, x_own = cut(0, Z_CUT), cut(HALF, X_CUT), cut(0, Z_CUT), cut(0, X_CUT)

    def wide_at(own):
        return [(slice(None), slice(None), cols) for cols in own]

    def flat_at(own):
        return [(slice(None), cols) for cols in own]

    def z_ring(layer):
        pair = pl.ds(2 * layer, 2)
        bufs = (z_a1.at[pair], z_b1.at[pair], z_m2.at[pair], z_p2.at[pair], *wide_at(z_own))
        return ring_sum(lambda t, k: grads.at[pair, t, :, z_cols[k]], z, zp_dev, zm_dev, bufs, 24 if layer else 0)

    z_big = [z_ring(0), z_ring(1)]
    def layer_of(target):
        return lax.div(target, 2)

    x_big = ring_sum(
        lambda t, k: grads.at[t, :, :, x_cols[k]], x, xp_dev, xm_dev, (x_a1, x_b1, x_m2, x_p2, *wide_at(x_own)), 6, layer_of
    )
    z_small = ring_sum(
        lambda t, k: z_r.at[t, :, z_own[k]], x, xp_dev, xm_dev, (z_sa1, z_sb1, z_sm2, z_sp2, *flat_at(z_own)), 12, layer_of
    )
    x_small = ring_sum(
        lambda t, k: x_r.at[t, :, x_own[k]], z, zp_dev, zm_dev, (x_sa1, x_sb1, x_sm2, x_sp2, *flat_at(x_own)), 18
    )
    out_at = [(slice(None), pl.ds(0, WIDE)), (slice(None), pl.ds(WIDE, WIDE))]
    o_ring = ring_sum(
        lambda t, k: grads_out.at[t, :, pl.ds(k * WIDE, WIDE)], x, xp_dev, xm_dev, (o_a1, o_b1, o_m2, o_p2, *out_at), 30
    )

    def sum_z(layer):
        pair = slice(2 * layer, 2 * layer + 2)
        z_r[pair] = (grads[pair, z, :, 0:HALF].astype(F32) + z_m2[pair].astype(F32) + z_p2[pair].astype(F32)).astype(BF16)

    shares[1].wait_recv()
    gradient(1)
    z_big[1][0]()
    x_big[0](1)
    shares[0].wait_recv()
    gradient(0)
    z_big[0][0]()
    x_big[0](0)

    @pl.when(y >= 2)
    def _():
        pass_attention()
        await_attention()

    pass_c(1)
    pass_c(0)
    gradient_out(1)
    gradient_out(0)
    z_big[1][1]()
    x_big[1](1)
    o_ring[0]()
    z_big[0][1]()
    x_big[1](0)
    z_big[1][2]()
    sum_z(1)
    z_small[0](1)
    o_ring[1]()
    z_big[0][2]()
    sum_z(0)
    z_small[0](0)
    x_big[2]()
    x_r[...] = (grads[x, :, :, HALF:QKV].astype(F32) + x_m2[...].astype(F32) + x_p2[...].astype(F32)).astype(BF16)
    x_small[0]()
    z_small[1](1)
    z_small[1](0)
    x_small[1]()
    last_sent = sent[-18:-6]
    for copy in sent[:-18] + sent[-6:]:
        copy.wait_send()

    @pl.when(y >= 2)
    def _():
        settle()

    @pl.when((y > 0) & (y < 3))
    def _():
        h_hop.wait_send()

    @pl.when(y > 0)
    def _():
        c_half(0).wait_send()
        c_half(1).wait_send()

    o_ring[2]()
    out_ref[:, QKV:COLS] = grads_out[x].astype(F32) + o_m2[...].astype(F32) + o_p2[...].astype(F32)
    z_small[2]()
    out_ref[:, 0:HALF] = z_r[x].astype(F32) + z_sm2[...].astype(F32) + z_sp2[...].astype(F32)
    x_small[2]()
    out_ref[:, HALF:QKV] = x_r[z].astype(F32) + x_sm2[...].astype(F32) + x_sp2[...].astype(F32)

    for copy in last_sent:
        copy.wait_send()


def split_columns(total_ref, gq_ref, go_ref):
    gq_ref[0] = total_ref[:, :QKV]
    go_ref[0] = total_ref[:, QKV:]


def on_device(inputs, cotangent, w_qkv, w_out):
    any_space = pl.BlockSpec(memory_space=pl.ANY)
    vmem = pl.BlockSpec(memory_space=pltpu.VMEM)
    dma = pltpu.SemaphoreType.DMA

    def flow(widths):
        first, second = widths
        both = first + second
        return [
            pltpu.VMEM((4, 64, first), BF16),
            pltpu.VMEM((4, 64, second), BF16),
            pltpu.VMEM((4, 64, both), BF16),
            pltpu.VMEM((4, 64, both), BF16),
            pltpu.VMEM((4, 64, both), BF16),
            pltpu.VMEM((64, first), BF16),
            pltpu.VMEM((64, second), BF16),
            pltpu.VMEM((64, both), BF16),
            pltpu.VMEM((64, both), BF16),
        ]

    total = pl.pallas_call(
        kernel,
        out_shape=jax.ShapeDtypeStruct((64, COLS), F32),
        in_specs=[any_space] * 4,
        out_specs=vmem,
        scratch_shapes=[
            pltpu.VMEM((2, D, QKV), BF16),
            pltpu.VMEM((2, D, D), BF16),
            pltpu.VMEM((2, QKV, D), BF16),
            pltpu.VMEM((2, D, D), BF16),
            pltpu.VMEM((2, SEQ, D), BF16),
            pltpu.VMEM((2, SEQ, D), BF16),
            pltpu.VMEM((3, SEQ, D), BF16),
            pltpu.VMEM((2, 2 * SEQ, D), BF16),
            pltpu.VMEM((2, SEQ, QKV), BF16),
            pltpu.VMEM((2, 4, 256, 256), BF16),
            pltpu.VMEM((2, 4, 256, 128), BF16),
            pltpu.VMEM((2, 4, 256, 128), BF16),
            pltpu.VMEM((2, 8, SEQ, D), BF16),
            pltpu.VMEM((3, SEQ, D), BF16),
            pltpu.VMEM((2, 2 * SEQ, QKV), BF16),
            pltpu.VMEM((2, 2, 2, 64, 128), F32),
            pltpu.VMEM((2, 4, 2, SEQ, 256), BF16),
            pltpu.VMEM((4, 4, 64, QKV), BF16),
            pltpu.VMEM((4, 64, D), BF16),
            *flow(Z_CUT),
            *flow(X_CUT),
            pltpu.VMEM((64, WIDE), BF16),
            pltpu.VMEM((64, WIDE), BF16),
            pltpu.VMEM((64, D), BF16),
            pltpu.VMEM((64, D), BF16),
            dma((6,)),
            dma((len(PARTS),)),
            dma((len(PARTS),)),
            dma((len(PARTS), 4)),
            dma((len(PARTS), 4)),
            dma((len(PARTS),)),
            dma((len(PARTS),)),
            dma((2,)),
            dma((2,)),
            dma((4,)),
            dma((4,)),
            dma((2,)),
            dma((2,)),
            dma((4,)),
            dma((4,)),
            dma((4,)),
            dma((4,)),
            dma((4,)),
            dma((4,)),
            dma((2, 4)),
            dma((2, 4)),
            dma((36,)),
            dma((36,)),
        ],
        compiler_params=pltpu.CompilerParams(
            collective_id=0, has_side_effects=True, vmem_limit_bytes=56 * 2**20
        ),
    )(inputs, cotangent, w_qkv, w_out)
    return pl.pallas_call(
        split_columns,
        out_shape=(jax.ShapeDtypeStruct((1, 64, QKV), F32), jax.ShapeDtypeStruct((1, 64, D), F32)),
    )(total)


def solution(mesh):
    placed = (
        P("dp", None, None, None, None),
        P("dp", None, None, None, None),
        P("section", None, None),
        P("section", None, None),
    )
    return jax.shard_map(
        on_device,
        mesh=mesh,
        in_specs=placed,
        out_specs=(P("section", "dp", None), P("section", "dp", None)),
        check_vma=False,
    )
```

```python
import functools

import jax
import jax.numpy as jnp
from jax import lax
from jax.experimental import pallas as pl
from jax.experimental.pallas import tpu as pltpu
from jax.sharding import PartitionSpec as P

MESH = pl.DeviceIdType.MESH
F32 = jnp.float32
BF16 = jnp.bfloat16
EPSILON = 1e-05

D = 1024
SEQ = 128
QKV = 1536
COLS = 2560
Z_CUT = (512, 384)
X_CUT = (256, 384)
HALF = sum(Z_CUT)
WIDE = 512
PARTS = [("q", k, 32) for k in range(4)] + [("o", k, 64) for k in range(2)]


def mm(a, b):
    return jnp.dot(a, b, preferred_element_type=F32)


def mm_nt(a, b):
    return lax.dot_general(a, b, (((1,), (1,)), ((), ())), preferred_element_type=F32)


def mm_tn(a, b):
    return lax.dot_general(a, b, (((0,), (0,)), ((), ())), preferred_element_type=F32)


def block_diagonal(pair, group):
    low = lax.broadcasted_iota(jnp.int32, pair.shape, 1) < 64
    wide = pair.astype(F32)
    rolled = pltpu.roll(wide, 64, 1)
    first, second = (wide, rolled) if group % 2 == 0 else (rolled, wide)
    zero = jnp.zeros_like(wide)
    return jnp.concatenate([jnp.where(low, first, zero), jnp.where(low, zero, second)], axis=0).astype(BF16)


def stack_pairs(x, group):
    at = group * 256
    blocks = []
    for start in range(0, x.shape[0], 64):
        blocks += [x[start : start + 64, at : at + 128], x[start : start + 64, at + 128 : at + 256]]
    return jnp.concatenate(blocks, axis=0)


def head_sums(x):
    return (jnp.sum(x[:128], axis=0, keepdims=True), jnp.sum(x[128:], axis=0, keepdims=True))


def kv_pairs(joined, group):
    at = (group // 2) * 128
    return joined[:, D + at : D + at + 128], joined[:, D + 256 + at : D + 256 + at + 128]


def attention_forward(joined, probs_ref, keys_ref, values_ref, att_ref, layer):
    key = lax.broadcasted_iota(jnp.int32, (256, 256), 0) & 127
    column = lax.broadcasted_iota(jnp.int32, (256, 256), 1)
    causal = key <= (column & 63) + 64 * lax.shift_right_logical(column, 7)
    for group in range(4):
        queries = stack_pairs(joined, group)
        keys, values = (block_diagonal(pair, group) for pair in kv_pairs(joined, group))
        keys_ref[layer, group] = keys
        values_ref[layer, group] = values
        scores = mm_nt(keys, queries) * 0.125
        exponent = jnp.where(causal, jnp.exp(scores), 0.0)
        first, second = head_sums(exponent)
        probs = jnp.concatenate([exponent[:128] * (1.0 / first), exponent[128:] * (1.0 / second)], axis=0).astype(BF16)
        probs_ref[layer, group] = probs
        mixed = mm_tn(probs, values).astype(BF16)
        at = group * 256
        for half in range(2):
            rows = slice(64 * half, 64 * half + 64)
            att_ref[rows, at : at + 128] = mixed[128 * half : 128 * half + 64]
            att_ref[rows, at + 128 : at + 256] = mixed[128 * half + 64 : 128 * half + 128]


def attention_backward(joined, d_attention, probs_ref, keys_ref, values_ref, dj_ref, carried, layer, half):
    rows = pl.ds(pl.multiple_of(64 * half, 64), 64)
    lanes = pl.ds(pl.multiple_of(128 * half, 128), 128)
    d_keys, d_values = [], []
    for group in range(4):
        queries = stack_pairs(joined, group)
        d_heads = stack_pairs(d_attention, group)
        probs = probs_ref[layer, group, :, lanes]
        d_probs = mm_nt(values_ref[layer, group], d_heads)
        wide = probs.astype(F32)
        first, second = head_sums(wide * d_probs)
        centred = jnp.concatenate([d_probs[:128] - first, d_probs[128:] - second], axis=0)
        d_scores = (wide * centred * 0.125).astype(BF16)
        d_keys.append(mm(d_scores, queries))
        d_values.append(mm(probs, d_heads))
        d_queries = mm_tn(d_scores, keys_ref[layer, group]).astype(BF16)
        lane = group * 256
        dj_ref[layer, rows, lane : lane + 128] = d_queries[:64]
        dj_ref[layer, rows, lane + 128 : lane + 256] = d_queries[64:]
    low = lax.broadcasted_iota(jnp.int32, (128, 128), 1) < 64

    def merged(even, odd):
        first = even[:128] + pltpu.roll(even[128:], 64, 1)
        second = pltpu.roll(odd[:128], 64, 1) + odd[128:]
        return jnp.where(low, first, second)

    for number, parts in ((0, d_keys), (1, d_values)):
        for pair in range(2):
            total = merged(parts[2 * pair], parts[2 * pair + 1])
            lane = D + 256 * number + 128 * pair
            ours = jnp.where(half == 1, total[64:], total[:64] + carried[layer, number, pair])
            dj_ref[layer, rows, lane : lane + 128] = ours.astype(BF16)
            carried[layer, number, pair] = total[:64]


def inverse_norm(wide):
    return lax.rsqrt(jnp.mean(wide * wide, axis=-1, keepdims=True) + EPSILON)


def kernel(
    inputs_ref, cotangent_ref, wq_ref, wo_ref,
    out_ref,
    wq, wo, wqt, wot, entry, passed, hidden, normed, normed_t, joined, probs, keys, values, att, upstream, dj, carried, c_all, grads, grads_out,
    z_a1, z_b1, z_m2, z_p2, z_r, z_sa1, z_sb1, z_sm2, z_sp2,
    x_a1, x_b1, x_m2, x_p2, x_r, x_sa1, x_sb1, x_sm2, x_sp2,
    o_a1, o_b1, o_m2, o_p2,
    load_sem, flip_send, flip_recv, spread_send, spread_recv, core_send, core_recv,
    entry_send, entry_recv, hop_send, hop_recv, c_hop_send, c_hop_recv, share_send, share_recv,
    att_send, att_recv, att_core_send, att_core_recv, c_send, c_recv, sum_send, sum_recv,
):
    section, dp = lax.axis_index("section"), lax.axis_index("dp")
    y, x_hi = lax.div(section, 2), lax.rem(section, 2)
    z, x_lo, core = lax.div(dp, 4), lax.rem(lax.div(dp, 2), 2), lax.rem(dp, 2)
    x = 2 * x_hi + x_lo
    slot = 2 * z + core

    def place(y, x, z, core):
        return (2 * y + lax.div(x, 2), 4 * z + 2 * lax.rem(x, 2) + core)

    core_dev = place(y, x, z, 1 - core)
    xp_dev, xm_dev = place(y, lax.rem(x + 1, 4), z, core), place(y, lax.rem(x + 3, 4), z, core)
    zp_dev, zm_dev = place(y, x, lax.rem(z + 1, 4), core), place(y, x, lax.rem(z + 3, 4), core)
    yp_dev, ym_dev = place(lax.rem(y + 1, 4), x, z, core), place(lax.rem(y + 3, 4), x, z, core)
    column = [[place(y, x, lax.rem(z + k, 4), c) for c in (core, 1 - core)] for k in range(4)]
    flip_dev = place(y, 3 - x, z, core)
    side_dev = place(y, 2 * x_hi + 1 - x_lo, z, core)
    up_across_dev, down_across_dev = place(lax.rem(y + 1, 4), 3 - x, z, core), place(lax.rem(y + 3, 4), 3 - x, z, core)

    def remote(src, dst, send_sem, recv_sem, device):
        return pltpu.make_async_remote_copy(
            src_ref=src, dst_ref=dst, send_sem=send_sem, recv_sem=recv_sem, device_id=device, device_id_type=MESH
        )

    sent = []

    def go(copy):
        copy.start()
        sent.append(copy)

    loads = [
        pltpu.make_async_copy(wq_ref.at[0], wq.at[x_hi], load_sem.at[0]),
        pltpu.make_async_copy(wo_ref.at[0], wo.at[x_hi], load_sem.at[1]),
    ]
    load_in = pltpu.make_async_copy(inputs_ref.at[0, 0, 0], hidden.at[0], load_sem.at[2])
    load_cot = pltpu.make_async_copy(cotangent_ref.at[0, 0, 0], upstream.at[2], load_sem.at[3])
    load_entry = [pltpu.make_async_copy(inputs_ref.at[0, s, 0], entry.at[s], load_sem.at[4 + s]) for s in range(2)]
    for copy in loads:
        copy.start()

    near, far = x_hi == 0, x_hi == 1

    @pl.when((y == 0) & near)
    def _():
        load_entry[0].start()
        load_entry[1].start()
        load_in.start()

    @pl.when((y == 3) & near)
    def _():
        load_cot.start()

    barrier = pltpu.get_barrier_semaphore()
    for device in (core_dev, xp_dev, xm_dev, zp_dev, zm_dev, yp_dev, ym_dev):
        pl.semaphore_signal(barrier, inc=1, device_id=device, device_id_type=MESH)
    pl.semaphore_wait(barrier, 7)

    in_hop = remote(inputs_ref.at[0, 1, 0], hidden.at[0], hop_send.at[2], hop_recv.at[2], side_dev)
    cot_hop = remote(cotangent_ref.at[0, 1, 0], upstream.at[2], hop_send.at[3], hop_recv.at[3], side_dev)

    @pl.when((y == 0) & far)
    def _():
        in_hop.start()

    @pl.when((y == 3) & far)
    def _():
        cot_hop.start()

    h_hop = remote(hidden.at[2], hidden.at[0], hop_send.at[0], hop_recv.at[0], yp_dev)
    def run_forward(h, weights, layer, turned=False):
        wide = h.astype(F32)
        inverse = inverse_norm(wide)
        normed[layer, 0:SEQ] = (wide * inverse).astype(BF16)
        joined[layer] = (mm(h, wq[weights]) * inverse).astype(BF16)
        attention_forward(joined[layer], probs, keys, values, att.at[layer, slot], layer)
        update = mm(att[layer, slot], wot[weights]) if turned else mm_nt(att[layer, slot], wo[weights])
        return (wide + update).astype(BF16)

    other = 1 - x_hi
    piece = lax.rem(z + 2 * x_lo, 4)
    pieces = [lax.rem(piece + k, 4) for k in range(4)]

    def chunk(buf, slot, which, half, part):
        name, k, rows = part
        at = (half * 4 + which) * 128 + k * rows
        return buf[name].at[slot, pl.ds(pl.multiple_of(at, rows), rows)]

    held, given = {"q": wq, "o": wo}, {"q": wq_ref, "o": wo_ref}

    def flip_copy(i, block, source=None):
        return remote(block if source is None else source, block, flip_send.at[i], flip_recv.at[i], flip_dev)

    flips = [
        flip_copy(i, chunk(held, x_hi, pieces[2], core, part), chunk(given, 0, pieces[2], core, part))
        for i, part in enumerate(PARTS)
    ]
    sent.extend(flips)

    @pl.when((y == 0) & far)
    def _():
        for copy in flips:
            copy.start()

    across = [remote(passed.at[s], entry.at[s], entry_send.at[s], entry_recv.at[s], flip_dev) for s in range(2)]
    onward = [
        remote(passed.at[0], hidden.at[0], entry_send.at[0], hop_recv.at[0], up_across_dev),
        remote(passed.at[1], hidden.at[0], entry_send.at[1], hop_recv.at[0], yp_dev),
    ]

    @pl.when(y == 0)
    def _():
        for copy in loads:
            copy.wait()

        def first_pass(s, carry):
            for k in range(2):
                @pl.when((s == k) & near)
                def _():
                    load_entry[k].wait()

                @pl.when((s == k) & far)
                def _():
                    across[k].wait_recv()

            passed[s] = run_forward(entry[s], x_hi, 0)
            for k in range(2):
                @pl.when((s == k) & near)
                def _():
                    across[k].start()

                @pl.when((s == k) & far)
                def _():
                    onward[k].start()

            return carry

        lax.fori_loop(0, 2, first_pass, 0)

        @pl.when(near)
        def _():
            for copy in across:
                copy.wait_send()

        @pl.when(far)
        def _():
            for copy in onward:
                copy.wait_send()

    @pl.when((y > 0) | near)
    def _():
        for copy in flips:
            copy.start()

    def spread(i, part):
        flip_copy(i, chunk(held, other, pieces[0], core, part)).wait_recv()
        block = chunk(held, other, pieces[0], core, part)
        for k, device in ((1, zm_dev), (2, side_dev), (3, zp_dev)):
            go(remote(block, block, spread_send.at[i, k], spread_recv.at[i, k], device))

    def core_copy(i, part, half):
        name, k, rows = part
        block = held[name].at[other].reshape(8, 128, held[name].shape[2])
        block = block.at[pl.ds(half * 4, 4), pl.ds(k * rows, rows)]
        return remote(block, block, core_send.at[i], core_recv.at[i], core_dev)

    def gather_rest(i, part):
        for k in (1, 2, 3):
            block = chunk(held, other, pieces[k], core, part)
            remote(block, block, spread_send.at[i, k], spread_recv.at[i, k], side_dev).wait_recv()
        go(core_copy(i, part, core))

    for i, part in enumerate(PARTS):
        spread(i, part)
        if i > 0:
            gather_rest(i - 1, PARTS[i - 1])
    gather_rest(len(PARTS) - 1, PARTS[-1])
    for i, part in enumerate(PARTS):
        core_copy(i, part, 1 - core).wait_recv()

    def transpose_weights():
        def one(k, carry):
            layer, cols = lax.div(k, 6), pl.ds(pl.multiple_of(lax.rem(k, 6) * 256, 256), 256)
            wqt[layer, cols] = wq[layer, :, cols].T
            return carry

        lax.fori_loop(0, 12, one, 0)

    @pl.when(y > 0)
    def _():
        for copy in loads:
            copy.wait()

    @pl.when(y >= 2)
    def _():
        def one(k, carry):
            layer, rows = lax.div(k, 4), pl.ds(pl.multiple_of(lax.rem(k, 4) * 256, 256), 256)
            wot[layer, :, rows] = wo[layer, rows].T
            return carry

        lax.fori_loop(0, 8, one, 0)
        transpose_weights()

    @pl.when((y == 0) & near)
    def _():
        load_in.wait()

    @pl.when((y == 0) & far)
    def _():
        in_hop.wait()

    @pl.when(y > 0)
    def _():
        h_hop.wait_recv()

    def forward(turned, layer, carry):
        hidden[layer + 1] = run_forward(hidden[layer], layer, layer, turned)
        return carry

    @pl.when(y < 2)
    def _():
        lax.fori_loop(0, 2, functools.partial(forward, False), 0)

    @pl.when(y >= 2)
    def _():
        lax.fori_loop(0, 2, functools.partial(forward, True), 0)

    @pl.when((y > 0) & (y < 3))
    def _():
        h_hop.start()

    def share(buf, layer, number):
        return remote(
            buf.at[layer, 0:SEQ], buf.at[layer, SEQ : 2 * SEQ], share_send.at[number], share_recv.at[number], core_dev
        )

    shares = [share(dj, 0, 0), share(dj, 1, 1)]
    share_normed = remote(
        normed.at[:, 0:SEQ], normed.at[:, SEQ : 2 * SEQ], share_send.at[2], share_recv.at[2], core_dev
    )
    sent.extend(shares)

    def att_block(k, half):
        return att.at[:, 2 * lax.rem(z + 4 - k, 4) + half]

    def att_copy(k):
        return remote(att_block(0, core), att_block(0, core), att_send.at[k], att_recv.at[k], column[k][0])

    def core_att(k):
        return remote(att_block(k, core), att_block(k, core), att_core_send.at[k], att_core_recv.at[k], core_dev)

    def send_attention():
        share_normed.start()
        for k in (1, 3, 2):
            att_copy(k).start()

    def pass_attention():
        core_att(0).start()
        for k in (1, 3, 2):
            remote(att_block(k, core), att_block(k, core), att_send.at[k], att_recv.at[k], core_dev).wait_recv()
            core_att(k).start()

    def await_attention():
        for k in range(4):
            block = att_block(k, 1 - core)
            remote(block, block, att_core_send.at[k], att_core_recv.at[k], core_dev).wait_recv()

    early = sent[: -len(shares)]
    del sent[: len(early)]

    def settle():
        for copy in early:
            copy.wait_send()
        share_normed.wait_send()
        for k in (1, 3, 2):
            att_copy(k).wait_send()
        for k in range(4):
            core_att(k).wait_send()

    def c_columns(layer, k):
        return upstream.at[layer + 1, :, pl.ds(pl.multiple_of(256 * lax.rem(z + k, 4), 256), 256)]

    def c_copy(layer, k):
        return remote(c_columns(layer, k), c_all.at[layer, z, core], c_send.at[layer, k], c_recv.at[layer, k], column[k][0])

    def core_c(layer, half):
        block = c_all.at[layer, :, half]
        return remote(block, block, c_send.at[layer, 0], c_recv.at[layer, 0], core_dev)

    def send_c(layer):
        for k in (1, 3, 2):
            c_copy(layer, k).start()

    def pass_c(layer):
        c_all[layer, z, core] = c_columns(layer, 0)[...]
        for k in (1, 3, 2):
            block = c_all.at[layer, lax.rem(z + 4 - k, 4), core]
            remote(block, block, c_send.at[layer, k], c_recv.at[layer, k], core_dev).wait_recv()
        core_c(layer, core).start()

    sent.extend(c_copy(layer, k) for layer in range(2) for k in (1, 3, 2))
    sent.extend(core_c(layer, core) for layer in range(2))

    low = lax.broadcasted_iota(jnp.int32, (2 * SEQ, 128), 1) < 64

    def own_columns(block):
        def tile(k):
            return block[:, 128 * k : 128 * k + 128].astype(F32)

        tiles = []
        for lo in range(2):
            for pair in range(2):
                a, b = tile(4 * pair + lo), tile(4 * pair + 2 + lo)
                first = jnp.where(core == 0, a, pltpu.roll(a, 64, 1))
                second = jnp.where(core == 0, pltpu.roll(b, 64, 1), b)
                tiles.append(jnp.where(low, first, second).astype(BF16))
        return jnp.concatenate(tiles, axis=1)

    def turn_normed():
        for layer in range(2):
            normed_t[layer] = own_columns(normed[layer]).T

    send_attention()

    @pl.when(y < 2)
    def _():
        transpose_weights()
        pass_attention()
        await_attention()
        share_normed.wait_recv()
        turn_normed()
        settle()

    @pl.when((y == 3) & near)
    def _():
        load_cot.wait()

    @pl.when((y == 3) & far)
    def _():
        cot_hop.wait()

    def c_half(half):
        rows = pl.ds(pl.multiple_of(64 * half, 64), 64)
        return remote(upstream.at[0, rows], upstream.at[2, rows], c_hop_send.at[half], c_hop_recv.at[half], ym_dev)

    def backward(step, carry):
        half, layer = 1 - lax.div(step, 2), 1 - lax.rem(step, 2)
        rows = pl.ds(pl.multiple_of(64 * half, 64), 64)

        @pl.when((y < 3) & (layer == 1))
        def _():
            c_half(half).wait_recv()

        @pl.when((y == 0) & (half == 0))
        def _():
            send_c(layer)

        d_attention = mm(upstream[layer + 1, rows], wo[layer]).astype(BF16)
        attention_backward(joined[layer, rows], d_attention, probs, keys, values, dj, carried, layer, half)

        @pl.when(half == 0)
        def _():
            share(dj, layer, layer).start()

        @pl.when((layer > 0) | (y > 0))
        def _():
            d_normed = mm(dj[layer, rows], wqt[layer])
            wide = hidden[layer, rows].astype(F32)
            inverse = inverse_norm(wide)
            scaled = wide * inverse
            along = jnp.mean(d_normed * scaled, axis=-1, keepdims=True)
            upstream[layer, rows] = (
                upstream[layer + 1, rows].astype(F32) + inverse * (d_normed - scaled * along)
            ).astype(BF16)

        @pl.when((y > 0) & (layer == 0))
        def _():
            c_half(half).start()

        return carry

    lax.fori_loop(0, 4, backward, 0)

    @pl.when(y > 0)
    def _():
        send_c(1)
        send_c(0)

    @pl.when(y >= 2)
    def _():
        share_normed.wait_recv()
        turn_normed()

    def gradient(layer):
        for lo in range(2):
            part = mm(normed_t[layer, 256 * lo : 256 * lo + 256], dj[layer]).astype(BF16)
            grads[2 * layer + lo] = part.reshape(4, 64, QKV)

    def gradient_out(layer):
        core_c(layer, 1 - core).wait_recv()
        a = c_all[layer, :, :, :, 0:128].reshape(8 * SEQ, 128).astype(F32)
        b = c_all[layer, :, :, :, 128:256].reshape(8 * SEQ, 128).astype(F32)
        first = jnp.where(core == 0, a, pltpu.roll(a, 64, 1))
        second = jnp.where(core == 0, pltpu.roll(b, 64, 1), b)
        left = jnp.where(lax.broadcasted_iota(jnp.int32, a.shape, 1) < 64, first, second).astype(BF16)
        part = mm_tn(left, att[layer].reshape(8 * SEQ, D)).astype(BF16)
        grads_out[2 * layer : 2 * layer + 2] = part.reshape(2, 64, D)

    def ring_sum(view, position, plus, minus, bufs, sems, layers=None):
        a1, b1, m2, p2, alpha, beta = bufs
        opposite, after, before = (lax.rem(position + k, 4) for k in (2, 1, 3))
        s, r = sum_send.at, sum_recv.at
        copies = [
            remote(view(opposite, 0), a1, s[sems], r[sems], plus),
            remote(view(opposite, 1), b1, s[sems + 1], r[sems + 1], minus),
            remote(view(after, 1), m2.at[beta], s[sems + 2], r[sems + 2], plus),
            remote(view(before, 0), p2.at[alpha], s[sems + 3], r[sems + 3], minus),
            remote(view(after, 0), m2.at[alpha], s[sems + 4], r[sems + 4], plus),
            remote(view(before, 1), p2.at[beta], s[sems + 5], r[sems + 5], minus),
        ]
        sent.extend(copies)

        def only(stage, target):
            if stage is None:
                return lambda body: body()
            return pl.when(layers(target) == stage)

        def first(stage=None):
            @only(stage, opposite)
            def _():
                copies[0].start()
                copies[1].start()

            @only(stage, after)
            def _():
                copies[2].start()

            @only(stage, before)
            def _():
                copies[3].start()

        def second(stage=None):
            @only(stage, after)
            def _():
                mine = view(after, 0)
                copies[0].wait_recv()
                mine[...] = (mine[...].astype(F32) + a1[...].astype(F32)).astype(BF16)
                copies[4].start()

            @only(stage, before)
            def _():
                mine = view(before, 1)
                copies[1].wait_recv()
                mine[...] = (mine[...].astype(F32) + b1[...].astype(F32)).astype(BF16)
                copies[5].start()

        def last():
            for copy in copies[2:]:
                copy.wait_recv()

        return first, second, last

    def cut(offset, widths):
        return [pl.ds(offset, widths[0]), pl.ds(offset + widths[0], widths[1])]

    z_cols, x_cols, z_own, x_own = cut(0, Z_CUT), cut(HALF, X_CUT), cut(0, Z_CUT), cut(0, X_CUT)

    def wide_at(own):
        return [(slice(None), slice(None), cols) for cols in own]

    def flat_at(own):
        return [(slice(None), cols) for cols in own]

    def z_ring(layer):
        pair = pl.ds(2 * layer, 2)
        bufs = (z_a1.at[pair], z_b1.at[pair], z_m2.at[pair], z_p2.at[pair], *wide_at(z_own))
        return ring_sum(lambda t, k: grads.at[pair, t, :, z_cols[k]], z, zp_dev, zm_dev, bufs, 24 if layer else 0)

    z_big = [z_ring(0), z_ring(1)]
    def layer_of(target):
        return lax.div(target, 2)

    x_big = ring_sum(
        lambda t, k: grads.at[t, :, :, x_cols[k]], x, xp_dev, xm_dev, (x_a1, x_b1, x_m2, x_p2, *wide_at(x_own)), 6, layer_of
    )
    z_small = ring_sum(
        lambda t, k: z_r.at[t, :, z_own[k]], x, xp_dev, xm_dev, (z_sa1, z_sb1, z_sm2, z_sp2, *flat_at(z_own)), 12, layer_of
    )
    x_small = ring_sum(
        lambda t, k: x_r.at[t, :, x_own[k]], z, zp_dev, zm_dev, (x_sa1, x_sb1, x_sm2, x_sp2, *flat_at(x_own)), 18
    )
    out_at = [(slice(None), pl.ds(0, WIDE)), (slice(None), pl.ds(WIDE, WIDE))]
    o_ring = ring_sum(
        lambda t, k: grads_out.at[t, :, pl.ds(k * WIDE, WIDE)], x, xp_dev, xm_dev, (o_a1, o_b1, o_m2, o_p2, *out_at), 30
    )

    def sum_z(layer):
        pair = slice(2 * layer, 2 * layer + 2)
        z_r[pair] = (grads[pair, z, :, 0:HALF].astype(F32) + z_m2[pair].astype(F32) + z_p2[pair].astype(F32)).astype(BF16)

    shares[1].wait_recv()
    gradient(1)
    z_big[1][0]()
    x_big[0](1)
    shares[0].wait_recv()
    gradient(0)
    z_big[0][0]()
    x_big[0](0)

    @pl.when(y >= 2)
    def _():
        pass_attention()
        await_attention()

    pass_c(1)
    pass_c(0)
    gradient_out(1)
    gradient_out(0)
    o_ring[0]()
    z_big[1][1]()
    x_big[1](1)
    z_big[0][1]()
    x_big[1](0)
    z_big[1][2]()
    sum_z(1)
    z_small[0](1)
    o_ring[1]()
    z_big[0][2]()
    sum_z(0)
    z_small[0](0)
    x_big[2]()
    x_r[...] = (grads[x, :, :, HALF:QKV].astype(F32) + x_m2[...].astype(F32) + x_p2[...].astype(F32)).astype(BF16)
    x_small[0]()
    z_small[1](1)
    z_small[1](0)
    x_small[1]()
    o_ring[2]()
    out_ref[:, QKV:COLS] = grads_out[x].astype(F32) + o_m2[...].astype(F32) + o_p2[...].astype(F32)
    z_small[2]()
    out_ref[:, 0:HALF] = z_r[x].astype(F32) + z_sm2[...].astype(F32) + z_sp2[...].astype(F32)
    x_small[2]()
    out_ref[:, HALF:QKV] = x_r[z].astype(F32) + x_sm2[...].astype(F32) + x_sp2[...].astype(F32)

    @pl.when(y >= 2)
    def _():
        settle()

    for copy in sent:
        copy.wait_send()

    @pl.when((y > 0) & (y < 3))
    def _():
        h_hop.wait_send()

    @pl.when(y > 0)
    def _():
        c_half(0).wait_send()
        c_half(1).wait_send()


def split_columns(total_ref, gq_ref, go_ref):
    gq_ref[0] = total_ref[:, :QKV]
    go_ref[0] = total_ref[:, QKV:]


def on_device(inputs, cotangent, w_qkv, w_out):
    any_space = pl.BlockSpec(memory_space=pl.ANY)
    vmem = pl.BlockSpec(memory_space=pltpu.VMEM)
    dma = pltpu.SemaphoreType.DMA

    def flow(widths):
        first, second = widths
        both = first + second
        return [
            pltpu.VMEM((4, 64, first), BF16),
            pltpu.VMEM((4, 64, second), BF16),
            pltpu.VMEM((4, 64, both), BF16),
            pltpu.VMEM((4, 64, both), BF16),
            pltpu.VMEM((4, 64, both), BF16),
            pltpu.VMEM((64, first), BF16),
            pltpu.VMEM((64, second), BF16),
            pltpu.VMEM((64, both), BF16),
            pltpu.VMEM((64, both), BF16),
        ]

    total = pl.pallas_call(
        kernel,
        out_shape=jax.ShapeDtypeStruct((64, COLS), F32),
        in_specs=[any_space] * 4,
        out_specs=vmem,
        scratch_shapes=[
            pltpu.VMEM((2, D, QKV), BF16),
            pltpu.VMEM((2, D, D), BF16),
            pltpu.VMEM((2, QKV, D), BF16),
            pltpu.VMEM((2, D, D), BF16),
            pltpu.VMEM((2, SEQ, D), BF16),
            pltpu.VMEM((2, SEQ, D), BF16),
            pltpu.VMEM((3, SEQ, D), BF16),
            pltpu.VMEM((2, 2 * SEQ, D), BF16),
            pltpu.VMEM((2, 512, 2 * SEQ), BF16),
            pltpu.VMEM((2, SEQ, QKV), BF16),
            pltpu.VMEM((2, 4, 256, 256), BF16),
            pltpu.VMEM((2, 4, 256, 128), BF16),
            pltpu.VMEM((2, 4, 256, 128), BF16),
            pltpu.VMEM((2, 8, SEQ, D), BF16),
            pltpu.VMEM((3, SEQ, D), BF16),
            pltpu.VMEM((2, 2 * SEQ, QKV), BF16),
            pltpu.VMEM((2, 2, 2, 64, 128), F32),
            pltpu.VMEM((2, 4, 2, SEQ, 256), BF16),
            pltpu.VMEM((4, 4, 64, QKV), BF16),
            pltpu.VMEM((4, 64, D), BF16),
            *flow(Z_CUT),
            *flow(X_CUT),
            pltpu.VMEM((64, WIDE), BF16),
            pltpu.VMEM((64, WIDE), BF16),
            pltpu.VMEM((64, D), BF16),
            pltpu.VMEM((64, D), BF16),
            dma((6,)),
            dma((len(PARTS),)),
            dma((len(PARTS),)),
            dma((len(PARTS), 4)),
            dma((len(PARTS), 4)),
            dma((len(PARTS),)),
            dma((len(PARTS),)),
            dma((2,)),
            dma((2,)),
            dma((4,)),
            dma((4,)),
            dma((2,)),
            dma((2,)),
            dma((4,)),
            dma((4,)),
            dma((4,)),
            dma((4,)),
            dma((4,)),
            dma((4,)),
            dma((2, 4)),
            dma((2, 4)),
            dma((36,)),
            dma((36,)),
        ],
        compiler_params=pltpu.CompilerParams(
            collective_id=0, has_side_effects=True, vmem_limit_bytes=56 * 2**20
        ),
    )(inputs, cotangent, w_qkv, w_out)
    return pl.pallas_call(
        split_columns,
        out_shape=(jax.ShapeDtypeStruct((1, 64, QKV), F32), jax.ShapeDtypeStruct((1, 64, D), F32)),
    )(total)


def solution(mesh):
    placed = (
        P("dp", None, None, None, None),
        P("dp", None, None, None, None),
        P("section", None, None),
        P("section", None, None),
    )
    return jax.shard_map(
        on_device,
        mesh=mesh,
        in_specs=placed,
        out_specs=(P("section", "dp", None), P("section", "dp", None)),
        check_vma=False,
    )
```
